32 devices in a mesh: rows: 8 (over z, y), heads: 4 (over x, core).
Axes of the slice: x: 2, y: 2, z: 4, core: 2. Of those that a mesh axis runs over, the one named last changes fastest.
Arguments:
- tokens: bfloat16 [24576, 768], P(('rows', 'heads')), may hold values from -6 to 6
- lengths: int32 [24, 24], P('rows'), may hold values from 1 to 512, 1024 in all within a row
- w_query: bfloat16 [768, 768], P(None, 'heads'), may hold values from -0.21875 to 0.21875
- w_key: bfloat16 [768, 768], P(None, 'heads'), may hold values from -0.21875 to 0.21875
- w_value: bfloat16 [768, 768], P(None, 'heads'), may hold values from -0.21875 to 0.21875
- w_out: bfloat16 [768, 768], P('heads'), may hold values from -0.625 to 0.625
- w_up: bfloat16 [768, 3072], P(None, 'heads'), may hold values from -0.21875 to 0.21875
- w_down: bfloat16 [3072, 768], P('heads'), may hold values from -0.109375 to 0.109375
- gain_first: bfloat16 [768], P('heads'), may hold values from 0.5 to 1.5
- shift_first: bfloat16 [768], P('heads'), may hold values from -3 to 3
- gain_second: bfloat16 [768], P('heads'), may hold values from 0.5 to 1.5
- shift_second: bfloat16 [768], P('heads'), may hold values from -3 to 3
- cotangent: bfloat16 [24576, 768], P(('rows', 'heads')), may hold values from -6 to 6
Outputs:
- mixed: bfloat16 [24576, 768], P(('rows', 'heads'))
- grad_tokens: float32 [24576, 768], P(('rows', 'heads'))
- grad_query: float32 [768, 768], P(None, 'heads')
- grad_key: float32 [768, 768], P(None, 'heads')
- grad_value: float32 [768, 768], P(None, 'heads')
- grad_out: float32 [768, 768], P('heads')
- grad_up: float32 [768, 3072], P(None, 'heads')
- grad_down: float32 [3072, 768], P('heads')
- grad_gain_first: float32 [768], P('heads')
- grad_shift_first: float32 [768], P('heads')
- grad_gain_second: float32 [768], P('heads')
- grad_shift_second: float32 [768], P('heads')
The draws below stay inside these ranges and needn't reach their ends.
Inputs may be any that keep to these rules, and one draw needn't show every extreme that they name: `lengths`: each packed row of 1024 tokens is filled exactly by its 24 documents, and every row holds one document of exactly 512 tokens.
All inputs are finite; a program needn't handle non-finite values.
Results may differ from the reference program's by a relative error of at most 0.013.
Values may be sent and summed in bfloat16 or wider, within the bound.
A program may use at most 128 MiB of HBM per device.

```python
import math
import jax
import jax.numpy as jnp
import numpy as np
from jax import lax

D = 768
HEAD_COUNT = 12
HEAD_WIDTH = 64
FF = 3072
PACKED_ROW_LEN = 1024
LONGEST_DOC_LEN = 512
DOCS_PER_ROW = 24
ROWS_PER_INDEX = 3
ALL_PACKED_ROWS = 24
TOKENS = 24576


def level_of(key, extent, cuts, least, high):
    loudness = 1.0
    for axis_at, parts in cuts:
        steps = jax.random.uniform(jax.random.fold_in(jax.random.fold_in(key, 6), axis_at), (parts,), jnp.float32, least / len(cuts), high / len(cuts))
        loudness = loudness * jnp.repeat(jnp.exp(steps), extent[axis_at] // parts).reshape((-1,) + (1,) * (len(extent) - 1 - axis_at))
    return loudness


def split_up(number_of, total, bound, lean):
    loads = [(1 << 20) // math.isqrt(grade ** lean) + 1 for grade in range(2, number_of + 1)]
    rest, counts = total - bound - (number_of - 1), [1] * (number_of - 1)
    while rest > 0:
        free = [i for i in range(number_of - 1) if counts[i] < bound]
        mass, remaining = sum([loads[i] for i in free]), rest
        for i in free:
            extra = min(bound - counts[i], max(1, remaining * loads[i] // mass), rest)
            counts[i] = counts[i] + extra
            rest = rest - extra
    return np.array([bound] + counts)


def uneven_parts(own_key, count, total, limit, skew):
    if count == 2:
        one = jax.random.randint(own_key, (), max(1, total - limit), min(limit, total - 1) + 1)
        return jnp.stack([one, total - one])
    sizes = jnp.asarray(split_up(count, total, limit, skew), jnp.int32)
    couples = (count - 1) // 2
    donor, receiver = sizes[1:1 + 2 * couples:2], sizes[2:2 + 2 * couples:2]
    margin = jnp.minimum(donor - 1, limit - receiver)
    moved = jax.random.randint(jax.random.fold_in(own_key, 1), (couples,), 0, 1 << 20) % (margin + 1)
    sizes = sizes.at[1:1 + 2 * couples:2].set(donor - moved).at[2:2 + 2 * couples:2].set(receiver + moved)
    return sizes[jax.random.permutation(jax.random.fold_in(own_key, 2), count)]


def bell_draw(stream_key, dims, scale, limit, split=(), kind=jnp.bfloat16):
    array = jax.random.normal(stream_key, dims, jnp.float32) * scale
    if len(split) > 0:
        array = level_of(stream_key, dims, split, -0.22, 0.18) * array
    return jnp.clip(array, min=-limit, max=limit).astype(kind)


def setup_inputs(seed: int = 0) -> dict:
    arg_keys = jax.random.split(jax.random.key(seed), 14)
    return {
        "tokens": bell_draw(arg_keys[0], (TOKENS, D), 1.0, 6.0, ((0, 32),)),
        "lengths": jax.vmap(lambda own: uneven_parts(own, DOCS_PER_ROW, PACKED_ROW_LEN, LONGEST_DOC_LEN, 2))(jax.random.split(arg_keys[1], ALL_PACKED_ROWS)).reshape((ALL_PACKED_ROWS, DOCS_PER_ROW)).astype(jnp.int32),
        "w_query": bell_draw(arg_keys[2], (D, D), D ** -0.5, 0.21875, ((1, 4),)),
        "w_key": bell_draw(arg_keys[3], (D, D), D ** -0.5, 0.21875, ((1, 4),)),
        "w_value": bell_draw(arg_keys[4], (D, D), D ** -0.5, 0.21875, ((1, 4),)),
        "w_out": bell_draw(arg_keys[5], (D, D), (D // 8) ** -0.5, 0.625, ((0, 4),)),
        "w_up": bell_draw(arg_keys[6], (D, FF), D ** -0.5, 0.21875, ((1, 4),)),
        "w_down": bell_draw(arg_keys[7], (FF, D), FF ** -0.5, 0.109375, ((0, 4),)),
        "gain_first": jnp.clip(1.0 + 0.1 * jax.random.normal(arg_keys[8], (D,), jnp.float32), 0.5, 1.5).astype(jnp.bfloat16),
        "shift_first": bell_draw(arg_keys[9], (D,), 0.5, 3.0, ((0, 4),)),
        "gain_second": jnp.clip(1.0 + 0.1 * jax.random.normal(arg_keys[10], (D,), jnp.float32), 0.5, 1.5).astype(jnp.bfloat16),
        "shift_second": bell_draw(arg_keys[11], (D,), 0.5, 3.0, ((0, 4),)),
        "cotangent": bell_draw(arg_keys[12], (TOKENS, D), 1.0, 6.0, ((0, 32),)),
    }


HIGHEST = lax.Precision.HIGHEST
norm_eps = 1e-12

@jax.custom_vjp
def low(v):
    return lax.optimization_barrier(v.astype(jnp.bfloat16)).astype(jnp.float32)

@jax.custom_vjp
def low_back(v):
    return v

def low_keep(v):
    return (low(v), None)

def low_pass(kept, grad):
    return (grad,)

def back_keep(v):
    return (v, None)

def back_low(kept, grad):
    return (low(grad),)
low.defvjp(low_keep, low_pass)
low_back.defvjp(back_keep, back_low)

def layer_norm(values, gain, shift):
    centre = lax.optimization_barrier(jnp.mean(values, axis=-1, keepdims=True))
    centred = values - centre
    spread = lax.optimization_barrier(jnp.mean(centred * centred, axis=-1, keepdims=True))
    return centred * lax.rsqrt(spread + norm_eps) * gain + shift

def gelu_exact(values):
    return jax.nn.gelu(values, approximate=False)

def document_spans(lengths, row_length):
    doc_ends = jnp.cumsum(lengths, axis=1).astype(jnp.int32)
    token_position = lax.broadcasted_iota(jnp.int32, (lengths.shape[0], row_length, lengths.shape[1]), 1)
    return lax.optimization_barrier(jnp.sum((token_position >= doc_ends[:, None, :]).astype(jnp.int32), axis=2)).astype(jnp.int32)

def reference(tokens, lengths, w_query, w_key, w_value, w_out, w_up, w_down, gain_first, shift_first, gain_second, shift_second, cotangent):
    document_span = document_spans(lengths, PACKED_ROW_LEN)
    scaling = float(HEAD_WIDTH) ** (-0.5)
    group_length = PACKED_ROW_LEN * ROWS_PER_INDEX

    def attend(pieces):
        query_row, key_row, value_row, seg_row = pieces
        same_doc = seg_row[:, None] == seg_row[None, :]
        scores = low_back(jnp.einsum('qhe,khe->hqk', query_row, key_row, precision=HIGHEST) * scaling)
        scores = jnp.where(same_doc[None], scores, -1e+30)
        row_max = lax.optimization_barrier(jnp.max(scores, axis=2, keepdims=True))
        exp_terms = jnp.exp(scores - row_max)
        attn_probs = exp_terms / lax.optimization_barrier(jnp.sum(exp_terms, axis=2, keepdims=True))
        return jnp.einsum('hqk,khe->qhe', low(attn_probs), value_row, precision=HIGHEST)

    def forward(layer_in, query_weight, key_weight, value_weight, out_weight, up_weight, down_weight, gain_one, shift_one, gain_two, shift_two):

        def project(weight):
            projected_rows = low_back(low(jnp.dot(layer_in, weight, precision=HIGHEST)))
            return projected_rows.reshape(ALL_PACKED_ROWS, PACKED_ROW_LEN, HEAD_COUNT, HEAD_WIDTH)
        context = lax.map(jax.checkpoint(attend), (project(query_weight), project(key_weight), project(value_weight), document_span))
        context = low_back(low(context.reshape(TOKENS, D)))
        attn_out = low_back(jnp.dot(context, out_weight, precision=HIGHEST))

        def dense(pieces):
            layer_blk, attn_blk = pieces
            hidden = layer_norm(layer_blk + attn_blk, gain_one, shift_one)
            up_proj = low_back(jnp.dot(low(hidden), up_weight, precision=HIGHEST))
            ffn_out = low_back(jnp.dot(low(gelu_exact(up_proj)), down_weight, precision=HIGHEST))
            return layer_norm(hidden + ffn_out, gain_two, shift_two)
        blocks = TOKENS // group_length
        result = lax.map(jax.checkpoint(dense), (layer_in.reshape(blocks, group_length, D), attn_out.reshape(blocks, group_length, D)))
        return result.reshape(TOKENS, D)
    f32 = jnp.float32
    mixed, backward = jax.vjp(forward, tokens.astype(f32), w_query.astype(f32), w_key.astype(f32), w_value.astype(f32), w_out.astype(f32), w_up.astype(f32), w_down.astype(f32), gain_first.astype(f32), shift_first.astype(f32), gain_second.astype(f32), shift_second.astype(f32))
    grads = backward(cotangent.astype(f32))
    return (mixed.astype(jnp.bfloat16), grads[0], grads[1], grads[2], grads[3], grads[4], grads[5], grads[6], grads[7], grads[8], grads[9], grads[10])
```

```python
import functools

import jax
import jax.numpy as jnp
from jax import lax
from jax.experimental import pallas as pl
from jax.experimental.pallas import tpu as pltpu
from jax.sharding import PartitionSpec as P

MESH = pl.DeviceIdType.MESH
BF = jnp.bfloat16
F32 = jnp.float32
HEAD_WIDTH = 64
LONGEST_DOC = 512
BLK = 256
HALO = LONGEST_DOC // BLK
NORM_EPS = 1e-12
VMEM_LIMIT = 60 * 1024 * 1024


def nt(left, right):
    return lax.dot_general(left, right, (((1,), (1,)), ((), ())), preferred_element_type=F32)


def nn(left, right):
    return lax.dot_general(left, right, (((1,), (0,)), ((), ())), preferred_element_type=F32)


def flip(index, bit):
    return index + bit - 2 * bit * ((index // bit) % 2)


def place():
    r, h = lax.axis_index("rows"), lax.axis_index("heads")
    return r, h


def greet(ids):
    barrier = pltpu.get_barrier_semaphore()
    for who in ids:
        pl.semaphore_signal(barrier, inc=1, device_id=who, device_id_type=MESH)
    pl.semaphore_wait(barrier, len(ids))


def group_of(r, h, groups):
    return [(r, lax.rem(h + i, groups)) for i in range(1, groups)]


def remote(src, dst, send, recv, who):
    return pltpu.make_async_remote_copy(
        src_ref=src, dst_ref=dst, send_sem=send, recv_sem=recv, device_id=who, device_id_type=MESH
    )


class Gather:
    def __init__(self, own, full, sems, at):
        self.own, self.full, self.sems, self.at = own, full, sems, at
        self.n = own.shape[1]
        self.u = self.n // 12
        r, h = place()
        self.r, self.h = r, h
        y, z = r % 2, (r // 2) % 2
        self.k = 2 * z + y
        self.ky = 2 * z + 1 - y
        self.kz = 2 * (1 - z) + y
        self.kd = 3 - self.k
        self.hx = flip(h, 2)
        self.hc = flip(h, 1)
        self.by_x = (r, self.hx)
        self.by_c = (r, self.hc)
        self.by_y = (flip(r, 1), h)
        self.by_z = (flip(r, 2), h)

    def rows(self, shard, sub, count):
        u = self.u
        return pl.ds(pl.multiple_of(shard * self.n + sub * u, 16), count * u)

    def part(self, slot, who, shard, sub, count, own=False):
        dst = self.full.at[:, self.rows(shard, sub, count), :]
        src = self.own.at[:, self.rows(0, sub, count), :] if own else dst
        send, recv = self.sems
        return remote(src, dst, send.at[self.at, slot], recv.at[self.at, slot], who)

    def x_main(self):
        return self.part(0, self.by_x, self.h, 3 * self.k, 3, own=True)

    def x_diag(self):
        return self.part(1, self.by_x, self.h, 3 * self.kd, 1, own=True)

    def y_main(self):
        return self.part(2, self.by_y, self.hx, 3 * self.k, 3)

    def z_main(self):
        return self.part(3, self.by_z, self.hx, 3 * self.k, 3)

    def y_diag(self):
        return self.part(4, self.by_y, self.hx, 3 * self.kz + 1, 1)

    def z_diag(self):
        return self.part(5, self.by_z, self.hx, 3 * self.ky + 2, 1)

    def c_own(self):
        return self.part(6, self.by_c, self.h, 0, 12, own=True)

    def c_part(self, i):
        return self.part(7 + i, self.by_c, self.hx, 3 * (self.k, self.ky, self.kz, self.kd)[i], 3)

    def local(self):
        send, _ = self.sems
        return pltpu.make_async_copy(
            self.own, self.full.at[:, self.rows(self.h, 0, 12), :], send.at[self.at, 11]
        )

    def start(self):
        self.x_main().start()
        self.x_diag().start()
        self.c_own().start()
        self.local().start()

    def step_x(self):
        self.x_main().wait_recv()
        self.y_main().start()
        self.z_main().start()
        self.c_part(0).start()

    def step_yz(self):
        self.y_main().wait_recv()
        self.z_diag().start()
        self.c_part(1).start()
        self.z_main().wait_recv()
        self.y_diag().start()
        self.c_part(2).start()

    def step_diag(self):
        self.x_diag().wait_recv()
        self.y_diag().wait_recv()
        self.z_diag().wait_recv()
        self.c_part(3).start()

    def near(self):
        self.c_own().wait_recv()
        self.local().wait()

    def far(self):
        for i in range(4):
            self.c_part(i).wait_recv()

    def sent(self):
        for copy in (self.x_main(), self.x_diag(), self.y_main(), self.z_main(), self.y_diag(), self.z_diag(), self.c_own()):
            copy.wait_send()
        for i in range(4):
            self.c_part(i).wait_send()


def window_start(h, j, own_blocks, row_blocks):
    g = own_blocks * h + j
    first = own_blocks * h - HALO
    row = row_blocks * (g // row_blocks)
    return jnp.clip(row, first, first + own_blocks + 2 * HALO - row_blocks) - first


def gather_attend_kernel(
    groups, row_blocks, tok, qkv_own, out_own, up_own, down_own, segk, segq,
    qkv_full, out_full, up_full, down_full, x_win, q_o, k_o, v_o, kt_o, ctx_o, ctxt_o, lse_o, bias,
    xw, w, vt, send, recv, side_send, side_recv, loc,
):
    r, h = place()
    own = tok.shape[0]
    nb = own // BLK
    nw = nb + 2 * HALO
    halo_rows = HALO * BLK
    x_half = (h // 2) % 2
    far_half = 1 - x_half
    half = 2 * qkv_own.shape[1]
    pairs = half // 128

    sems = (send, recv)
    gq = Gather(qkv_own, w, sems, 0)
    go = Gather(out_own, out_full, sems, 1)
    gu = Gather(up_own, up_full, sems, 2)
    gd = Gather(down_own, down_full, sems, 3)

    greet(group_of(r, h, groups) + [gq.by_y, gq.by_z])

    gq.start()
    to_right = remote(tok.at[pl.ds(own - halo_rows, halo_rows), :], xw.at[pl.ds(0, halo_rows), :], side_send.at[0], side_recv.at[0], (r, h + 1))
    to_left = remote(tok.at[pl.ds(0, halo_rows), :], xw.at[pl.ds(halo_rows + own, halo_rows), :], side_send.at[1], side_recv.at[1], (r, h - 1))

    @pl.when(h < groups - 1)
    def _():
        to_right.start()

    @pl.when(h > 0)
    def _():
        to_left.start()

    mine = pltpu.make_async_copy(tok, xw.at[pl.ds(halo_rows, own), :], loc.at[0])
    mine.start()

    @pl.when(h == 0)
    def _():
        xw[pl.ds(0, halo_rows), :] = jnp.zeros((halo_rows, xw.shape[1]), BF)

    @pl.when(h == groups - 1)
    def _():
        xw[pl.ds(halo_rows + own, halo_rows), :] = jnp.zeros((halo_rows, xw.shape[1]), BF)

    for j in range(nb):
        ws = window_start(h, j, nb, row_blocks)
        for kb in range(row_blocks):
            here = segk[pl.ds(pl.multiple_of((ws + kb) * BLK, BLK), BLK), :]
            bias[j, kb] = jnp.where(here == segq[:, j * BLK : (j + 1) * BLK], 0.0, -1e30).astype(F32)

    def project_keys(hx, b):
        base = pl.multiple_of(hx * half, 128)
        xb = xw[pl.ds(pl.multiple_of(b * BLK, BLK), BLK), :]
        wk = w[1, pl.ds(base, half), :]
        wv = w[2, pl.ds(base, half), :]
        key = nt(xb, wk).astype(BF)
        value = nt(xb, wv).astype(BF)
        for i in range(pairs):
            k_o[hx * pairs + i, pl.ds(pl.multiple_of(b * BLK, BLK), BLK), :] = key[:, i * 128 : (i + 1) * 128]
            v_o[hx * pairs + i, pl.ds(pl.multiple_of(b * BLK, BLK), BLK), :] = value[:, i * 128 : (i + 1) * 128]
        kt_o[b, pl.ds(base, half), :] = nt(wk, xb).astype(BF)
        vt[b, pl.ds(base, half), :] = nt(wv, xb).astype(BF)

    def project_query(hx, b):
        base = pl.multiple_of(hx * half, 128)
        xb = xw[pl.ds(pl.multiple_of((b + HALO) * BLK, BLK), BLK), :]
        query = nt(xb, w[0, pl.ds(base, half), :]).astype(BF) * BF(HEAD_WIDTH**-0.5)
        for i in range(pairs):
            q_o[hx * pairs + i, pl.ds(pl.multiple_of(b * BLK, BLK), BLK), :] = query[:, i * 128 : (i + 1) * 128]

    def attend(hx, t):
        j = t // pairs
        p = hx * pairs + t % pairs
        ws = window_start(h, j, nb, row_blocks)
        q = q_o[p, pl.ds(pl.multiple_of(j * BLK, BLK), BLK), :]
        lane = lax.broadcasted_iota(jnp.int32, q.shape, 1)
        for hh in range(2):
            head = 2 * p + hh
            qm = jnp.where(lane // HEAD_WIDTH == hh, q, jnp.zeros_like(q))
            scores = []
            top = None
            for kb in range(row_blocks):
                kblk = k_o[p, pl.ds(pl.multiple_of((ws + kb) * BLK, BLK), BLK), :]
                s = nt(kblk, qm) + bias[j, kb]
                m = jnp.max(s, axis=0, keepdims=True)
                top = m if top is None else jnp.maximum(top, m)
                scores.append(s)
            total = jnp.zeros_like(top)
            acc = jnp.zeros((HEAD_WIDTH, BLK), F32)
            for kb in range(row_blocks):
                e = jnp.exp(scores[kb] - top)
                total = total + jnp.sum(e, axis=0, keepdims=True)
                acc = acc + nn(vt[ws + kb, pl.ds(pl.multiple_of(head * HEAD_WIDTH, HEAD_WIDTH), HEAD_WIDTH), :], e.astype(BF))
            ctxt_o[j, pl.ds(pl.multiple_of(head * HEAD_WIDTH, HEAD_WIDTH), HEAD_WIDTH), :] = acc / total
            lse_o[j, head] = top + jnp.log(total)

    mine.wait()
    gq.near()
    for b in range(nb):
        project_query(x_half, b)
    lax.fori_loop(HALO, HALO + nb, lambda b, c: (project_keys(x_half, b), c)[1], 0)
    gq.step_x()
    go.start()
    gu.start()
    gd.start()

    @pl.when(h > 0)
    def _():
        to_right.wait_recv()

    @pl.when(h < groups - 1)
    def _():
        to_left.wait_recv()

    out_x = pltpu.make_async_copy(xw, x_win, loc.at[1])
    out_x.start()

    def sides(b, c):
        project_keys(x_half, b + jnp.where(b >= HALO, nb, 0))
        return c

    lax.fori_loop(0, 2 * HALO, sides, 0)
    gq.step_yz()
    gq.step_diag()

    steps = nb * pairs

    def first(t, c):
        attend(x_half, t)
        return c

    lax.fori_loop(0, steps, first, 0)
    go.step_x()
    gu.step_x()
    gq.far()
    out_w = pltpu.make_async_copy(w, qkv_full, loc.at[2])
    out_w.start()

    for b in range(nb):
        project_query(far_half, b)
    lax.fori_loop(0, nw, lambda b, c: (project_keys(far_half, b), c)[1], 0)
    go.step_yz()
    gd.step_x()
    go.step_diag()
    gu.step_yz()

    def second(t, c):
        attend(far_half, t)
        return c

    lax.fori_loop(0, steps, second, 0)
    gu.step_diag()
    gd.step_yz()
    gd.step_diag()
    for j in range(nb):
        ctx_o[j * BLK : (j + 1) * BLK, :] = ctxt_o[j].T.astype(BF)
    for g in (go, gu, gd):
        g.near()
        g.far()
    for g in (gq, go, gu, gd):
        g.sent()
    out_x.wait()
    out_w.wait()

    @pl.when(h < groups - 1)
    def _():
        to_right.wait_send()

    @pl.when(h > 0)
    def _():
        to_left.wait_send()


ANY = pl.BlockSpec(memory_space=pl.ANY)
VM = pl.BlockSpec(memory_space=pltpu.VMEM)


def gather_attend(groups, row_blocks, tok, qkv_own, out_own, up_own, down_own, segk, segq):
    own, width = tok.shape
    nb = own // BLK
    nw = nb + 2 * HALO
    all_pairs = groups * qkv_own.shape[1] // 128
    heads = 2 * all_pairs
    s = jax.ShapeDtypeStruct
    full = lambda a: s((a.shape[0], groups * a.shape[1], a.shape[2]), BF)
    outs = [
        (full(qkv_own), ANY),
        (full(out_own), ANY),
        (full(up_own), ANY),
        (full(down_own), ANY),
        (s((nw * BLK, width), BF), ANY),
        (s((all_pairs, own, 128), BF), VM),
        (s((all_pairs, nw * BLK, 128), BF), VM),
        (s((all_pairs, nw * BLK, 128), BF), VM),
        (s((nw, width, BLK), BF), VM),
        (s((own, width), BF), VM),
        (s((nb, width, BLK), F32), VM),
        (s((nb, heads, 1, BLK), F32), VM),
        (s((nb, row_blocks, BLK, BLK), F32), VM),
    ]
    return pl.pallas_call(
        functools.partial(gather_attend_kernel, groups, row_blocks),
        out_shape=[o[0] for o in outs],
        in_specs=[ANY] * 5 + [VM] * 2,
        out_specs=[o[1] for o in outs],
        scratch_shapes=[
            pltpu.VMEM((nw * BLK, width), BF),
            pltpu.VMEM((3, groups * qkv_own.shape[1], width), BF),
            pltpu.VMEM((nw, width, BLK), BF),
            pltpu.SemaphoreType.DMA((4, 12)),
            pltpu.SemaphoreType.DMA((4, 12)),
            pltpu.SemaphoreType.DMA((2,)),
            pltpu.SemaphoreType.DMA((2,)),
            pltpu.SemaphoreType.DMA((3,)),
        ],
        compiler_params=pltpu.CompilerParams(collective_id=0, has_side_effects=True, vmem_limit_bytes=VMEM_LIMIT),
        name="gather_attend",
    )(tok, qkv_own, out_own, up_own, down_own, segk, segq)


def gelu_parts(u):
    bell = jnp.exp(-0.5 * u * u)
    base = 1.0 + (0.3275911 * 0.7071067811865476) * jnp.abs(u)
    t = pl.reciprocal(base, approx=True)
    t = t * (2.0 - base * t)
    poly = t * (0.127414796 + t * (-0.142248368 + t * (0.7107068705 + t * (-0.7265760135 + t * 0.5307027145))))
    tail = poly * bell
    cdf = jnp.where(u >= 0.0, 1.0 - tail, tail)
    return u * cdf, cdf + u * (bell * 0.3989422804014327)


def dense_kernel(
    tok, cot, ctx, ctxt, out_w, up_w, down_w, vec,
    mixed, d_out, d_up, d_down, g_res_o, g_o, gt_delta, vec_o,
    hid, xhat, inv, hl, ht, ffn, act_t, slope, g_low, gup, g_hid,
):
    own, width = tok.shape
    nb = own // BLK
    shards = up_w.shape[0]
    gain1, shift1, gain2, shift2 = (vec[i : i + 1, :].astype(F32) for i in range(4))
    mean = lambda v: jnp.mean(v, axis=1, keepdims=True)
    rows = lambda b: pl.ds(pl.multiple_of(b * BLK, BLK), BLK)
    vec_o[...] = jnp.zeros_like(vec_o)

    def before(b, c):
        resid = tok[rows(b), :].astype(F32) + nn(ctx[rows(b), :], out_w[...])
        cen = resid - mean(resid)
        rs = lax.rsqrt(mean(cen * cen) + NORM_EPS)
        n = cen * rs
        hidden = n * gain1 + shift1
        xhat[rows(b), :] = n
        inv[rows(b), :] = jnp.broadcast_to(rs, (BLK, 128))
        hid[rows(b), :] = hidden
        low = hidden.astype(BF)
        hl[rows(b), :] = low
        ht[b] = low.T
        ffn[rows(b), :] = hidden
        return c

    lax.fori_loop(0, nb, before, 0)

    def forward(t, c):
        s, b = t // nb, t % nb
        up = nn(hl[rows(b), :], up_w[s])
        active, deriv = gelu_parts(up)
        active = active.astype(BF)
        slope[s, rows(b), :] = deriv.astype(BF)
        act_t[s, b] = active.T
        ffn[rows(b), :] += nn(active, down_w[s])
        return c

    lax.fori_loop(0, shards * nb, forward, 0)

    def middle(b, c):
        v = ffn[rows(b), :]
        cen = v - mean(v)
        rs = lax.rsqrt(mean(cen * cen) + NORM_EPS)
        n = cen * rs
        mixed[rows(b), :] = (n * gain2 + shift2).astype(BF)
        ct = cot[rows(b), :].astype(F32)
        vec_o[2:3, :] += jnp.sum(ct * n, axis=0, keepdims=True)
        vec_o[3:4, :] += jnp.sum(ct, axis=0, keepdims=True)
        e = ct * gain2
        g = rs * (e - mean(e) - n * mean(e * n))
        g_hid[rows(b), :] = g
        g_low[rows(b), :] = g.astype(BF)
        return c

    lax.fori_loop(0, nb, middle, 0)

    def backward(s, c):
        def one(b, cc):
            ga = nt(g_low[rows(b), :], down_w[s])
            gu = (slope[s, rows(b), :].astype(F32) * ga).astype(BF)
            gup[rows(b), :] = gu
            g_hid[rows(b), :] += nt(gu, up_w[s])
            return cc

        lax.fori_loop(0, nb, one, 0)

        def grads(i, cc):
            acc_d = jnp.zeros((BLK, width), F32)
            acc_u = jnp.zeros((BLK, width), F32)
            for b in range(nb):
                acc_d += nn(act_t[s, b, rows(i), :], g_low[b * BLK : (b + 1) * BLK, :])
                acc_u += nn(ht[b, rows(i), :], gup[b * BLK : (b + 1) * BLK, :])
            d_down[s, rows(i), :] = acc_d.astype(BF)
            d_up[s, rows(i), :] = acc_u.astype(BF)
            return cc

        lax.fori_loop(0, width // BLK, grads, 0)
        return c

    lax.fori_loop(0, shards, backward, 0)

    def after(b, c):
        g = g_hid[rows(b), :]
        n = xhat[rows(b), :]
        vec_o[0:1, :] += jnp.sum(g * n, axis=0, keepdims=True)
        vec_o[1:2, :] += jnp.sum(g, axis=0, keepdims=True)
        e = g * gain1
        res = inv[rows(b), 0:1] * (e - mean(e) - n * mean(e * n))
        g_res_o[rows(b), :] = res
        low = res.astype(BF)
        g_low[rows(b), :] = low
        gc = nt(low, out_w[...]).astype(BF)
        for i in range(width // 128):
            g_o[i, rows(b), :] = gc[:, i * 128 : (i + 1) * 128]
        gct = nt(out_w[...], low).astype(BF).astype(F32)
        prod = gct * ctxt[b]
        for i in range(width // HEAD_WIDTH):
            gt_delta[b, i] = jnp.sum(prod[i * HEAD_WIDTH : (i + 1) * HEAD_WIDTH, :], axis=0, keepdims=True)
        return c

    lax.fori_loop(0, nb, after, 0)

    def grad_out(i, c):
        acc = jnp.zeros((BLK, width), F32)
        for b in range(nb):
            acc += nn(ctxt[b, rows(i), :].astype(BF), g_low[b * BLK : (b + 1) * BLK, :])
        d_out[rows(i), :] = acc.astype(BF)
        return c

    lax.fori_loop(0, width // BLK, grad_out, 0)


def dense(tok, cot, ctx, ctxt, out_w, up_w, down_w, vec):
    own, width = tok.shape
    nb = own // BLK
    shards = up_w.shape[0]
    heads = width // HEAD_WIDTH
    s = jax.ShapeDtypeStruct
    outs = [
        s((own, width), BF),
        s((width, width), BF),
        s((shards, width, width), BF),
        s((shards, width, width), BF),
        s((own, width), F32),
        s((width // 128, own, 128), BF),
        s((nb, heads, 1, BLK), F32),
        s((8, width), F32),
    ]
    return pl.pallas_call(
        dense_kernel,
        out_shape=outs,
        in_specs=[VM] * 8,
        out_specs=[VM] * len(outs),
        scratch_shapes=[
            pltpu.VMEM((own, width), F32),
            pltpu.VMEM((own, width), F32),
            pltpu.VMEM((own, 128), F32),
            pltpu.VMEM((own, width), BF),
            pltpu.VMEM((nb, width, BLK), BF),
            pltpu.VMEM((own, width), F32),
            pltpu.VMEM((shards, nb, width, BLK), BF),
            pltpu.VMEM((shards, own, width), BF),
            pltpu.VMEM((own, width), BF),
            pltpu.VMEM((own, width), BF),
            pltpu.VMEM((own, width), F32),
        ],
        compiler_params=pltpu.CompilerParams(vmem_limit_bytes=VMEM_LIMIT),
        name="dense",
    )(tok, cot, ctx, ctxt, out_w, up_w, down_w, vec)


def attend_back_kernel(
    groups, row_blocks, q_i, k_i, v_i, kt_i, x_i, g_i, lse, delta, bias, w, g_res,
    d_qkv, gx, gx_left, gx_right,
    dk, dv, dqt, dkt, dvt,
):
    _, h = place()
    all_pairs, own, _ = q_i.shape
    width = x_i.shape[1]
    nb = own // BLK
    nw = nb + 2 * HALO
    rows = lambda b: pl.ds(pl.multiple_of(b * BLK, BLK), BLK)
    dk[...] = jnp.zeros_like(dk)
    dv[...] = jnp.zeros_like(dv)

    def unit(t, c):
        j, p = t // all_pairs, t % all_pairs
        ws = window_start(h, j, nb, row_blocks)
        q = q_i[p, rows(j), :]
        g = g_i[p, rows(j), :]
        lane = lax.broadcasted_iota(jnp.int32, q.shape, 1)
        qm = [jnp.where(lane // HEAD_WIDTH == hh, q, jnp.zeros_like(q)) for hh in range(2)]
        gm = [jnp.where(lane // HEAD_WIDTH == hh, g, jnp.zeros_like(g)) for hh in range(2)]
        acc = [jnp.zeros((HEAD_WIDTH, BLK), F32) for _ in range(2)]
        for kb in range(row_blocks):
            kblk = k_i[p, rows(ws + kb), :]
            vblk = v_i[p, rows(ws + kb), :]
            add_k = None
            for hh in range(2):
                head = 2 * p + hh
                s = nt(kblk, qm[hh]) + bias[j, kb]
                prob = jnp.exp(s - lse[j, head])
                gp = nt(vblk, gm[hh])
                gs = (prob * (gp - delta[j, head])).astype(BF)
                one_v = nn(prob.astype(BF), gm[hh])
                one_k = nn(gs, qm[hh])
                add_k, add_v = (one_k, one_v) if add_k is None else (add_k + one_k, add_v + one_v)
                acc[hh] += nn(kt_i[ws + kb, pl.ds(pl.multiple_of(head * HEAD_WIDTH, HEAD_WIDTH), HEAD_WIDTH), :], gs)
            dk[p, rows(ws + kb), :] += add_k
            dv[p, rows(ws + kb), :] += add_v
        for hh in range(2):
            head = 2 * p + hh
            dqt[j, pl.ds(pl.multiple_of(head * HEAD_WIDTH, HEAD_WIDTH), HEAD_WIDTH), :] = (acc[hh] * HEAD_WIDTH**-0.5).astype(BF)
        return c

    lax.fori_loop(0, nb * all_pairs, unit, 0)

    for b in range(nw):
        lo, hi = b * BLK, (b + 1) * BLK
        kb = jnp.concatenate([dk[p, lo:hi, :].astype(BF) for p in range(all_pairs)], axis=1)
        vb = jnp.concatenate([dv[p, lo:hi, :].astype(BF) for p in range(all_pairs)], axis=1)
        total = nn(kb, w[1]) + nn(vb, w[2])
        dkt[b] = kb.T
        dvt[b] = vb.T
        if HALO <= b < HALO + nb:
            j = b - HALO
            total = total + nn(dqt[j].T, w[0])
            gx[j * BLK : (j + 1) * BLK, :] = g_res[j * BLK : (j + 1) * BLK, :] + total
        elif b < HALO:
            gx_left[lo:hi, :] = total.astype(BF)
        else:
            k = b - HALO - nb
            gx_right[k * BLK : (k + 1) * BLK, :] = total.astype(BF)

    def grads(i, c):
        acc = jnp.zeros((BLK, width), F32)
        for j in range(nb):
            acc += nn(dqt[j, rows(i), :], x_i[(HALO + j) * BLK : (HALO + j + 1) * BLK, :])
        d_qkv[0, rows(i), :] = acc.astype(BF)
        for a, src in ((1, dkt), (2, dvt)):
            acc = jnp.zeros((BLK, width), F32)
            for b in range(nw):
                acc += nn(src[b, rows(i), :], x_i[b * BLK : (b + 1) * BLK, :])
            d_qkv[a, rows(i), :] = acc.astype(BF)
        return c

    lax.fori_loop(0, width // BLK, grads, 0)


def attend_back(groups, row_blocks, q, k, v, kt, x, g, lse, delta, bias, w, g_res):
    all_pairs, own, _ = q.shape
    width = x.shape[1]
    nb = own // BLK
    nw = nb + 2 * HALO
    s = jax.ShapeDtypeStruct
    outs = [
        s((3, width, width), BF),
        s((own, width), F32),
        s((HALO * BLK, width), BF),
        s((HALO * BLK, width), BF),
    ]
    return pl.pallas_call(
        functools.partial(attend_back_kernel, groups, row_blocks),
        out_shape=outs,
        in_specs=[VM] * 11,
        out_specs=[VM] * len(outs),
        scratch_shapes=[
            pltpu.VMEM((all_pairs, nw * BLK, 128), F32),
            pltpu.VMEM((all_pairs, nw * BLK, 128), F32),
            pltpu.VMEM((nb, width, BLK), BF),
            pltpu.VMEM((nw, width, BLK), BF),
            pltpu.VMEM((nw, width, BLK), BF),
        ],
        compiler_params=pltpu.CompilerParams(vmem_limit_bytes=VMEM_LIMIT),
        name="attend_back",
    )(q, k, v, kt, x, g, lse, delta, bias, w, g_res)


class Reduce:
    def __init__(self, src, shard_rows, lo, n, bits, bufs, sems, at):
        self.src, self.N, self.lo, self.n, self.bits = src, shard_rows, lo, n, bits
        self.rc, self.far, self.res, self.rx, self.ry, self.rz, self.rest = bufs
        self.send, self.recv = sems
        self.at = at
        r, h = place()
        self.h = h
        self.y, self.z = r % 2, (r // 2) % 2
        self.hx, self.hc = flip(h, 2), flip(h, 1)
        self.by_x, self.by_c = (r, self.hx), (r, self.hc)
        self.by_y, self.by_z = (flip(r, 1), h), (flip(r, 2), h)
        self.by_rest = [(flip(r, b), h) for b in bits]

    def copy(self, slot, src, dst, who):
        return remote(src, dst, self.send.at[self.at, slot], self.recv.at[self.at, slot], who)

    def shard(self, s):
        return self.src.at[:, pl.ds(pl.multiple_of(s * self.N + self.lo, 16), self.n), :]

    def core(self, i):
        s = flip(self.hc, 2) if i == 0 else self.hc
        return self.copy(i, self.shard(s), self.rc.at[i], self.by_c)

    def start(self):
        self.core(0).start()
        self.core(1).start()

    def x(self):
        return self.copy(2, self.far, self.rx, self.by_x)

    def step_core(self):
        self.core(0).wait_recv()
        self.far[...] = (self.shard(self.hx)[...].astype(F32) + self.rc[0].astype(F32)).astype(BF)
        self.x().start()
        self.core(1).wait_recv()
        self.res[...] = (self.shard(self.h)[...].astype(F32) + self.rc[1].astype(F32)).astype(BF)

    def half(self, which):
        return self.res.at[:, pl.ds(pl.multiple_of(which * (self.n // 2), 16), self.n // 2), :]

    def quarter(self, half, which):
        return self.res.at[:, pl.ds(pl.multiple_of(half * (self.n // 2) + which * (self.n // 4), 16), self.n // 4), :]

    def landed(self, half, which):
        return self.rx.at[:, pl.ds(pl.multiple_of(half * (self.n // 2) + which * (self.n // 4), 16), self.n // 4), :]

    def y_down(self):
        return self.copy(3, self.half(1 - self.y), self.ry, self.by_y)

    def z_down(self):
        return self.copy(4, self.quarter(self.y, 1 - self.z), self.rz, self.by_z)

    def z_up(self):
        return self.copy(5, self.quarter(self.y, self.z), self.landed(self.y, self.z), self.by_z)

    def y_up(self):
        return self.copy(6, self.quarter(self.y, self.z), self.landed(self.y, self.z), self.by_y)

    def y_up2(self):
        return self.copy(7, self.landed(self.y, 1 - self.z), self.landed(self.y, 1 - self.z), self.by_y)

    def swap(self, i):
        return self.copy(8 + i, self.quarter(self.y, self.z), self.rest.at[i], self.by_rest[i])

    def add(self, ref, got):
        ref[...] = (ref[...].astype(F32) + got[...].astype(F32)).astype(BF)

    def step_x(self):
        self.x().wait_recv()
        self.add(self.res, self.rx)
        self.y_down().start()

    def step_y(self):
        self.y_down().wait_recv()
        self.add(self.half(self.y), self.ry)
        self.z_down().start()

    def step_z(self):
        self.z_down().wait_recv()
        self.add(self.quarter(self.y, self.z), self.rz)
        if self.bits:
            self.swap(0).start()

    def step_rest(self, i):
        self.swap(i).wait_recv()
        self.swap(i).wait_send()
        self.add(self.quarter(self.y, self.z), self.rest.at[i])
        if i + 1 < len(self.bits):
            self.swap(i + 1).start()

    def step_up(self):
        self.z_up().start()
        self.y_up().start()

    def step_up2(self):
        self.z_up().wait_recv()
        self.y_up2().start()

    def step_end(self):
        self.y_up().wait_recv()
        self.y_up2().wait_recv()

    def store(self, out):
        q = self.n // 4
        for half in range(2):
            for which in range(2):
                lo = half * (self.n // 2) + which * q
                mine = jnp.logical_and(self.y == half, self.z == which)
                for there, src in ((mine, self.res), (jnp.logical_not(mine), self.rx)):

                    @pl.when(there)
                    def _():
                        out[:, self.lo + lo : self.lo + lo + q, :] = src[:, lo : lo + q, :].astype(F32)

    def steps(self):
        return (
            [self.start, self.step_core, self.step_x, self.step_y, self.step_z]
            + [functools.partial(self.step_rest, i) for i in range(len(self.bits))]
            + [self.step_up, self.step_up2, self.step_end]
        )

    def sent(self):
        for c in (self.core(0), self.core(1), self.x(), self.y_down(), self.z_down(), self.z_up(), self.y_up(), self.y_up2()):
            c.wait_send()


def other_bits(count):
    bits, b = [], 4
    while b < count:
        bits.append(b)
        b *= 2
    return tuple(bits)


def chunk_plan(width, shard_qkv):
    plan = []
    for a in (0, 1):
        for lo in range(0, width, width // 2):
            plan.append((a, 1, width, lo, width // 2))
    plan.append((2, 1, shard_qkv, 0, shard_qkv))
    plan.append((3, 3, shard_qkv, 0, shard_qkv))
    return plan


def reduce_kernel(
    groups, plan, bits, d_down, d_up, d_out, d_qkv, gx, gx_left, gx_right, vec,
    o_down, o_up, o_out, o_qkv, o_tok, o_vec,
    *scratch,
):
    r, h = place()
    n = len(plan)
    bufs = [scratch[i * 7 : (i + 1) * 7] for i in range(n)]
    send, recv, side_send, side_recv, vsend, vrecv, side, vin, vacc = scratch[7 * n :]
    srcs = (d_down, d_up, d_out, d_qkv)
    dsts = (o_down, o_up, o_out, o_qkv)
    parts = [Reduce(srcs[a], rows, lo, cnt, bits, bufs[i], (send, recv), i) for i, (a, m, rows, lo, cnt) in enumerate(plan)]
    one = parts[0]
    greet(group_of(r, h, groups) + [one.by_y, one.by_z] + one.by_rest)

    halo = gx_left.shape[0]
    own = gx.shape[0]
    to_left = remote(gx_left, side.at[1], side_send.at[0], side_recv.at[0], (r, h - 1))
    to_right = remote(gx_right, side.at[0], side_send.at[1], side_recv.at[1], (r, h + 1))

    @pl.when(h > 0)
    def _():
        to_left.start()

    @pl.when(h < groups - 1)
    def _():
        to_right.start()

    vec_ids = [one.by_c, one.by_x, one.by_y, one.by_z] + one.by_rest

    def vstep(i):
        src = vec if i == 0 else vacc.at[i - 1]
        return remote(src, vin.at[i], vsend.at[i], vrecv.at[i], vec_ids[i])

    vstep(0).start()

    def vnext(i):
        vstep(i).wait_recv()
        before = vec[...] if i == 0 else vacc[i - 1]
        vacc[i] = before + vin[i]
        if i + 1 < len(vec_ids):
            vstep(i + 1).start()

    lists = [p.steps() for p in parts]
    depth = len(lists[0])
    tick = 0
    for tick in range(n + depth - 1):
        for i in range(n):
            s = tick - i
            if 0 <= s < depth:
                lists[i][s]()
                if s == depth - 1:
                    a, m, rows, lo, cnt = plan[i]
                    parts[i].store(dsts[a])
        if tick < len(vec_ids):
            vnext(tick)
    for i in range(n + depth - 1, len(vec_ids)):
        vnext(i)
    o_vec[...] = vacc[len(vec_ids) - 1]

    o_tok[...] = gx[...]

    @pl.when(h < groups - 1)
    def _():
        to_left.wait_recv()
        o_tok[own - halo :, :] += side[1].astype(F32)

    @pl.when(h > 0)
    def _():
        to_right.wait_recv()
        o_tok[:halo, :] += side[0].astype(F32)

    for p in parts:
        p.sent()
    for i in range(len(vec_ids)):
        vstep(i).wait_send()

    @pl.when(h > 0)
    def _():
        to_left.wait_send()

    @pl.when(h < groups - 1)
    def _():
        to_right.wait_send()


def reduce(groups, row_devices, d_down, d_up, d_out, d_qkv, gx, gx_left, gx_right, vec):
    width = gx.shape[1]
    s_qkv = d_qkv.shape[1] // groups
    plan = chunk_plan(width, s_qkv)
    bits = other_bits(row_devices)
    scratch = []
    for a, m, rows, lo, cnt in plan:
        scratch += [
            pltpu.VMEM((2, m, cnt, width), BF),
            pltpu.VMEM((m, cnt, width), BF),
            pltpu.VMEM((m, cnt, width), BF),
            pltpu.VMEM((m, cnt, width), BF),
            pltpu.VMEM((m, cnt // 2, width), BF),
            pltpu.VMEM((m, cnt // 4, width), BF),
            pltpu.VMEM((max(1, len(bits)), m, cnt // 4, width), BF),
        ]
    hops = 4 + len(bits)
    scratch += [
        pltpu.SemaphoreType.DMA((len(plan), 8 + len(bits))),
        pltpu.SemaphoreType.DMA((len(plan), 8 + len(bits))),
        pltpu.SemaphoreType.DMA((2,)),
        pltpu.SemaphoreType.DMA((2,)),
        pltpu.SemaphoreType.DMA((hops,)),
        pltpu.SemaphoreType.DMA((hops,)),
        pltpu.VMEM((2,) + gx_left.shape, BF),
        pltpu.VMEM((hops,) + vec.shape, F32),
        pltpu.VMEM((hops,) + vec.shape, F32),
    ]
    s = jax.ShapeDtypeStruct
    outs = [
        s((1, width, width), F32),
        s((1, width, width), F32),
        s((1, s_qkv, width), F32),
        s((3, s_qkv, width), F32),
        s(gx.shape, F32),
        s(vec.shape, F32),
    ]
    return pl.pallas_call(
        functools.partial(reduce_kernel, groups, plan, bits),
        out_shape=outs,
        in_specs=[VM] * 8,
        out_specs=[VM] * len(outs),
        scratch_shapes=scratch,
        compiler_params=pltpu.CompilerParams(collective_id=1, has_side_effects=True, vmem_limit_bytes=VMEM_LIMIT),
        name="reduce",
    )(d_down, d_up, d_out, d_qkv, gx, gx_left, gx_right, vec)


def local(
    groups, row_devices,
    tokens, lengths, w_query, w_key, w_value, w_out, w_up, w_down,
    gain_first, shift_first, gain_second, shift_second, cotangent,
):
    packed_rows = lengths.shape[0]
    own, width = tokens.shape
    row_length = groups * own // packed_rows
    row_blocks = row_length // BLK
    nw = own // BLK + 2 * HALO
    h = lax.axis_index("heads")

    vec = lax.all_gather(jnp.stack([gain_first, shift_first, gain_second, shift_second]), "heads", axis=1, tiled=True)
    doc_ends = jnp.cumsum(lengths, axis=1)
    position = lax.broadcasted_iota(jnp.int32, (packed_rows, row_length, lengths.shape[1]), 1)
    span = jnp.sum((position >= doc_ends[:, None, :]).astype(jnp.int32), axis=2)
    ids = span + lengths.shape[1] * lax.broadcasted_iota(jnp.int32, span.shape, 0)
    ids = jnp.pad(ids.reshape(-1), (HALO * BLK, HALO * BLK), constant_values=-1)
    seg_k = lax.dynamic_slice(ids, (own * h,), (nw * BLK,))
    seg_q = seg_k[HALO * BLK : HALO * BLK + own]

    qkv_own = jnp.stack([w_query.T, w_key.T, w_value.T])
    shard_cols = w_up.shape[1]
    (qkv, out_w, up_w, down_w, x_win, q, k, v, kt, ctx, ctxt, lse, bias) = gather_attend(
        groups, row_blocks, tokens, qkv_own, w_out[None], w_up[None], w_down[None], seg_k[:, None], seg_q[None, :]
    )
    up_w = up_w.reshape(groups, width, shard_cols)
    down_w = down_w.reshape(groups, shard_cols, width)
    mixed, d_out, d_up, d_down, g_res, g, delta, vec_grads = dense(tokens, cotangent, ctx, ctxt, out_w[0], up_w, down_w, vec)
    d_qkv, gx, gx_left, gx_right = attend_back(groups, row_blocks, q, k, v, kt, x_win, g, lse, delta, bias, qkv, g_res)
    o_down, o_up, o_out, o_qkv, o_tok, o_vec = reduce(
        groups, row_devices,
        d_down.reshape(1, -1, width), d_up.reshape(1, -1, width), d_out[None], d_qkv, gx, gx_left, gx_right, vec_grads,
    )
    n = gain_first.shape[0]
    mine = lax.dynamic_slice(o_vec, (0, n * h), (4, n))
    return (
        mixed, o_tok, o_qkv[0].T, o_qkv[1].T, o_qkv[2].T, o_out[0], o_up[0], o_down[0],
        mine[0], mine[1], mine[2], mine[3],
    )


def solution(mesh):
    both, heads = P(("rows", "heads"), None), P("heads")
    cols, rows = P(None, "heads"), P("heads", None)
    return jax.shard_map(
        functools.partial(local, mesh.shape["heads"], mesh.shape["rows"]),
        mesh=mesh,
        in_specs=(both, P("rows", None), cols, cols, cols, rows, cols, rows, heads, heads, heads, heads, both),
        out_specs=(both, both, cols, cols, cols, rows, cols, rows, heads, heads, heads, heads),
        check_vma=False,
    )
```

```python
import functools

import jax
import jax.numpy as jnp
from jax import lax
from jax.experimental import pallas as pl
from jax.experimental.pallas import tpu as pltpu
from jax.sharding import PartitionSpec as P

MESH = pl.DeviceIdType.MESH
BF = jnp.bfloat16
F32 = jnp.float32
HEAD_WIDTH = 64
LONGEST_DOC = 512
BLK = 256
HALO = LONGEST_DOC // BLK
NORM_EPS = 1e-12
VMEM_LIMIT = 62 * 1024 * 1024


def nt(left, right):
    return lax.dot_general(left, right, (((1,), (1,)), ((), ())), preferred_element_type=F32)


def nn(left, right):
    return lax.dot_general(left, right, (((1,), (0,)), ((), ())), preferred_element_type=F32)


def flip(index, bit):
    return index + bit - 2 * bit * ((index // bit) % 2)


def place():
    r, h = lax.axis_index("rows"), lax.axis_index("heads")
    return r, h


def greet(ids):
    barrier = pltpu.get_barrier_semaphore()
    for who in ids:
        pl.semaphore_signal(barrier, inc=1, device_id=who, device_id_type=MESH)
    pl.semaphore_wait(barrier, len(ids))


def group_of(r, h, groups):
    return [(r, lax.rem(h + i, groups)) for i in range(1, groups)]


def remote(src, dst, send, recv, who):
    return pltpu.make_async_remote_copy(
        src_ref=src, dst_ref=dst, send_sem=send, recv_sem=recv, device_id=who, device_id_type=MESH
    )


class Gather:
    def __init__(self, own, full, sems, at):
        self.own, self.full, self.sems, self.at = own, full, sems, at
        self.n = own.shape[1]
        self.u = self.n // 12
        r, h = place()
        self.r, self.h = r, h
        y, z = r % 2, (r // 2) % 2
        self.k = 2 * z + y
        self.ky = 2 * z + 1 - y
        self.kz = 2 * (1 - z) + y
        self.kd = 3 - self.k
        self.hx = flip(h, 2)
        self.hc = flip(h, 1)
        self.by_x = (r, self.hx)
        self.by_c = (r, self.hc)
        self.by_y = (flip(r, 1), h)
        self.by_z = (flip(r, 2), h)

    def rows(self, shard, sub, count):
        u = self.u
        return pl.ds(pl.multiple_of(shard * self.n + sub * u, 16), count * u)

    def part(self, slot, who, shard, sub, count, own=False):
        dst = self.full.at[:, self.rows(shard, sub, count), :]
        src = self.own.at[:, self.rows(0, sub, count), :] if own else dst
        send, recv = self.sems
        return remote(src, dst, send.at[self.at, slot], recv.at[self.at, slot], who)

    def x_main(self):
        return self.part(0, self.by_x, self.h, 3 * self.k, 3, own=True)

    def x_diag(self):
        return self.part(1, self.by_x, self.h, 3 * self.kd, 1, own=True)

    def y_main(self):
        return self.part(2, self.by_y, self.hx, 3 * self.k, 3)

    def z_main(self):
        return self.part(3, self.by_z, self.hx, 3 * self.k, 3)

    def y_diag(self):
        return self.part(4, self.by_y, self.hx, 3 * self.kz + 1, 1)

    def z_diag(self):
        return self.part(5, self.by_z, self.hx, 3 * self.ky + 2, 1)

    def c_own(self):
        return self.part(6, self.by_c, self.h, 0, 12, own=True)

    def c_part(self, i):
        return self.part(7 + i, self.by_c, self.hx, 3 * (self.k, self.ky, self.kz, self.kd)[i], 3)

    def local(self):
        send, _ = self.sems
        return pltpu.make_async_copy(
            self.own, self.full.at[:, self.rows(self.h, 0, 12), :], send.at[self.at, 11]
        )

    def start_x(self):
        self.x_main().start()
        self.x_diag().start()

    def start_c(self):
        self.c_own().start()
        self.local().start()

    def step_x(self):
        self.x_main().wait_recv()
        self.y_main().start()
        self.z_main().start()
        self.c_part(0).start()

    def step_yz(self):
        self.y_main().wait_recv()
        self.z_diag().start()
        self.c_part(1).start()
        self.z_main().wait_recv()
        self.y_diag().start()
        self.c_part(2).start()

    def step_diag(self):
        self.x_diag().wait_recv()
        self.y_diag().wait_recv()
        self.z_diag().wait_recv()
        self.c_part(3).start()

    def near(self):
        self.c_own().wait_recv()
        self.local().wait()

    def far(self):
        for i in range(4):
            self.c_part(i).wait_recv()

    def sent(self):
        for copy in (self.x_main(), self.x_diag(), self.y_main(), self.z_main(), self.y_diag(), self.z_diag(), self.c_own()):
            copy.wait_send()
        for i in range(4):
            self.c_part(i).wait_send()


def window_start(h, j, own_blocks, row_blocks):
    g = own_blocks * h + j
    first = own_blocks * h - HALO
    row = row_blocks * (g // row_blocks)
    return jnp.clip(row, first, first + own_blocks + 2 * HALO - row_blocks) - first


def mask_of(keys, queries):
    down = jnp.broadcast_to(keys, (8, BLK)).T[:, 0:1]
    return jnp.where(down == queries, 0.0, -1e30).astype(F32)


def gather_attend_kernel(
    groups, row_blocks, tok, qkv_own, out_own, up_own, down_own, vec_own, seg,
    qkv_full, out_full, up_full, down_full, vec_all, x_win, q_o, k_o, v_o, kt_o, ctx_o, ctxt_o, lse_o,
    bias, xw, w, vt, send, recv, side_send, side_recv, vec_send, vec_recv, loc,
):
    r, h = place()
    own = tok.shape[0]
    nb = own // BLK
    nw = nb + 2 * HALO
    halo_rows = HALO * BLK
    x_half = (h // 2) % 2
    far_half = 1 - x_half
    half = 2 * qkv_own.shape[1]
    pairs = half // 128

    sems = (send, recv)
    gq = Gather(qkv_own, w, sems, 0)
    go = Gather(out_own, out_full, sems, 1)
    gu = Gather(up_own, up_full, sems, 2)
    gd = Gather(down_own, down_full, sems, 3)

    greet(group_of(r, h, groups) + [gq.by_y, gq.by_z])

    gq.start_c()
    to_right = remote(tok.at[pl.ds(own - halo_rows, halo_rows), :], xw.at[pl.ds(0, halo_rows), :], side_send.at[0], side_recv.at[0], (r, h + 1))
    to_left = remote(tok.at[pl.ds(0, halo_rows), :], xw.at[pl.ds(halo_rows + own, halo_rows), :], side_send.at[1], side_recv.at[1], (r, h - 1))

    @pl.when(h < groups - 1)
    def _():
        to_right.start()

    @pl.when(h > 0)
    def _():
        to_left.start()

    gq.start_x()
    mine = pltpu.make_async_copy(tok, xw.at[pl.ds(halo_rows, own), :], loc.at[0])
    mine.start()

    def vec_to(i):
        who = (r, lax.rem(h + 1 + i, groups))
        return remote(vec_own, vec_all.at[h], vec_send.at[i], vec_recv.at[groups - 2 - i], who)

    def vec_from(i):
        return remote(vec_own, vec_all.at[h], vec_send.at[i], vec_recv.at[i], (r, lax.rem(h + 1 + i, groups)))

    for i in range(groups - 1):
        vec_to(i).start()
    vec_mine = pltpu.make_async_copy(vec_own, vec_all.at[h], loc.at[3])
    vec_mine.start()

    @pl.when(h == 0)
    def _():
        xw[pl.ds(0, halo_rows), :] = jnp.zeros((halo_rows, xw.shape[1]), BF)

    @pl.when(h == groups - 1)
    def _():
        xw[pl.ds(halo_rows + own, halo_rows), :] = jnp.zeros((halo_rows, xw.shape[1]), BF)

    for j in range(nb):
        ws = window_start(h, j, nb, row_blocks)
        for kb in range(row_blocks):
            bias[j, kb] = mask_of(seg[ws + kb], seg[HALO + j])

    def project_keys(hx, b):
        base = pl.multiple_of(hx * half, 128)
        xb = xw[pl.ds(pl.multiple_of(b * BLK, BLK), BLK), :]
        wk = w[1, pl.ds(base, half), :]
        wv = w[2, pl.ds(base, half), :]
        key = nt(xb, wk).astype(BF)
        value = nt(xb, wv).astype(BF)
        for i in range(pairs):
            k_o[hx * pairs + i, pl.ds(pl.multiple_of(b * BLK, BLK), BLK), :] = key[:, i * 128 : (i + 1) * 128]
            v_o[hx * pairs + i, pl.ds(pl.multiple_of(b * BLK, BLK), BLK), :] = value[:, i * 128 : (i + 1) * 128]
        kt_o[b, pl.ds(base, half), :] = nt(wk, xb).astype(BF)
        vt[b, pl.ds(base, half), :] = nt(wv, xb).astype(BF)

    def project_query(hx, b):
        base = pl.multiple_of(hx * half, 128)
        xb = xw[pl.ds(pl.multiple_of((b + HALO) * BLK, BLK), BLK), :]
        query = nt(xb, w[0, pl.ds(base, half), :]).astype(BF) * BF(HEAD_WIDTH**-0.5)
        for i in range(pairs):
            q_o[hx * pairs + i, pl.ds(pl.multiple_of(b * BLK, BLK), BLK), :] = query[:, i * 128 : (i + 1) * 128]

    def attend(hx, t):
        j = t // pairs
        p = hx * pairs + t % pairs
        ws = window_start(h, j, nb, row_blocks)
        q = q_o[p, pl.ds(pl.multiple_of(j * BLK, BLK), BLK), :]
        lane = lax.broadcasted_iota(jnp.int32, q.shape, 1)
        for hh in range(2):
            head = 2 * p + hh
            qm = jnp.where(lane // HEAD_WIDTH == hh, q, jnp.zeros_like(q))
            scores = []
            top = None
            for kb in range(row_blocks):
                kblk = k_o[p, pl.ds(pl.multiple_of((ws + kb) * BLK, BLK), BLK), :]
                s = nt(kblk, qm) + bias[j, kb]
                m = jnp.max(s, axis=0, keepdims=True)
                top = m if top is None else jnp.maximum(top, m)
                scores.append(s)
            total = jnp.zeros_like(top)
            acc = jnp.zeros((HEAD_WIDTH, BLK), F32)
            for kb in range(row_blocks):
                e = jnp.exp(scores[kb] - top)
                total = total + jnp.sum(e, axis=0, keepdims=True)
                acc = acc + nn(vt[ws + kb, pl.ds(pl.multiple_of(head * HEAD_WIDTH, HEAD_WIDTH), HEAD_WIDTH), :], e.astype(BF))
            ctxt_o[j, pl.ds(pl.multiple_of(head * HEAD_WIDTH, HEAD_WIDTH), HEAD_WIDTH), :] = acc / total
            lse_o[j, head] = top + jnp.log(total)

    mine.wait()
    gq.near()
    for b in range(nb):
        project_query(x_half, b)
    lax.fori_loop(HALO, HALO + nb, lambda b, c: (project_keys(x_half, b), c)[1], 0)
    gq.step_x()
    go.start_x()
    gu.start_x()
    for g in (go, gu, gd):
        g.start_c()

    @pl.when(h > 0)
    def _():
        to_right.wait_recv()

    @pl.when(h < groups - 1)
    def _():
        to_left.wait_recv()

    out_x = pltpu.make_async_copy(xw, x_win, loc.at[1])
    out_x.start()

    def sides(b, c):
        project_keys(x_half, b + jnp.where(b >= HALO, nb, 0))
        return c

    lax.fori_loop(0, 2 * HALO, sides, 0)

    def attend_all(hx, hooks):
        def body(t, c):
            for at, steps in hooks.items():

                @pl.when(t == at)
                def _():
                    for step in steps:
                        step()

            attend(hx, t)
            return c

        lax.fori_loop(0, nb * pairs, body, 0)

    attend_all(x_half, {0: [gq.step_yz], 1: [gq.step_diag], 2: [go.step_x], 4: [gu.step_x, gd.start_x], 6: [go.step_yz], 7: [go.step_diag]})
    gq.far()
    out_w = pltpu.make_async_copy(w, qkv_full, loc.at[2])
    out_w.start()
    gu.step_yz()

    for b in range(nb):
        project_query(far_half, b)
    lax.fori_loop(0, nw, lambda b, c: (project_keys(far_half, b), c)[1], 0)

    attend_all(far_half, {0: [gu.step_diag, gd.step_x], 4: [gd.step_yz], 6: [gd.step_diag]})
    for j in range(nb):
        ctx_o[j * BLK : (j + 1) * BLK, :] = ctxt_o[j].T.astype(BF)
    for g in (go, gu, gd):
        g.near()
        g.far()
    for g in (gq, go, gu, gd):
        g.sent()
    for i in range(groups - 1):
        vec_to(i).wait_send()
        vec_from(i).wait_recv()
    vec_mine.wait()
    out_x.wait()
    out_w.wait()

    @pl.when(h < groups - 1)
    def _():
        to_right.wait_send()

    @pl.when(h > 0)
    def _():
        to_left.wait_send()


ANY = pl.BlockSpec(memory_space=pl.ANY)
VM = pl.BlockSpec(memory_space=pltpu.VMEM)


def gather_attend(groups, row_blocks, tok, qkv_own, out_own, up_own, down_own, vec_own, seg):
    own, width = tok.shape
    nb = own // BLK
    nw = nb + 2 * HALO
    all_pairs = groups * qkv_own.shape[1] // 128
    heads = 2 * all_pairs
    s = jax.ShapeDtypeStruct
    full = lambda a: s((a.shape[0], groups * a.shape[1], a.shape[2]), BF)
    outs = [
        (full(qkv_own), ANY),
        (full(out_own), ANY),
        (full(up_own), ANY),
        (full(down_own), ANY),
        (s((groups,) + vec_own.shape, BF), ANY),
        (s((nw * BLK, width), BF), ANY),
        (s((all_pairs, own, 128), BF), VM),
        (s((all_pairs, nw * BLK, 128), BF), VM),
        (s((all_pairs, nw * BLK, 128), BF), VM),
        (s((nw, width, BLK), BF), VM),
        (s((own, width), BF), VM),
        (s((nb, width, BLK), F32), VM),
        (s((nb, heads, 1, BLK), F32), VM),
    ]
    return pl.pallas_call(
        functools.partial(gather_attend_kernel, groups, row_blocks),
        out_shape=[o[0] for o in outs],
        in_specs=[ANY] * 2 + [VM] * 5,
        out_specs=[o[1] for o in outs],
        scratch_shapes=[
            pltpu.VMEM((nb, row_blocks, BLK, BLK), F32),
            pltpu.VMEM((nw * BLK, width), BF),
            pltpu.VMEM((3, groups * qkv_own.shape[1], width), BF),
            pltpu.VMEM((nw, width, BLK), BF),
            pltpu.SemaphoreType.DMA((4, 12)),
            pltpu.SemaphoreType.DMA((4, 12)),
            pltpu.SemaphoreType.DMA((2,)),
            pltpu.SemaphoreType.DMA((2,)),
            pltpu.SemaphoreType.DMA((groups - 1,)),
            pltpu.SemaphoreType.DMA((groups - 1,)),
            pltpu.SemaphoreType.DMA((4,)),
        ],
        compiler_params=pltpu.CompilerParams(collective_id=0, has_side_effects=True, vmem_limit_bytes=VMEM_LIMIT),
        name="gather_attend",
    )(tok, qkv_own, out_own, up_own, down_own, vec_own, seg)


def gelu_parts(u):
    bell = jnp.exp(-0.5 * u * u)
    base = 1.0 + (0.3275911 * 0.7071067811865476) * jnp.abs(u)
    t = pl.reciprocal(base, approx=True)
    t = t * (2.0 - base * t)
    poly = t * (0.127414796 + t * (-0.142248368 + t * (0.7107068705 + t * (-0.7265760135 + t * 0.5307027145))))
    tail = poly * bell
    cdf = jnp.where(u >= 0.0, 1.0 - tail, tail)
    return u * cdf, cdf + u * (bell * 0.3989422804014327)


class Sum:
    def __init__(self, n, bits, bufs, sems, at):
        self.n, self.bits, self.at = n, bits, at
        self.mine, self.rc, self.rx, self.ry, self.rz, self.rest = bufs
        self.send, self.recv, self.keep = sems
        r, h = place()
        self.y, self.z = r % 2, (r // 2) % 2
        self.by_x, self.by_c = (r, flip(h, 2)), (r, flip(h, 1))
        self.by_y, self.by_z = (flip(r, 1), h), (flip(r, 2), h)
        self.by_rest = [(flip(r, b), h) for b in bits]

    def copy(self, slot, src, dst, who):
        return remote(src, dst, self.send.at[self.at, slot], self.recv.at[self.at, slot], who)

    def core(self, i):
        return self.copy(i, self.mine.at[0], self.rc.at[i], self.by_c)

    def x(self):
        return self.copy(2, self.mine.at[1], self.rx, self.by_x)

    def half(self, which):
        return pl.ds(pl.multiple_of(which * (self.n // 2), 16), self.n // 2)

    def quarter(self, half, which):
        return pl.ds(pl.multiple_of(half * (self.n // 2) + which * (self.n // 4), 16), self.n // 4)

    def own(self):
        return self.mine.at[2, self.quarter(self.y, self.z), :]

    def landed(self, half, which):
        return self.rx.at[self.quarter(half, which), :]

    def y_down(self):
        return self.copy(3, self.mine.at[2, self.half(1 - self.y), :], self.ry, self.by_y)

    def z_down(self):
        return self.copy(4, self.mine.at[2, self.quarter(self.y, 1 - self.z), :], self.rz, self.by_z)

    def z_up(self):
        return self.copy(5, self.own(), self.landed(self.y, self.z), self.by_z)

    def y_up(self):
        return self.copy(6, self.own(), self.landed(self.y, self.z), self.by_y)

    def y_up2(self):
        return self.copy(7, self.landed(self.y, 1 - self.z), self.landed(self.y, 1 - self.z), self.by_y)

    def swap(self, i):
        return self.copy(8 + i, self.own(), self.rest.at[i], self.by_rest[i])

    def add(self, ref, got):
        ref[...] = (ref[...].astype(F32) + got[...].astype(F32)).astype(BF)

    def c0(self):
        self.core(0).start()

    def f(self):
        self.core(0).wait_recv()
        self.add(self.mine.at[1], self.rc.at[0])

    def xs(self):
        self.x().start()

    def c1(self):
        self.core(1).start()

    def s(self):
        self.core(1).wait_recv()
        self.add(self.mine.at[2], self.rc.at[1])

    def r(self):
        self.x().wait_recv()
        self.add(self.mine.at[2], self.rx)
        self.y_down().start()

    def yy(self):
        self.y_down().wait_recv()
        self.add(self.mine.at[2, self.half(self.y), :], self.ry)
        self.z_down().start()

    def zz(self):
        self.z_down().wait_recv()
        self.add(self.own(), self.rz)
        if self.bits:
            self.swap(0).start()

    def w(self):
        for i in range(len(self.bits)):
            self.swap(i).wait_recv()
            self.swap(i).wait_send()
            self.add(self.own(), self.rest.at[i])
            if i + 1 < len(self.bits):
                self.swap(i + 1).start()
        self.z_up().start()
        self.y_up().start()

    def u(self):
        self.z_up().wait_recv()
        self.y_up2().start()

    def outs(self, out, lo):
        def local(i, src, rows):
            start = pl.multiple_of(lo + rows.start, 16)
            return pltpu.make_async_copy(src, out.at[pl.ds(start, rows.size), :], self.keep.at[self.at, i])

        mine, beside, other = self.quarter(self.y, self.z), self.quarter(self.y, 1 - self.z), self.half(1 - self.y)
        return (
            local(0, self.own(), mine),
            local(1, self.rx.at[beside, :], beside),
            local(2, self.rx.at[other, :], other),
        )

    def e(self, out, lo):
        self.y_up().wait_recv()
        self.y_up2().wait_recv()
        for c in self.outs(out, lo):
            c.start()

    def sent(self, out, lo):
        for c in (self.core(1), self.x(), self.y_down(), self.z_down(), self.z_up(), self.y_up(), self.y_up2()):
            c.wait_send()
        for c in self.outs(out, lo):
            c.wait()


def other_bits(count):
    bits, b = [], 4
    while b < count:
        bits.append(b)
        b *= 2
    return tuple(bits)


def hooks_at(t, plan):
    for at, steps in plan.items():

        @pl.when(t == at)
        def _():
            for step in steps:
                step()


def rest_kernel(
    groups, row_blocks, bits, chunks,
    tok, cot, ctx, ctxt, out_w, up_w, down_w, vec, seg, lse, q_i, k_i, v_i, kt_i, x_i, w_i,
    mixed, o_down, o_up, o_out, o_qkv, o_tok, o_left, o_right, o_vec,
    xhat, inv, g_hid, gx_side, vec_acc, vin, vacc, *scratch,
):
    r, h = place()
    own, width = tok.shape
    nb = own // BLK
    nw = nb + 2 * HALO
    halo = HALO * BLK
    shards = up_w.shape[0]
    all_pairs = q_i.shape[0]
    pairs = all_pairs // 2
    half = pairs * 128
    shard_rows = half // 2
    x_half = (h // 2) % 2
    far_half = 1 - x_half
    core = h % 2
    rows = lambda b: pl.ds(pl.multiple_of(b * BLK, BLK), BLK)
    mean = lambda v: jnp.mean(v, axis=1, keepdims=True)
    gain1, shift1, gain2, shift2 = (vec[i : i + 1, :].astype(F32) for i in range(4))

    n_chunks = len(chunks)
    (send, recv, keep, side_send, side_recv, vsend, vrecv, loc) = scratch[6 * n_chunks :]
    sems = (send, recv, keep)
    outs = {"down": o_down, "up": o_up, "out": o_out, "q": o_qkv.at[0], "k": o_qkv.at[1], "v": o_qkv.at[2]}
    parts = [Sum(n, bits, scratch[6 * i : 6 * i + 6], sems, i) for i, (_, _, n) in enumerate(chunks)]
    by_name = {}
    for part, (name, lo, _) in zip(parts, chunks):
        part.end = functools.partial(part.e, outs[name], lo)
        part.done = functools.partial(part.sent, outs[name], lo)
        by_name.setdefault(name, []).append(part)
    downs, ups, (out_c,) = by_name["down"], by_name["up"], by_name["out"]
    q_c, k_c, v_c = (by_name[name][0] for name in "qkv")
    one = parts[0]

    def shard_of(i):
        across = 1 - i // 2
        other = 1 - i % 2
        return h + across * (2 - 4 * x_half) + other * (1 - 2 * core)

    def slot_of(i):
        return (i % 2) * (1 + i // 2)

    def fetch(src, dst, i):
        return pltpu.make_async_copy(src, dst, loc.at[i])

    vec_ids = [one.by_c, one.by_x, one.by_y, one.by_z] + one.by_rest

    def vstep(i):
        src = vec_acc if i == 0 else vacc.at[i - 1]
        return remote(src, vin.at[i], vsend.at[i], vrecv.at[i], vec_ids[i])

    def vnext(i):
        vstep(i).wait_recv()
        vacc[i] = (vec_acc[...] if i == 0 else vacc[i - 1]) + vin[i]
        if i + 1 < len(vec_ids):
            vstep(i + 1).start()

    def dense(tok_v, cot_v, ctx_v, out_v, up_v, down_v, mix_v, hl, ht, ffn, act_t, slope, g_low, gup):
        first = [fetch(a, b, i) for i, (a, b) in enumerate(((tok, tok_v), (ctx, ctx_v), (out_w, out_v), (cot, cot_v)))]
        for c in first:
            c.start()

        def weights(s, slot):
            return fetch(up_w.at[s], up_v.at[slot], 4 + slot), fetch(down_w.at[s], down_v.at[slot], 6 + slot)

        def start_weights(s, slot):
            for c in weights(s, slot):
                c.start()

        def wait_weights(s, slot):
            for c in weights(s, slot):
                c.wait()

        for i in range(2):
            start_weights(shard_of(3 - i), i)
        greet(group_of(r, h, groups) + [one.by_y, one.by_z] + one.by_rest)
        vec_acc[...] = jnp.zeros_like(vec_acc)
        for c in first:
            c.wait()

        def before(b, c):
            resid = tok_v[rows(b), :].astype(F32) + nn(ctx_v[rows(b), :], out_v[...])
            cen = resid - mean(resid)
            rs = lax.rsqrt(mean(cen * cen) + NORM_EPS)
            n = cen * rs
            hidden = n * gain1 + shift1
            xhat[rows(b), :] = n
            inv[rows(b), :] = jnp.broadcast_to(rs, (BLK, 128))
            low = hidden.astype(BF)
            hl[rows(b), :] = low
            ht[b] = low.T
            ffn[rows(b), :] = hidden
            return c

        lax.fori_loop(0, nb, before, 0)

        def forward(i, c):
            s, slot = shard_of(3 - i), i % 2
            wait_weights(s, slot)

            def one_block(b, cc):
                up = nn(hl[rows(b), :], up_v[slot])
                active, deriv = gelu_parts(up)
                active = active.astype(BF)
                slope[s, rows(b), :] = deriv.astype(BF)
                act_t[s, b] = active.T
                ffn[rows(b), :] += nn(active, down_v[slot])
                return cc

            lax.fori_loop(0, nb, one_block, 0)

            @pl.when(i + 2 < shards)
            def _():
                start_weights(shard_of(1 - i), slot)

            return c

        lax.fori_loop(0, shards, forward, 0)

        def middle(b, c):
            v = ffn[rows(b), :]
            cen = v - mean(v)
            rs = lax.rsqrt(mean(cen * cen) + NORM_EPS)
            n = cen * rs
            mix_v[rows(b), :] = (n * gain2 + shift2).astype(BF)
            ct = cot_v[rows(b), :].astype(F32)
            vec_acc[2:3, :] += jnp.sum(ct * n, axis=0, keepdims=True)
            vec_acc[3:4, :] += jnp.sum(ct, axis=0, keepdims=True)
            e = ct * gain2
            g = rs * (e - mean(e) - n * mean(e * n))
            g_hid[rows(b), :] = g
            g_low[rows(b), :] = g.astype(BF)
            return c

        lax.fori_loop(0, nb, middle, 0)
        mix_out = fetch(mix_v, mixed, 0)
        mix_out.start()

        def grad_rows(left, right, part, part_i, slot):
            n = part.n
            acc = jnp.zeros((n, width), F32)
            for b in range(nb):
                acc += nn(left(b, pl.ds(part_i * n, n)), right[b * BLK : (b + 1) * BLK, :])
            part.mine[slot] = acc.astype(BF)

        def down_grads(i, c):
            s, slot = shard_of(i), slot_of(i)

            @pl.when(i == 2)
            def _():
                for p in downs:
                    p.core(0).wait_send()

            for k, p in enumerate(downs):
                grad_rows(lambda b, n: act_t[s, b, n, :], g_low, p, k, slot)
            hooks_at(i, {
                0: [p.c0 for p in downs],
                1: [f for p in downs for f in (p.f, p.xs)],
                2: [p.c1 for p in downs],
                3: [p.s for p in downs],
            })
            return c

        lax.fori_loop(0, shards, down_grads, 0)

        def backward(i, c):
            s, slot = shard_of(i), 1 - i % 2

            @pl.when(i >= 2)
            def _():
                wait_weights(s, slot)

            def one_block(b, cc):
                ga = nt(g_low[rows(b), :], down_v[slot])
                gu = (slope[s, rows(b), :].astype(F32) * ga).astype(BF)
                gup[rows(b), :] = gu
                g_hid[rows(b), :] += nt(gu, up_v[slot])
                return cc

            lax.fori_loop(0, nb, one_block, 0)

            @pl.when(i < 2)
            def _():
                start_weights(shard_of(i + 2), slot)

            @pl.when(i == 2)
            def _():
                for p in ups:
                    p.core(0).wait_send()

            for k, p in enumerate(ups):
                grad_rows(lambda b, n: ht[b, n, :], gup, p, k, slot_of(i))
            hooks_at(i, {
                0: [p.c0 for p in ups],
                1: [p.f for p in ups],
                2: [p.c1 for p in ups],
                3: [p.s for p in ups] + [f for d, p in zip(downs, ups) for f in (d.r, p.xs)],
            })
            return c

        lax.fori_loop(0, shards, backward, 0)
        mix_out.wait()

    pl.run_scoped(
        dense,
        *[pltpu.VMEM((own, width), BF)] * 4,
        pltpu.VMEM((2, width, width), BF),
        pltpu.VMEM((2, width, width), BF),
        pltpu.VMEM((own, width), BF),
        pltpu.VMEM((own, width), BF),
        pltpu.VMEM((nb, width, BLK), BF),
        pltpu.VMEM((own, width), F32),
        pltpu.VMEM((shards, nb, width, BLK), BF),
        pltpu.VMEM((shards, own, width), BF),
        pltpu.VMEM((own, width), BF),
        pltpu.VMEM((own, width), BF),
    )

    def attention(q_v, g_v, x_v, w_v, k_v, v_v, kt_v, delta, bias, dk, dv, dqt, dkt, dvt):
        def keys(hf):
            base = pl.multiple_of(hf * half, 128)
            return (
                fetch(k_i.at[pl.ds(hf * pairs, pairs)], k_v, 0),
                fetch(v_i.at[pl.ds(hf * pairs, pairs)], v_v, 1),
                fetch(kt_i.at[:, pl.ds(base, half), :], kt_v, 2),
            )

        q_in, x_in, w_in = fetch(q_i, q_v, 3), fetch(x_i, x_v, 4), fetch(w_i, w_v, 5)
        for c in (*keys(far_half), q_in, x_in, w_in):
            c.start()

        def between(out_v, ctxt_v, low_v):
            o_in, c_in = fetch(out_w, out_v, 6), fetch(ctxt, ctxt_v, 7)
            o_in.start()
            c_in.start()
            o_in.wait()
            c_in.wait()

            def after(b, c):
                g = g_hid[rows(b), :]
                n = xhat[rows(b), :]
                vec_acc[0:1, :] += jnp.sum(g * n, axis=0, keepdims=True)
                vec_acc[1:2, :] += jnp.sum(g, axis=0, keepdims=True)
                e = g * gain1
                res = inv[rows(b), 0:1] * (e - mean(e) - n * mean(e * n))
                g_hid[rows(b), :] = res
                low = res.astype(BF)
                low_v[rows(b), :] = low
                gc = nt(low, out_v[...]).astype(BF)
                for i in range(all_pairs):
                    g_v[i, rows(b), :] = gc[:, i * 128 : (i + 1) * 128]
                prod = nt(out_v[...], low).astype(BF).astype(F32) * ctxt_v[b]
                for i in range(2 * all_pairs):
                    delta[b, i] = jnp.sum(prod[i * HEAD_WIDTH : (i + 1) * HEAD_WIDTH, :], axis=0, keepdims=True)
                return c

            lax.fori_loop(0, nb, after, 0)
            vstep(0).start()
            downs[0].yy()

            def grad_out(i, c):
                @pl.when(i == 2)
                def _():
                    out_c.core(0).wait_send()

                base = pl.multiple_of(shard_of(i) * shard_rows, 16)
                acc = jnp.zeros((shard_rows, width), F32)
                for b in range(nb):
                    acc += nn(ctxt_v[b, pl.ds(base, shard_rows), :].astype(BF), low_v[b * BLK : (b + 1) * BLK, :])
                out_c.mine[slot_of(i)] = acc.astype(BF)
                hooks_at(i, {0: [out_c.c0], 1: [out_c.f], 2: [out_c.c1], 3: [out_c.s]})
                return c

            lax.fori_loop(0, shards, grad_out, 0)
            downs[1].yy()
            downs[0].zz()

        pl.run_scoped(
            between,
            pltpu.VMEM((width, width), BF),
            pltpu.VMEM((nb, width, BLK), F32),
            pltpu.VMEM((own, width), BF),
        )
        q_in.wait()

        def unit(hf, t):
            j, i = t // pairs, t % pairs
            p = hf * pairs + i
            ws = window_start(h, j, nb, row_blocks)

            @pl.when(i == 0)
            def _():
                for kb in range(row_blocks):
                    bias[kb] = mask_of(seg[ws + kb], seg[HALO + j])

            q = q_v[p, rows(j), :]
            g = g_v[p, rows(j), :]
            lane = lax.broadcasted_iota(jnp.int32, q.shape, 1)
            qm = [jnp.where(lane // HEAD_WIDTH == hh, q, jnp.zeros_like(q)) for hh in range(2)]
            gm = [jnp.where(lane // HEAD_WIDTH == hh, g, jnp.zeros_like(g)) for hh in range(2)]
            acc = [jnp.zeros((HEAD_WIDTH, BLK), F32) for _ in range(2)]
            for kb in range(row_blocks):
                kblk = k_v[i, rows(ws + kb), :]
                vblk = v_v[i, rows(ws + kb), :]
                add_k = None
                for hh in range(2):
                    head = 2 * p + hh
                    s = nt(kblk, qm[hh]) + bias[kb]
                    prob = jnp.exp(s - lse[j, head])
                    gp = nt(vblk, gm[hh])
                    gs = (prob * (gp - delta[j, head])).astype(BF)
                    one_v = nn(prob.astype(BF), gm[hh])
                    one_k = nn(gs, qm[hh])
                    add_k, add_v = (one_k, one_v) if add_k is None else (add_k + one_k, add_v + one_v)
                    at = pl.multiple_of((2 * i + hh) * HEAD_WIDTH, HEAD_WIDTH)
                    acc[hh] += nn(kt_v[ws + kb, pl.ds(at, HEAD_WIDTH), :], gs)
                dk[i, rows(ws + kb), :] += add_k
                dv[i, rows(ws + kb), :] += add_v
            for hh in range(2):
                at = pl.multiple_of((2 * i + hh) * HEAD_WIDTH, HEAD_WIDTH)
                dqt[j, pl.ds(at, HEAD_WIDTH), :] = (acc[hh] * HEAD_WIDTH**-0.5).astype(BF)

        def attend_half(hf, plan):
            dk[...] = jnp.zeros_like(dk)
            dv[...] = jnp.zeros_like(dv)

            def body(t, c):
                hooks_at(t, plan)
                unit(hf, t)
                return c

            lax.fori_loop(0, nb * pairs, body, 0)
            for b in range(nw):
                lo, hi = b * BLK, (b + 1) * BLK
                dkt[b] = jnp.concatenate([dk[p, lo:hi, :].astype(BF) for p in range(pairs)], axis=1).T
                dvt[b] = jnp.concatenate([dv[p, lo:hi, :].astype(BF) for p in range(pairs)], axis=1).T

        def weight_grads(which, slot):
            at = pl.multiple_of(which * shard_rows, 16)
            acc = jnp.zeros((shard_rows, width), F32)
            for j in range(nb):
                acc += nn(dqt[j, pl.ds(at, shard_rows), :], x_v[(HALO + j) * BLK : (HALO + j + 1) * BLK, :])
            q_c.mine[slot] = acc.astype(BF)
            for c, src in ((k_c, dkt), (v_c, dvt)):
                acc = jnp.zeros((shard_rows, width), F32)
                for b in range(nw):
                    acc += nn(src[b, pl.ds(at, shard_rows), :], x_v[b * BLK : (b + 1) * BLK, :])
                c.mine[slot] = acc.astype(BF)

        def input_grads(hf, last):
            base = pl.multiple_of(hf * half, 128)
            wk, wv = w_v.at[1, pl.ds(base, half), :], w_v.at[2, pl.ds(base, half), :]

            def block(b):
                kb = jnp.concatenate([dk[p, rows(b), :].astype(BF) for p in range(pairs)], axis=1)
                vb = jnp.concatenate([dv[p, rows(b), :].astype(BF) for p in range(pairs)], axis=1)
                return nn(kb, wk[...]) + nn(vb, wv[...])

            def side(i, c):
                b = i + jnp.where(i >= HALO, nb, 0)
                total = block(b)
                if last:
                    total = total + gx_side[rows(i), :].astype(F32)
                gx_side[rows(i), :] = total.astype(BF)
                return c

            lax.fori_loop(0, 2 * HALO, side, 0)

            def inner(j, c):
                g_hid[rows(j), :] += block(j + HALO) + nn(dqt[j].T, w_v[0, pl.ds(base, half), :])
                return c

            return lambda: lax.fori_loop(0, nb, inner, 0)

        for c in keys(far_half):
            c.wait()
        d0, d1 = downs
        u0, u1 = ups
        attend_half(far_half, {
            1: [d1.zz], 2: [d0.w], 3: [d1.w], 5: [d0.u, d1.u],
            7: [u0.r, u1.r, out_c.xs], 8: [d0.end, d1.end],
        })
        for c in keys(x_half):
            c.start()
        x_in.wait()
        w_in.wait()
        weight_grads(1 - core, 0)
        for p in (q_c, k_c, v_c):
            p.c0()
        weight_grads(core, 1)
        for p in (q_c, k_c, v_c):
            p.f()
            p.xs()
        u0.yy()
        u1.yy()
        input_grads(far_half, False)()
        u0.zz()
        u1.zz()
        out_c.r()
        for c in keys(x_half):
            c.wait()
        attend_half(x_half, {
            0: [lambda: vnext(0)], 1: [u0.w, lambda: vnext(1)], 2: [u1.w, out_c.yy, lambda: vnext(2)], 3: [out_c.zz, lambda: vnext(3)],
            4: [u0.u, u1.u], 5: [out_c.w], 6: [u0.end, u1.end, out_c.u], 7: [out_c.end],
            8: [functools.partial(vnext, i) for i in range(4, len(vec_ids))],
        })
        for p in (q_c, k_c, v_c):
            p.core(0).wait_send()
        weight_grads(1 - core, 0)
        for p in (q_c, k_c, v_c):
            p.c1()
        weight_grads(core, 2)
        for p in (q_c, k_c, v_c):
            p.s()
            p.r()
        finish = input_grads(x_half, True)

        @pl.when(h > 0)
        def _():
            to_left.start()

        @pl.when(h < groups - 1)
        def _():
            to_right.start()

        for p in (q_c, k_c, v_c):
            p.yy()
        for p in (q_c, k_c, v_c):
            p.zz()
        finish()
        tok_out = fetch(g_hid, o_tok, 3)
        tok_out.start()
        for p in (q_c, k_c, v_c):
            p.w()
        for p in (q_c, k_c, v_c):
            p.u()
        for p in (q_c, k_c, v_c):
            p.end()
        tok_out.wait()

    to_left = remote(gx_side.at[pl.ds(0, halo), :], o_right, side_send.at[0], side_recv.at[0], (r, h - 1))
    to_right = remote(gx_side.at[pl.ds(halo, halo), :], o_left, side_send.at[1], side_recv.at[1], (r, h + 1))

    pl.run_scoped(
        attention,
        pltpu.VMEM((all_pairs, own, 128), BF),
        pltpu.VMEM((all_pairs, own, 128), BF),
        pltpu.VMEM((nw * BLK, width), BF),
        pltpu.VMEM((3, width, width), BF),
        pltpu.VMEM((pairs, nw * BLK, 128), BF),
        pltpu.VMEM((pairs, nw * BLK, 128), BF),
        pltpu.VMEM((nw, half, BLK), BF),
        pltpu.VMEM((nb, 2 * all_pairs, 1, BLK), F32),
        pltpu.VMEM((row_blocks, BLK, BLK), F32),
        pltpu.VMEM((pairs, nw * BLK, 128), F32),
        pltpu.VMEM((pairs, nw * BLK, 128), F32),
        pltpu.VMEM((nb, half, BLK), BF),
        pltpu.VMEM((nw, half, BLK), BF),
        pltpu.VMEM((nw, half, BLK), BF),
    )

    o_vec[...] = vacc[len(vec_ids) - 1]
    for p in parts:
        p.done()
    for i in range(len(vec_ids)):
        vstep(i).wait_send()

    @pl.when(h > 0)
    def _():
        to_left.wait_send()
        to_right.wait_recv()

    @pl.when(h == 0)
    def _():
        gx_side[pl.ds(0, halo), :] = jnp.zeros((halo, width), BF)
        pltpu.sync_copy(gx_side.at[pl.ds(0, halo), :], o_left)

    @pl.when(h < groups - 1)
    def _():
        to_right.wait_send()
        to_left.wait_recv()

    @pl.when(h == groups - 1)
    def _():
        gx_side[pl.ds(halo, halo), :] = jnp.zeros((halo, width), BF)
        pltpu.sync_copy(gx_side.at[pl.ds(halo, halo), :], o_right)


def rest(groups, row_blocks, row_devices, tok, cot, ctx, ctxt, out_w, up_w, down_w, vec, seg, lse, q, k, v, kt, x, w):
    own, width = tok.shape
    shard_rows = width // groups
    nb = own // BLK
    bits = other_bits(row_devices)
    split = width // 2
    chunks = [(name, lo, split) for name in ("down", "up") for lo in range(0, width, split)]
    chunks += [(name, 0, shard_rows) for name in ("out", "q", "k", "v")]
    hops = 4 + len(bits)
    scratch = [
        pltpu.VMEM((own, width), F32),
        pltpu.VMEM((own, 128), F32),
        pltpu.VMEM((own, width), F32),
        pltpu.VMEM((2 * HALO * BLK, width), BF),
        pltpu.VMEM((8, width), F32),
        pltpu.VMEM((hops, 8, width), F32),
        pltpu.VMEM((hops, 8, width), F32),
    ]
    for _, _, n in chunks:
        scratch += [
            pltpu.VMEM((3, n, width), BF),
            pltpu.VMEM((2, n, width), BF),
            pltpu.VMEM((n, width), BF),
            pltpu.VMEM((n // 2, width), BF),
            pltpu.VMEM((n // 4, width), BF),
            pltpu.VMEM((max(1, len(bits)), n // 4, width), BF),
        ]
    scratch += [
        pltpu.SemaphoreType.DMA((len(chunks), 8 + len(bits))),
        pltpu.SemaphoreType.DMA((len(chunks), 8 + len(bits))),
        pltpu.SemaphoreType.DMA((len(chunks), 3)),
        pltpu.SemaphoreType.DMA((2,)),
        pltpu.SemaphoreType.DMA((2,)),
        pltpu.SemaphoreType.DMA((hops,)),
        pltpu.SemaphoreType.DMA((hops,)),
        pltpu.SemaphoreType.DMA((8,)),
    ]
    s = jax.ShapeDtypeStruct
    side = s((HALO * BLK, width), BF)
    outs = [
        (s((own, width), BF), ANY),
        (s((width, width), BF), ANY),
        (s((width, width), BF), ANY),
        (s((shard_rows, width), BF), ANY),
        (s((3, shard_rows, width), BF), ANY),
        (s((own, width), F32), ANY),
        (side, ANY),
        (side, ANY),
        (s((8, width), F32), VM),
    ]
    return pl.pallas_call(
        functools.partial(rest_kernel, groups, row_blocks, bits, chunks),
        out_shape=[o[0] for o in outs],
        in_specs=[ANY] * 7 + [VM] * 3 + [ANY] * 6,
        out_specs=[o[1] for o in outs],
        scratch_shapes=scratch,
        compiler_params=pltpu.CompilerParams(collective_id=1, has_side_effects=True, vmem_limit_bytes=VMEM_LIMIT),
        name="rest",
    )(tok, cot, ctx, ctxt, out_w, up_w, down_w, vec, seg, lse, q, k, v, kt, x, w)


def local(
    groups, row_devices,
    tokens, lengths, w_query, w_key, w_value, w_out, w_up, w_down,
    gain_first, shift_first, gain_second, shift_second, cotangent,
):
    packed_rows = lengths.shape[0]
    own, width = tokens.shape
    row_length = groups * own // packed_rows
    row_blocks = row_length // BLK
    nw = own // BLK + 2 * HALO
    h = lax.axis_index("heads")

    n_vec = gain_first.shape[0]
    vec_own = jnp.pad(jnp.stack([gain_first, shift_first, gain_second, shift_second]), ((0, 12), (0, -n_vec % 128)))
    doc_ends = jnp.cumsum(lengths, axis=1)
    position = lax.broadcasted_iota(jnp.int32, (packed_rows, row_length, lengths.shape[1]), 1)
    span = jnp.sum((position >= doc_ends[:, None, :]).astype(jnp.int32), axis=2)
    ids = span + lengths.shape[1] * lax.broadcasted_iota(jnp.int32, span.shape, 0)
    ids = jnp.pad(ids.reshape(-1), (HALO * BLK, HALO * BLK), constant_values=-1)
    seg = lax.dynamic_slice(ids, (own * h,), (nw * BLK,)).reshape(nw, 1, BLK)

    qkv_own = jnp.stack([w_query.T, w_key.T, w_value.T])
    shard_cols = w_up.shape[1]
    (qkv, out_w, up_w, down_w, vec_all, x_win, q, k, v, kt, ctx, ctxt, lse) = gather_attend(
        groups, row_blocks, tokens, qkv_own, w_out[None], w_up[None], w_down[None], vec_own, seg
    )
    vec = vec_all[:, :4, :n_vec].transpose(1, 0, 2).reshape(4, width)
    up_w = up_w.reshape(groups, width, shard_cols)
    down_w = down_w.reshape(groups, shard_cols, width)
    mixed, o_down, o_up, o_out, o_qkv, gx, gx_left, gx_right, o_vec = rest(
        groups, row_blocks, row_devices, tokens, cotangent, ctx, ctxt, out_w[0], up_w, down_w, vec,
        seg, lse, q, k, v, kt, x_win, qkv,
    )
    halo = HALO * BLK
    o_tok = gx + jnp.pad(gx_left.astype(F32), ((0, own - halo), (0, 0))) + jnp.pad(gx_right.astype(F32), ((own - halo, 0), (0, 0)))
    mine = lax.dynamic_slice(o_vec, (0, n_vec * h), (4, n_vec))
    wide = lambda a: a.astype(F32)
    return (
        mixed, o_tok, wide(o_qkv[0].T), wide(o_qkv[1].T), wide(o_qkv[2].T), wide(o_out), wide(o_up), wide(o_down),
        mine[0], mine[1], mine[2], mine[3],
    )


def solution(mesh):
    both, heads = P(("rows", "heads"), None), P("heads")
    cols, rows = P(None, "heads"), P("heads", None)
    return jax.shard_map(
        functools.partial(local, mesh.shape["heads"], mesh.shape["rows"]),
        mesh=mesh,
        in_specs=(both, P("rows", None), cols, cols, cols, rows, cols, rows, heads, heads, heads, heads, both),
        out_specs=(both, both, cols, cols, cols, rows, cols, rows, heads, heads, heads, heads),
        check_vma=False,
    )
```

```python
import functools

import jax
import jax.numpy as jnp
from jax import lax
from jax.experimental import pallas as pl
from jax.experimental.pallas import tpu as pltpu
from jax.sharding import PartitionSpec as P

MESH = pl.DeviceIdType.MESH
BF = jnp.bfloat16
F32 = jnp.float32
HEAD_WIDTH = 64
LONGEST_DOC = 512
BLK = 256
HALO = LONGEST_DOC // BLK
NORM_EPS = 1e-12
VMEM_LIMIT = 62 * 1024 * 1024


def nt(left, right):
    return lax.dot_general(left, right, (((1,), (1,)), ((), ())), preferred_element_type=F32)


def nn(left, right):
    return lax.dot_general(left, right, (((1,), (0,)), ((), ())), preferred_element_type=F32)


def flip(index, bit):
    return index + bit - 2 * bit * ((index // bit) % 2)


def place():
    r, h = lax.axis_index("rows"), lax.axis_index("heads")
    return r, h


def greet(ids):
    barrier = pltpu.get_barrier_semaphore()
    for who in ids:
        pl.semaphore_signal(barrier, inc=1, device_id=who, device_id_type=MESH)
    pl.semaphore_wait(barrier, len(ids))


def group_of(r, h, groups):
    return [(r, lax.rem(h + i, groups)) for i in range(1, groups)]


def remote(src, dst, send, recv, who):
    return pltpu.make_async_remote_copy(
        src_ref=src, dst_ref=dst, send_sem=send, recv_sem=recv, device_id=who, device_id_type=MESH
    )


class Gather:
    def __init__(self, own, full, sems, at):
        self.own, self.full, self.sems, self.at = own, full, sems, at
        self.n = own.shape[1]
        self.u = self.n // 12
        r, h = place()
        self.r, self.h = r, h
        y, z = r % 2, (r // 2) % 2
        self.k = 2 * z + y
        self.ky = 2 * z + 1 - y
        self.kz = 2 * (1 - z) + y
        self.kd = 3 - self.k
        self.hx = flip(h, 2)
        self.hc = flip(h, 1)
        self.by_x = (r, self.hx)
        self.by_c = (r, self.hc)
        self.by_y = (flip(r, 1), h)
        self.by_z = (flip(r, 2), h)

    def rows(self, shard, sub, count):
        u = self.u
        return pl.ds(pl.multiple_of(shard * self.n + sub * u, 16), count * u)

    def part(self, slot, who, shard, sub, count, own=False):
        dst = self.full.at[:, self.rows(shard, sub, count), :]
        src = self.own.at[:, self.rows(0, sub, count), :] if own else dst
        send, recv = self.sems
        return remote(src, dst, send.at[self.at, slot], recv.at[self.at, slot], who)

    def x_main(self):
        return self.part(0, self.by_x, self.h, 3 * self.k, 3, own=True)

    def x_diag(self):
        return self.part(1, self.by_x, self.h, 3 * self.kd, 1, own=True)

    def y_main(self):
        return self.part(2, self.by_y, self.hx, 3 * self.k, 3)

    def z_main(self):
        return self.part(3, self.by_z, self.hx, 3 * self.k, 3)

    def y_diag(self):
        return self.part(4, self.by_y, self.hx, 3 * self.kz + 1, 1)

    def z_diag(self):
        return self.part(5, self.by_z, self.hx, 3 * self.ky + 2, 1)

    def c_own(self):
        return self.part(6, self.by_c, self.h, 0, 12, own=True)

    def c_part(self, i):
        return self.part(7 + i, self.by_c, self.hx, 3 * (self.k, self.ky, self.kz, self.kd)[i], 3)

    def local(self):
        send, _ = self.sems
        return pltpu.make_async_copy(
            self.own, self.full.at[:, self.rows(self.h, 0, 12), :], send.at[self.at, 11]
        )

    def start_x(self):
        self.x_main().start()
        self.x_diag().start()

    def start_c(self, keep):
        self.c_own().start()
        if keep:
            self.local().start()

    def step_x(self):
        self.x_main().wait_recv()
        self.y_main().start()
        self.z_main().start()
        self.c_part(0).start()

    def step_yz(self):
        self.y_main().wait_recv()
        self.z_diag().start()
        self.c_part(1).start()
        self.z_main().wait_recv()
        self.y_diag().start()
        self.c_part(2).start()

    def step_diag(self):
        self.x_diag().wait_recv()
        self.y_diag().wait_recv()
        self.z_diag().wait_recv()
        self.c_part(3).start()

    def near(self, keep):
        self.c_own().wait_recv()
        if keep:
            self.local().wait()

    def far(self):
        for i in range(4):
            self.c_part(i).wait_recv()

    def sent(self):
        for copy in (self.x_main(), self.x_diag(), self.y_main(), self.z_main(), self.y_diag(), self.z_diag(), self.c_own()):
            copy.wait_send()
        for i in range(4):
            self.c_part(i).wait_send()


def window_start(h, j, own_blocks, row_blocks):
    g = own_blocks * h + j
    first = own_blocks * h - HALO
    row = row_blocks * (g // row_blocks)
    return jnp.clip(row, first, first + own_blocks + 2 * HALO - row_blocks) - first


def mask_of(keys, queries):
    down = jnp.broadcast_to(keys, (8, BLK)).T[:, 0:1]
    return jnp.where(down == queries, 0.0, -1e30).astype(F32)


ANY = pl.BlockSpec(memory_space=pl.ANY)
VM = pl.BlockSpec(memory_space=pltpu.VMEM)


def gelu_parts(u):
    bell = jnp.exp(-0.5 * u * u)
    base = 1.0 + (0.3275911 * 0.7071067811865476) * jnp.abs(u)
    t = pl.reciprocal(base, approx=True)
    t = t * (2.0 - base * t)
    poly = t * (0.127414796 + t * (-0.142248368 + t * (0.7107068705 + t * (-0.7265760135 + t * 0.5307027145))))
    tail = poly * bell
    cdf = jnp.where(u >= 0.0, 1.0 - tail, tail)
    return u * cdf, cdf + u * (bell * 0.3989422804014327)


class Sum:
    def __init__(self, n, bits, bufs, sems, at):
        self.n, self.bits, self.at = n, bits, at
        self.mine, self.rc, self.rx, self.ry, self.rz, self.rest = bufs
        self.send, self.recv, self.keep = sems
        r, h = place()
        self.y, self.z = r % 2, (r // 2) % 2
        self.by_x, self.by_c = (r, flip(h, 2)), (r, flip(h, 1))
        self.by_y, self.by_z = (flip(r, 1), h), (flip(r, 2), h)
        self.by_rest = [(flip(r, b), h) for b in bits]

    def copy(self, slot, src, dst, who):
        return remote(src, dst, self.send.at[self.at, slot], self.recv.at[self.at, slot], who)

    def core(self, i):
        return self.copy(i, self.mine.at[0], self.rc.at[i], self.by_c)

    def x(self):
        return self.copy(2, self.mine.at[1], self.rx, self.by_x)

    def half(self, which):
        return pl.ds(pl.multiple_of(which * (self.n // 2), 16), self.n // 2)

    def quarter(self, half, which):
        return pl.ds(pl.multiple_of(half * (self.n // 2) + which * (self.n // 4), 16), self.n // 4)

    def own(self):
        return self.mine.at[2, self.quarter(self.y, self.z), :]

    def landed(self, half, which):
        return self.rx.at[self.quarter(half, which), :]

    def y_down(self):
        return self.copy(3, self.mine.at[2, self.half(1 - self.y), :], self.ry, self.by_y)

    def z_down(self):
        return self.copy(4, self.mine.at[2, self.quarter(self.y, 1 - self.z), :], self.rz, self.by_z)

    def z_up(self):
        return self.copy(5, self.own(), self.landed(self.y, self.z), self.by_z)

    def y_up(self):
        return self.copy(6, self.own(), self.landed(self.y, self.z), self.by_y)

    def y_up2(self):
        return self.copy(7, self.landed(self.y, 1 - self.z), self.landed(self.y, 1 - self.z), self.by_y)

    def swap(self, i):
        return self.copy(8 + i, self.own(), self.rest.at[i], self.by_rest[i])

    def add(self, ref, got):
        ref[...] = (ref[...].astype(F32) + got[...].astype(F32)).astype(BF)

    def c0(self):
        self.core(0).start()

    def f(self):
        self.core(0).wait_recv()
        self.add(self.mine.at[1], self.rc.at[0])

    def xs(self):
        self.x().start()

    def c1(self):
        self.core(1).start()

    def s(self):
        self.core(1).wait_recv()
        self.add(self.mine.at[2], self.rc.at[1])

    def r(self):
        self.x().wait_recv()
        self.add(self.mine.at[2], self.rx)
        self.y_down().start()

    def yy(self):
        self.y_down().wait_recv()
        self.add(self.mine.at[2, self.half(self.y), :], self.ry)
        self.z_down().start()

    def zz(self):
        self.z_down().wait_recv()
        self.add(self.own(), self.rz)
        if self.bits:
            self.swap(0).start()

    def w(self):
        for i in range(len(self.bits)):
            self.swap(i).wait_recv()
            self.swap(i).wait_send()
            self.add(self.own(), self.rest.at[i])
            if i + 1 < len(self.bits):
                self.swap(i + 1).start()
        self.z_up().start()
        self.y_up().start()

    def u(self):
        self.z_up().wait_recv()
        self.y_up2().start()

    def outs(self, out, lo):
        def local(i, src, rows):
            start = pl.multiple_of(lo + rows.start, 16)
            return pltpu.make_async_copy(src, out.at[pl.ds(start, rows.size), :], self.keep.at[self.at, i])

        mine, beside, other = self.quarter(self.y, self.z), self.quarter(self.y, 1 - self.z), self.half(1 - self.y)
        return (
            local(0, self.own(), mine),
            local(1, self.rx.at[beside, :], beside),
            local(2, self.rx.at[other, :], other),
        )

    def e(self, out, lo):
        self.y_up().wait_recv()
        self.y_up2().wait_recv()
        for c in self.outs(out, lo):
            c.start()

    def sent(self, out, lo):
        for c in (self.core(1), self.x(), self.y_down(), self.z_down(), self.z_up(), self.y_up(), self.y_up2()):
            c.wait_send()
        for c in self.outs(out, lo):
            c.wait()


def other_bits(count):
    bits, b = [], 4
    while b < count:
        bits.append(b)
        b *= 2
    return tuple(bits)


def hooks_at(t, plan):
    for at, steps in plan.items():

        @pl.when(t == at)
        def _():
            for step in steps:
                step()


def layer_kernel(
    groups, row_blocks, bits, chunks,
    tok, cot, qkv_own, out_own, up_own, down_own, vec_own, lengths,
    mixed, o_down, o_up, o_out, o_qkv, o_tok, o_left, o_right, o_vec,
    out_w, up_w, down_w, ctxt, k_i, v_i, kt_i,
    w_v, x_v, q_v, ctx_v, lse, seg, vec_all, xhat, inv, g_hid, gx_side, vec_acc, vin, vacc, *scratch,
):
    r, h = place()
    own, width = tok.shape
    nb = own // BLK
    nw = nb + 2 * HALO
    halo = HALO * BLK
    shards = groups
    all_pairs = q_v.shape[0]
    pairs = all_pairs // 2
    half = pairs * 128
    shard_rows = half // 2
    x_half = (h // 2) % 2
    far_half = 1 - x_half
    core = h % 2
    rows = lambda b: pl.ds(pl.multiple_of(b * BLK, BLK), BLK)
    mean = lambda v: jnp.mean(v, axis=1, keepdims=True)
    n_chunks = len(chunks)
    (send, recv, keep, gsend, grecv, in_send, in_recv, side_send, side_recv, psend, precv, vsend, vrecv, loc) = scratch[6 * n_chunks :]
    sems = (send, recv, keep)
    outs = {"down": o_down, "up": o_up, "out": o_out, "q": o_qkv.at[0], "k": o_qkv.at[1], "v": o_qkv.at[2]}
    parts = [Sum(n, bits, scratch[6 * i : 6 * i + 6], sems, i) for i, (_, _, n) in enumerate(chunks)]
    by_name = {}
    for part, (name, lo, _) in zip(parts, chunks):
        part.end = functools.partial(part.e, outs[name], lo)
        part.done = functools.partial(part.sent, outs[name], lo)
        by_name.setdefault(name, []).append(part)
    downs, ups, (out_c,) = by_name["down"], by_name["up"], by_name["out"]
    q_c, k_c, v_c = (by_name[name][0] for name in "qkv")
    one = parts[0]
    gq = Gather(qkv_own, w_v, (gsend, grecv), 0)
    go = Gather(out_own, out_w, (gsend, grecv), 1)
    gu = Gather(up_own, up_w, (gsend, grecv), 2)
    gd = Gather(down_own, down_w, (gsend, grecv), 3)

    def shard_of(i):
        across = 1 - i // 2
        other = 1 - i % 2
        return h + across * (2 - 4 * x_half) + other * (1 - 2 * core)

    def slot_of(i):
        return (i % 2) * (1 + i // 2)

    def fetch(src, dst, i):
        return pltpu.make_async_copy(src, dst, loc.at[i])

    vec_ids = [one.by_c, one.by_x, one.by_y, one.by_z] + one.by_rest

    def vstep(i):
        src = vec_acc if i == 0 else vacc.at[i - 1]
        return remote(src, vin.at[i], vsend.at[i], vrecv.at[i], vec_ids[i])

    def vnext(i):
        vstep(i).wait_recv()
        vacc[i] = (vec_acc[...] if i == 0 else vacc[i - 1]) + vin[i]
        if i + 1 < len(vec_ids):
            vstep(i + 1).start()

    def project(vt, k_s, v_s, kt_s, bias, ctx_t):
        total_blocks = groups * nb
        in_right = remote(tok.at[pl.ds(own - halo, halo), :], x_v.at[pl.ds(0, halo), :], in_send.at[0], in_recv.at[0], (r, h + 1))
        in_left = remote(tok.at[pl.ds(0, halo), :], x_v.at[pl.ds(halo + own, halo), :], in_send.at[1], in_recv.at[1], (r, h - 1))
        odd = h % 2 == 1

        def par(i):
            who = (r, lax.rem(h + 1 + i, groups))
            return remote(vec_own, vec_all.at[h], psend.at[i], precv.at[groups - 2 - i], who)

        def par_from(i):
            return remote(vec_own, vec_all.at[h], psend.at[i], precv.at[i], (r, lax.rem(h + 1 + i, groups)))

        mine = fetch(tok, x_v.at[pl.ds(halo, own), :], 0)
        mine.start()
        greet(group_of(r, h, groups) + [one.by_y, one.by_z] + one.by_rest)

        @pl.when(h < groups - 1)
        def _():
            in_right.start()

        @pl.when(h > 0)
        def _():
            in_left.start()

        gq.start_c(True)
        gq.start_x()
        for i in range(groups - 1):
            par(i).start()
        go.start_c(True)
        gu.start_c(False)
        gd.start_c(False)
        vec_all[h] = vec_own[...]

        @pl.when(h == 0)
        def _():
            x_v[pl.ds(0, halo), :] = jnp.zeros((halo, width), BF)

        @pl.when(h == groups - 1)
        def _():
            x_v[pl.ds(halo + own, halo), :] = jnp.zeros((halo, width), BF)

        packed, docs = lengths.shape
        down = lax.broadcasted_iota(jnp.int32, (docs, docs), 0)
        across = lax.broadcasted_iota(jnp.int32, (docs, docs), 1)
        for b in range(nw):
            g = nb * h - HALO + b
            row = jnp.clip(g // row_blocks, 0, packed - 1)
            sizes = lengths[pl.ds(row, 1), :].astype(F32)
            ends = jnp.sum(jnp.where(across <= down, jnp.broadcast_to(sizes, (docs, docs)), 0.0), axis=1, keepdims=True)
            at = (lax.broadcasted_iota(jnp.int32, (docs, BLK), 1) + (g % row_blocks) * BLK).astype(F32)
            ids = jnp.sum(jnp.where(at >= ends, 1.0, 0.0), axis=0, keepdims=True) + (row * docs).astype(F32)
            inside = jnp.logical_and(g >= 0, g < total_blocks)
            seg[b] = jnp.where(inside, ids, -1.0)
        for j in range(nb):
            ws = window_start(h, j, nb, row_blocks)
            for kb in range(row_blocks):
                bias[j, kb] = mask_of(seg[ws + kb], seg[HALO + j])

        def project_keys(hx, b):
            base = pl.multiple_of(hx * half, 128)
            xb = x_v[rows(b), :]
            wk = w_v[1, pl.ds(base, half), :]
            wv = w_v[2, pl.ds(base, half), :]
            key = nt(xb, wk).astype(BF)
            value = nt(xb, wv).astype(BF)
            for i in range(pairs):
                k_s[hx * pairs + i, rows(b), :] = key[:, i * 128 : (i + 1) * 128]
                v_s[hx * pairs + i, rows(b), :] = value[:, i * 128 : (i + 1) * 128]
            kt_s[b, pl.ds(base, half), :] = nt(wk, xb).astype(BF)
            vt[b, pl.ds(base, half), :] = nt(wv, xb).astype(BF)

        def project_query(hx, b):
            base = pl.multiple_of(hx * half, 128)
            xb = x_v[rows(b + HALO), :]
            query = nt(xb, w_v[0, pl.ds(base, half), :]).astype(BF) * BF(HEAD_WIDTH**-0.5)
            for i in range(pairs):
                q_v[hx * pairs + i, rows(b), :] = query[:, i * 128 : (i + 1) * 128]

        def side_keys(hx, first):
            def body(b, c):
                project_keys(hx, first + b)
                return c

            lax.fori_loop(0, HALO, body, 0)

        def attend(hx, t):
            j = jnp.where(odd, t // pairs, nb - 1 - t // pairs)
            p = hx * pairs + t % pairs
            ws = window_start(h, j, nb, row_blocks)
            q = q_v[p, rows(j), :]
            lane = lax.broadcasted_iota(jnp.int32, q.shape, 1)
            for hh in range(2):
                head = 2 * p + hh
                qm = jnp.where(lane // HEAD_WIDTH == hh, q, jnp.zeros_like(q))
                scores = []
                top = None
                for kb in range(row_blocks):
                    s = nt(k_s[p, rows(ws + kb), :], qm) + bias[j, kb]
                    m = jnp.max(s, axis=0, keepdims=True)
                    top = m if top is None else jnp.maximum(top, m)
                    scores.append(s)
                total = jnp.zeros_like(top)
                acc = jnp.zeros((HEAD_WIDTH, BLK), F32)
                at = pl.multiple_of(head * HEAD_WIDTH, HEAD_WIDTH)
                for kb in range(row_blocks):
                    e = jnp.exp(scores[kb] - top)
                    total = total + jnp.sum(e, axis=0, keepdims=True)
                    acc = acc + nn(vt[ws + kb, pl.ds(at, HEAD_WIDTH), :], e.astype(BF))
                ctx_t[j, pl.ds(at, HEAD_WIDTH), :] = acc / total
                lse[j, head] = top + jnp.log(total)

        def attend_all(hx, plan):
            def body(t, c):
                hooks_at(t, plan)
                attend(hx, t)
                return c

            lax.fori_loop(0, nb * pairs, body, 0)

        def far_side():
            @pl.when(jnp.logical_and(odd, h < groups - 1))
            def _():
                in_left.wait_recv()

            @pl.when(jnp.logical_and(jnp.logical_not(odd), h > 0))
            def _():
                in_right.wait_recv()

            side_keys(x_half, jnp.where(odd, HALO + nb, 0))

        mine.wait()
        gq.near(True)
        for b in range(nb):
            project_query(x_half, b)
        lax.fori_loop(HALO, HALO + nb, lambda b, c: (project_keys(x_half, b), c)[1], 0)

        @pl.when(odd)
        def _():
            in_right.wait_recv()

        @pl.when(jnp.logical_not(odd))
        def _():
            in_left.wait_recv()

        side_keys(x_half, jnp.where(odd, 0, HALO + nb))
        attend_all(x_half, {
            2: [gq.step_x, go.start_x, gu.start_x],
            3: [far_side],
            6: [gq.step_yz], 8: [gq.step_diag, go.step_x],
        })
        gq.far()
        for b in range(nb):
            project_query(far_half, b)
        lax.fori_loop(0, nw, lambda b, c: (project_keys(far_half, b), c)[1], 0)
        keys_out = [fetch(a, b, i) for i, (a, b) in enumerate(((k_s, k_i), (v_s, v_i), (kt_s, kt_i)))]
        for c in keys_out:
            c.start()
        attend_all(far_half, {
            0: [gu.step_x, gd.start_x], 2: [go.step_yz], 4: [go.step_diag, gu.step_yz], 6: [gu.step_diag],
        })
        ctx_out = fetch(ctx_t, ctxt, 3)
        ctx_out.start()
        for j in range(nb):
            ctx_v[j * BLK : (j + 1) * BLK, :] = ctx_t[j].T.astype(BF)
        gd.step_x()
        go.near(True)
        go.far()
        for c in keys_out:
            c.wait()
        ctx_out.wait()
        for i in range(groups - 1):
            par(i).wait_send()
            par_from(i).wait_recv()

        @pl.when(h < groups - 1)
        def _():
            in_right.wait_send()

        @pl.when(h > 0)
        def _():
            in_left.wait_send()

    def dense(cot_v, out_v, up_v, down_v, hl, ht, act_t, slope):
        ffn, gup, mix_v, g_low = g_hid, hl, ctx_v, cot_v
        params = vec_all[0].astype(F32)
        for i in range(1, groups):
            params = params + vec_all[i].astype(F32)
        gain1, shift1, gain2, shift2 = (params[i : i + 1, :] for i in range(4))
        first = [fetch(a, b, i) for i, (a, b) in enumerate(((out_w.at[0], out_v), (cot, cot_v)))]
        for c in first:
            c.start()

        def weights(i, slot):
            if i == shards - 1:
                return fetch(up_own.at[0], up_v.at[slot], 4 + slot), fetch(down_own.at[0], down_v.at[slot], 6 + slot)
            here = pl.ds(pl.multiple_of(shard_of(i) * width, 16), width)
            return fetch(up_w.at[0, here, :], up_v.at[slot], 4 + slot), fetch(down_w.at[0, here, :], down_v.at[slot], 6 + slot)

        def start_weights(i, slot):
            for c in weights(i, slot):
                c.start()

        def wait_weights(i, slot):
            for c in weights(i, slot):
                c.wait()

        start_weights(3, 0)
        gu.near(False)
        gd.near(False)
        start_weights(2, 1)
        vec_acc[...] = jnp.zeros_like(vec_acc)
        for c in first:
            c.wait()

        def before(b, c):
            resid = x_v[rows(b + HALO), :].astype(F32) + nn(ctx_v[rows(b), :], out_v[...])
            cen = resid - mean(resid)
            rs = lax.rsqrt(mean(cen * cen) + NORM_EPS)
            n = cen * rs
            hidden = n * gain1 + shift1
            xhat[rows(b), :] = n
            inv[rows(b), :] = jnp.broadcast_to(rs, (BLK, 128))
            low = hidden.astype(BF)
            hl[rows(b), :] = low
            ht[b] = low.T
            ffn[rows(b), :] = hidden
            return c

        lax.fori_loop(0, nb, before, 0)

        def forward(i, c):
            slot = i % 2
            wait_weights(0, slot)
            for b in range(nb):
                up = nn(hl[rows(b), :], up_v[slot])
                active, deriv = gelu_parts(up)
                active = active.astype(BF)
                slope[i, rows(b), :] = deriv.astype(BF)
                act_t[i, b] = active.T
                ffn[rows(b), :] += nn(active, down_v[slot])
            return c

        def two(first, then):
            def body(i, c):
                forward(i, c)
                hooks_at(i, then)
                return c

            lax.fori_loop(first, first + 2, body, 0)

        two(0, {0: [gd.step_yz], 1: [gd.step_diag]})
        gu.far()
        gd.far()
        start_weights(1, 0)
        start_weights(0, 1)
        two(2, {})

        def middle(b, c):
            v = ffn[rows(b), :]
            cen = v - mean(v)
            rs = lax.rsqrt(mean(cen * cen) + NORM_EPS)
            n = cen * rs
            mix_v[rows(b), :] = (n * gain2 + shift2).astype(BF)
            ct = cot_v[rows(b), :].astype(F32)
            vec_acc[2:3, :] += jnp.sum(ct * n, axis=0, keepdims=True)
            vec_acc[3:4, :] += jnp.sum(ct, axis=0, keepdims=True)
            e = ct * gain2
            g = rs * (e - mean(e) - n * mean(e * n))
            g_hid[rows(b), :] = g
            g_low[rows(b), :] = g.astype(BF)
            return c

        lax.fori_loop(0, nb, middle, 0)
        mix_out = fetch(mix_v, mixed, 0)
        mix_out.start()

        def grad_rows(left, right, part, part_i, slot):
            n = part.n
            acc = jnp.zeros((n, width), F32)
            for b in range(nb):
                acc += nn(left(b, pl.ds(part_i * n, n)), right[b * BLK : (b + 1) * BLK, :])
            part.mine[slot] = acc.astype(BF)

        def down_grads(i, c):
            slot = slot_of(i)

            @pl.when(i == 2)
            def _():
                for p in downs:
                    p.core(0).wait_send()

            for k, p in enumerate(downs):
                grad_rows(lambda b, n: act_t[shards - 1 - i, b, n, :], g_low, p, k, slot)
            hooks_at(i, {
                0: [p.c0 for p in downs],
                1: [downs[0].f, downs[0].xs, downs[1].f],
                2: [p.c1 for p in downs],
                3: [p.s for p in downs],
            })
            return c

        lax.fori_loop(0, shards, down_grads, 0)

        def backward(i, c):
            slot = 1 - i % 2

            @pl.when(i >= 2)
            def _():
                wait_weights(0, slot)

            def one_block(b, cc):
                ga = nt(g_low[rows(b), :], down_v[slot])
                gu = (slope[shards - 1 - i, rows(b), :].astype(F32) * ga).astype(BF)
                gup[rows(b), :] = gu
                g_hid[rows(b), :] += nt(gu, up_v[slot])
                return cc

            lax.fori_loop(0, nb, one_block, 0)

            for back in (0, 1):

                @pl.when(i == back)
                def _():
                    start_weights(back + 2, 1 - back)

            @pl.when(i == 2)
            def _():
                for p in ups:
                    p.core(0).wait_send()

            for k, p in enumerate(ups):
                grad_rows(lambda b, n: ht[b, n, :], gup, p, k, slot_of(i))
            hooks_at(i, {
                0: [p.c0 for p in ups],
                1: [p.f for p in ups] + [downs[1].xs],
                2: [p.c1 for p in ups],
                3: [p.s for p in ups] + [downs[0].r],
            })
            return c

        lax.fori_loop(0, shards, backward, 0)
        mix_out.wait()

    pl.run_scoped(
        project,
        pltpu.VMEM((nw, width, BLK), BF),
        pltpu.VMEM((all_pairs, nw * BLK, 128), BF),
        pltpu.VMEM((all_pairs, nw * BLK, 128), BF),
        pltpu.VMEM((nw, width, BLK), BF),
        pltpu.VMEM((nb, row_blocks, BLK, BLK), F32),
        pltpu.VMEM((nb, width, BLK), F32),
    )
    pl.run_scoped(
        dense,
        pltpu.VMEM((own, width), BF),
        pltpu.VMEM((width, width), BF),
        pltpu.VMEM((2, width, width), BF),
        pltpu.VMEM((2, width, width), BF),
        pltpu.VMEM((own, width), BF),
        pltpu.VMEM((nb, width, BLK), BF),
        pltpu.VMEM((shards, nb, width, BLK), BF),
        pltpu.VMEM((shards, own, width), BF),
    )

    def attention(g_v, k_v, v_v, kt_v, delta, bias, dk, dv, dqt, dkt, dvt):
        gain1 = vec_all[0, 0:1, :].astype(F32)
        for i in range(1, groups):
            gain1 = gain1 + vec_all[i, 0:1, :].astype(F32)
        def keys(hf):
            base = pl.multiple_of(hf * half, 128)
            return (
                fetch(k_i.at[pl.ds(hf * pairs, pairs)], k_v, 0),
                fetch(v_i.at[pl.ds(hf * pairs, pairs)], v_v, 1),
                fetch(kt_i.at[:, pl.ds(base, half), :], kt_v, 2),
            )

        for c in keys(far_half):
            c.start()

        def between(out_v, ctxt_v):
            low_v = ctx_v
            o_in, c_in = fetch(out_w.at[0], out_v, 6), fetch(ctxt, ctxt_v, 7)
            o_in.start()
            c_in.start()
            o_in.wait()
            c_in.wait()

            def after(b, c):
                g = g_hid[rows(b), :]
                n = xhat[rows(b), :]
                vec_acc[0:1, :] += jnp.sum(g * n, axis=0, keepdims=True)
                vec_acc[1:2, :] += jnp.sum(g, axis=0, keepdims=True)
                e = g * gain1
                res = inv[rows(b), 0:1] * (e - mean(e) - n * mean(e * n))
                g_hid[rows(b), :] = res
                low = res.astype(BF)
                low_v[rows(b), :] = low
                gc = nt(low, out_v[...]).astype(BF)
                for i in range(all_pairs):
                    g_v[i, rows(b), :] = gc[:, i * 128 : (i + 1) * 128]
                prod = nt(out_v[...], low).astype(BF).astype(F32) * ctxt_v[b]
                for i in range(2 * all_pairs):
                    delta[b, i] = jnp.sum(prod[i * HEAD_WIDTH : (i + 1) * HEAD_WIDTH, :], axis=0, keepdims=True)
                return c

            lax.fori_loop(0, nb, after, 0)
            vstep(0).start()
            ups[0].xs()

            def grad_out(i, c):
                @pl.when(i == 2)
                def _():
                    out_c.core(0).wait_send()

                base = pl.multiple_of(shard_of(i) * shard_rows, 16)
                acc = jnp.zeros((shard_rows, width), F32)
                for b in range(nb):
                    acc += nn(ctxt_v[b, pl.ds(base, shard_rows), :].astype(BF), low_v[b * BLK : (b + 1) * BLK, :])
                out_c.mine[slot_of(i)] = acc.astype(BF)
                hooks_at(i, {0: [out_c.c0], 1: [out_c.f], 2: [out_c.c1], 3: [out_c.s]})
                return c

            lax.fori_loop(0, shards, grad_out, 0)
            downs[0].yy()
            downs[1].r()

        pl.run_scoped(
            between,
            pltpu.VMEM((width, width), BF),
            pltpu.VMEM((nb, width, BLK), F32),
        )
        def unit(hf, t):
            j, i = t // pairs, t % pairs
            p = hf * pairs + i
            ws = window_start(h, j, nb, row_blocks)

            @pl.when(i == 0)
            def _():
                for kb in range(row_blocks):
                    bias[kb] = mask_of(seg[ws + kb], seg[HALO + j])

            q = q_v[p, rows(j), :]
            g = g_v[p, rows(j), :]
            lane = lax.broadcasted_iota(jnp.int32, q.shape, 1)
            qm = [jnp.where(lane // HEAD_WIDTH == hh, q, jnp.zeros_like(q)) for hh in range(2)]
            gm = [jnp.where(lane // HEAD_WIDTH == hh, g, jnp.zeros_like(g)) for hh in range(2)]
            acc = [jnp.zeros((HEAD_WIDTH, BLK), F32) for _ in range(2)]
            for kb in range(row_blocks):
                kblk = k_v[i, rows(ws + kb), :]
                vblk = v_v[i, rows(ws + kb), :]
                add_k = None
                for hh in range(2):
                    head = 2 * p + hh
                    s = nt(kblk, qm[hh]) + bias[kb]
                    prob = jnp.exp(s - lse[j, head])
                    gp = nt(vblk, gm[hh])
                    gs = (prob * (gp - delta[j, head])).astype(BF)
                    one_v = nn(prob.astype(BF), gm[hh])
                    one_k = nn(gs, qm[hh])
                    add_k, add_v = (one_k, one_v) if add_k is None else (add_k + one_k, add_v + one_v)
                    at = pl.multiple_of((2 * i + hh) * HEAD_WIDTH, HEAD_WIDTH)
                    acc[hh] += nn(kt_v[ws + kb, pl.ds(at, HEAD_WIDTH), :], gs)
                dk[i, rows(ws + kb), :] += add_k
                dv[i, rows(ws + kb), :] += add_v
            for hh in range(2):
                at = pl.multiple_of((2 * i + hh) * HEAD_WIDTH, HEAD_WIDTH)
                dqt[j, pl.ds(at, HEAD_WIDTH), :] = (acc[hh] * HEAD_WIDTH**-0.5).astype(BF)

        def attend_half(hf, plan, then):
            dk[...] = jnp.zeros_like(dk)
            dv[...] = jnp.zeros_like(dv)

            def body(t, c):
                hooks_at(t, plan)
                unit(hf, t)
                return c

            lax.fori_loop(0, nb * pairs, body, 0)
            for step in then:
                step()
            for b in range(nw):
                lo, hi = b * BLK, (b + 1) * BLK
                dkt[b] = jnp.concatenate([dk[p, lo:hi, :].astype(BF) for p in range(pairs)], axis=1).T
                dvt[b] = jnp.concatenate([dv[p, lo:hi, :].astype(BF) for p in range(pairs)], axis=1).T

        def weight_grads(which, slot):
            at = pl.multiple_of(which * shard_rows, 16)
            acc = jnp.zeros((shard_rows, width), F32)
            for j in range(nb):
                acc += nn(dqt[j, pl.ds(at, shard_rows), :], x_v[(HALO + j) * BLK : (HALO + j + 1) * BLK, :])
            q_c.mine[slot] = acc.astype(BF)
            for c, src in ((k_c, dkt), (v_c, dvt)):
                acc = jnp.zeros((shard_rows, width), F32)
                for b in range(nw):
                    acc += nn(src[b, pl.ds(at, shard_rows), :], x_v[b * BLK : (b + 1) * BLK, :])
                c.mine[slot] = acc.astype(BF)

        def input_grads(hf, last):
            base = pl.multiple_of(hf * half, 128)
            wk, wv = w_v.at[1, pl.ds(base, half), :], w_v.at[2, pl.ds(base, half), :]

            def block(b):
                kb = jnp.concatenate([dk[p, rows(b), :].astype(BF) for p in range(pairs)], axis=1)
                vb = jnp.concatenate([dv[p, rows(b), :].astype(BF) for p in range(pairs)], axis=1)
                return nn(kb, wk[...]) + nn(vb, wv[...])

            def side(i, c):
                b = i + jnp.where(i >= HALO, nb, 0)
                total = block(b)
                if last:
                    total = total + gx_side[rows(i), :].astype(F32)
                gx_side[rows(i), :] = total.astype(BF)
                return c

            lax.fori_loop(0, 2 * HALO, side, 0)

            def inner(j, c):
                g_hid[rows(j), :] += block(j + HALO) + nn(dqt[j].T, w_v[0, pl.ds(base, half), :])
                return c

            return lambda: lax.fori_loop(0, nb, inner, 0)

        for c in keys(far_half):
            c.wait()
        d0, d1 = downs
        u0, u1 = ups
        vs = [functools.partial(vnext, i) for i in range(len(vec_ids))]
        attend_half(far_half, {
            1: [vs[0]], 2: [d0.zz], 3: [u1.xs, vs[1]], 4: [d1.yy], 5: [u0.r, vs[2]], 6: [d0.w, d1.zz], 7: [vs[3]], 8: [d0.u],
        }, [u0.yy, out_c.xs])
        for c in keys(x_half):
            c.start()
        u1.r()
        d1.w()
        weight_grads(1 - core, 0)
        for p in (q_c, k_c, v_c):
            p.c0()
        weight_grads(core, 1)
        for p in (q_c, k_c, v_c):
            p.f()
            p.xs()
        u0.zz()
        d0.end()
        input_grads(far_half, False)()
        d1.u()
        out_c.r()
        for c in keys(x_half):
            c.wait()
        attend_half(x_half, {
            1: [d1.end, *vs[4:]], 2: [u1.yy], 3: [u0.w], 4: [out_c.yy], 5: [u1.zz, u0.u], 6: [out_c.zz], 7: [u0.end],
        }, [u1.w, out_c.w])
        for p in (q_c, k_c, v_c):
            p.core(0).wait_send()
        weight_grads(1 - core, 0)
        for p in (q_c, k_c, v_c):
            p.c1()
        weight_grads(core, 2)
        u1.u()
        out_c.u()
        for p in (q_c, k_c, v_c):
            p.s()
            p.r()
        finish = input_grads(x_half, True)

        @pl.when(h > 0)
        def _():
            to_left.start()

        @pl.when(h < groups - 1)
        def _():
            to_right.start()

        for p in (q_c, k_c, v_c):
            p.yy()
        for p in (q_c, k_c, v_c):
            p.zz()
        finish()
        tok_out = fetch(g_hid, o_tok, 3)
        tok_out.start()
        u1.end()
        out_c.end()
        for p in (q_c, k_c, v_c):
            p.w()
        for p in (q_c, k_c, v_c):
            p.u()
        for p in (q_c, k_c, v_c):
            p.end()
        tok_out.wait()

    to_left = remote(gx_side.at[pl.ds(0, halo), :], o_right, side_send.at[0], side_recv.at[0], (r, h - 1))
    to_right = remote(gx_side.at[pl.ds(halo, halo), :], o_left, side_send.at[1], side_recv.at[1], (r, h + 1))

    pl.run_scoped(
        attention,
        pltpu.VMEM((all_pairs, own, 128), BF),
        pltpu.VMEM((pairs, nw * BLK, 128), BF),
        pltpu.VMEM((pairs, nw * BLK, 128), BF),
        pltpu.VMEM((nw, half, BLK), BF),
        pltpu.VMEM((nb, 2 * all_pairs, 1, BLK), F32),
        pltpu.VMEM((row_blocks, BLK, BLK), F32),
        pltpu.VMEM((pairs, nw * BLK, 128), F32),
        pltpu.VMEM((pairs, nw * BLK, 128), F32),
        pltpu.VMEM((nb, half, BLK), BF),
        pltpu.VMEM((nw, half, BLK), BF),
        pltpu.VMEM((nw, half, BLK), BF),
    )

    o_vec[...] = vacc[len(vec_ids) - 1]
    for g in (gq, go, gu, gd):
        g.sent()
    for p in parts:
        p.done()
    for i in range(len(vec_ids)):
        vstep(i).wait_send()

    @pl.when(h > 0)
    def _():
        to_left.wait_send()
        to_right.wait_recv()

    @pl.when(h == 0)
    def _():
        gx_side[pl.ds(0, halo), :] = jnp.zeros((halo, width), BF)
        pltpu.sync_copy(gx_side.at[pl.ds(0, halo), :], o_left)

    @pl.when(h < groups - 1)
    def _():
        to_right.wait_send()
        to_left.wait_recv()

    @pl.when(h == groups - 1)
    def _():
        gx_side[pl.ds(halo, halo), :] = jnp.zeros((halo, width), BF)
        pltpu.sync_copy(gx_side.at[pl.ds(halo, halo), :], o_right)


def layer(groups, row_blocks, row_devices, tok, cot, qkv_own, out_own, up_own, down_own, vec_own, lengths):
    own, width = tok.shape
    shard_rows = width // groups
    nb = own // BLK
    nw = nb + 2 * HALO
    all_pairs = width // 128
    bits = other_bits(row_devices)
    split = width // 2
    chunks = [(name, lo, split) for name in ("down", "up") for lo in range(0, width, split)]
    chunks += [(name, 0, shard_rows) for name in ("out", "q", "k", "v")]
    hops = 4 + len(bits)
    scratch = [
        pltpu.VMEM((3, width, width), BF),
        pltpu.VMEM((nw * BLK, width), BF),
        pltpu.VMEM((all_pairs, own, 128), BF),
        pltpu.VMEM((own, width), BF),
        pltpu.VMEM((nb, 2 * all_pairs, 1, BLK), F32),
        pltpu.VMEM((nw, 1, BLK), F32),
        pltpu.VMEM((groups,) + vec_own.shape, BF),
        pltpu.VMEM((own, width), F32),
        pltpu.VMEM((own, 128), F32),
        pltpu.VMEM((own, width), F32),
        pltpu.VMEM((2 * HALO * BLK, width), BF),
        pltpu.VMEM((8, width), F32),
        pltpu.VMEM((hops, 8, width), F32),
        pltpu.VMEM((hops, 8, width), F32),
    ]
    for _, _, n in chunks:
        scratch += [
            pltpu.VMEM((3, n, width), BF),
            pltpu.VMEM((2, n, width), BF),
            pltpu.VMEM((n, width), BF),
            pltpu.VMEM((n // 2, width), BF),
            pltpu.VMEM((n // 4, width), BF),
            pltpu.VMEM((max(1, len(bits)), n // 4, width), BF),
        ]
    dma = pltpu.SemaphoreType.DMA
    scratch += [dma((len(chunks), 8 + len(bits)))] * 2 + [dma((len(chunks), 3))] + [dma((4, 12))] * 2
    scratch += [dma((2,))] * 4 + [dma((groups - 1,))] * 2 + [dma((hops,))] * 2 + [dma((8,))]
    s = jax.ShapeDtypeStruct
    side = s((HALO * BLK, width), BF)
    outs = [
        (s((own, width), BF), ANY),
        (s((width, width), BF), ANY),
        (s((width, width), BF), ANY),
        (s((shard_rows, width), BF), ANY),
        (s((3, shard_rows, width), BF), ANY),
        (s((own, width), F32), ANY),
        (side, ANY),
        (side, ANY),
        (s((8, width), F32), VM),
        (s((1, width, width), BF), ANY),
        (s((1, groups * width, width), BF), ANY),
        (s((1, groups * width, width), BF), ANY),
        (s((nb, width, BLK), F32), ANY),
        (s((all_pairs, nw * BLK, 128), BF), ANY),
        (s((all_pairs, nw * BLK, 128), BF), ANY),
        (s((nw, width, BLK), BF), ANY),
    ]
    return pl.pallas_call(
        functools.partial(layer_kernel, groups, row_blocks, bits, chunks),
        out_shape=[o[0] for o in outs],
        in_specs=[ANY] * 6 + [VM] * 2,
        out_specs=[o[1] for o in outs],
        scratch_shapes=scratch,
        compiler_params=pltpu.CompilerParams(collective_id=0, has_side_effects=True, vmem_limit_bytes=VMEM_LIMIT),
        name="layer",
    )(tok, cot, qkv_own, out_own, up_own, down_own, vec_own, lengths)


def local(
    groups, row_devices,
    tokens, lengths, w_query, w_key, w_value, w_out, w_up, w_down,
    gain_first, shift_first, gain_second, shift_second, cotangent,
):
    packed_rows = lengths.shape[0]
    own, width = tokens.shape
    row_length = groups * own // packed_rows
    row_blocks = row_length // BLK
    h = lax.axis_index("heads")
    n_vec = gain_first.shape[0]
    vec_own = jnp.stack([gain_first, shift_first, gain_second, shift_second])
    vec_own = lax.dynamic_update_slice(jnp.zeros((16, width), BF), vec_own, (0, n_vec * h))
    qkv_own = jnp.stack([w_query.T, w_key.T, w_value.T])
    mixed, o_down, o_up, o_out, o_qkv, gx, gx_left, gx_right, o_vec = layer(
        groups, row_blocks, row_devices, tokens, cotangent, qkv_own, w_out[None], w_up[None], w_down[None], vec_own, lengths
    )[:9]
    halo = HALO * BLK
    o_tok = gx + jnp.pad(gx_left.astype(F32), ((0, own - halo), (0, 0))) + jnp.pad(gx_right.astype(F32), ((own - halo, 0), (0, 0)))
    mine = lax.dynamic_slice(o_vec, (0, n_vec * h), (4, n_vec))
    wide = lambda a: a.astype(F32)
    return (
        mixed, o_tok, wide(o_qkv[0].T), wide(o_qkv[1].T), wide(o_qkv[2].T), wide(o_out), wide(o_up), wide(o_down),
        mine[0], mine[1], mine[2], mine[3],
    )


def solution(mesh):
    both, heads = P(("rows", "heads"), None), P("heads")
    cols, rows = P(None, "heads"), P("heads", None)
    return jax.shard_map(
        functools.partial(local, mesh.shape["heads"], mesh.shape["rows"]),
        mesh=mesh,
        in_specs=(both, P("rows", None), cols, cols, cols, rows, cols, rows, heads, heads, heads, heads, both),
        out_specs=(both, both, cols, cols, cols, rows, cols, rows, heads, heads, heads, heads),
        check_vma=False,
    )
```

```python
import functools

import jax
import jax.numpy as jnp
from jax import lax
from jax.experimental import pallas as pl
from jax.experimental.pallas import tpu as pltpu
from jax.sharding import PartitionSpec as P

MESH = pl.DeviceIdType.MESH
BF = jnp.bfloat16
F32 = jnp.float32
HEAD_WIDTH = 64
LONGEST_DOC = 512
BLK = 256
HALO = LONGEST_DOC // BLK
NORM_EPS = 1e-12
VMEM_LIMIT = 62 * 1024 * 1024


def nt(left, right):
    return lax.dot_general(left, right, (((1,), (1,)), ((), ())), preferred_element_type=F32)


def nn(left, right):
    return lax.dot_general(left, right, (((1,), (0,)), ((), ())), preferred_element_type=F32)


def flip(index, bit):
    return index + bit - 2 * bit * ((index // bit) % 2)


def place():
    r, h = lax.axis_index("rows"), lax.axis_index("heads")
    return r, h


def greet(ids):
    barrier = pltpu.get_barrier_semaphore()
    for who in ids:
        pl.semaphore_signal(barrier, inc=1, device_id=who, device_id_type=MESH)
    pl.semaphore_wait(barrier, len(ids))


def group_of(r, h, groups):
    return [(r, lax.rem(h + i, groups)) for i in range(1, groups)]


def remote(src, dst, send, recv, who):
    return pltpu.make_async_remote_copy(
        src_ref=src, dst_ref=dst, send_sem=send, recv_sem=recv, device_id=who, device_id_type=MESH
    )


class Gather:
    def __init__(self, own, full, sems, at):
        self.own, self.full, self.sems, self.at = own, full, sems, at
        self.n = own.shape[1]
        self.u = self.n // 12
        r, h = place()
        self.r, self.h = r, h
        y, z = r % 2, (r // 2) % 2
        self.k = 2 * z + y
        self.ky = 2 * z + 1 - y
        self.kz = 2 * (1 - z) + y
        self.kd = 3 - self.k
        self.hx = flip(h, 2)
        self.hc = flip(h, 1)
        self.by_x = (r, self.hx)
        self.by_c = (r, self.hc)
        self.by_y = (flip(r, 1), h)
        self.by_z = (flip(r, 2), h)

    def rows(self, shard, sub, count):
        u = self.u
        return pl.ds(pl.multiple_of(shard * self.n + sub * u, 16), count * u)

    def part(self, slot, who, shard, sub, count, own=False):
        dst = self.full.at[:, self.rows(shard, sub, count), :]
        src = self.own.at[:, self.rows(0, sub, count), :] if own else dst
        send, recv = self.sems
        return remote(src, dst, send.at[self.at, slot], recv.at[self.at, slot], who)

    def x_main(self):
        return self.part(0, self.by_x, self.h, 3 * self.k, 3, own=True)

    def x_diag(self):
        return self.part(1, self.by_x, self.h, 3 * self.kd, 1, own=True)

    def y_main(self):
        return self.part(2, self.by_y, self.hx, 3 * self.k, 3)

    def z_main(self):
        return self.part(3, self.by_z, self.hx, 3 * self.k, 3)

    def y_diag(self):
        return self.part(4, self.by_y, self.hx, 3 * self.kz + 1, 1)

    def z_diag(self):
        return self.part(5, self.by_z, self.hx, 3 * self.ky + 2, 1)

    def c_own(self):
        return self.part(6, self.by_c, self.h, 0, 12, own=True)

    def c_part(self, i):
        return self.part(7 + i, self.by_c, self.hx, 3 * (self.k, self.ky, self.kz, self.kd)[i], 3)

    def local(self):
        send, _ = self.sems
        return pltpu.make_async_copy(
            self.own, self.full.at[:, self.rows(self.h, 0, 12), :], send.at[self.at, 11]
        )

    def start_x(self):
        self.x_main().start()
        self.x_diag().start()

    def start_main(self):
        self.x_main().start()

    def start_diag(self):
        self.x_diag().start()

    def start_c(self, keep):
        self.c_own().start()
        if keep:
            self.local().start()

    def step_x(self):
        self.x_main().wait_recv()
        self.y_main().start()
        self.z_main().start()
        self.c_part(0).start()

    def step_yz(self):
        self.y_main().wait_recv()
        self.z_diag().start()
        self.c_part(1).start()
        self.z_main().wait_recv()
        self.y_diag().start()
        self.c_part(2).start()

    def step_diag(self):
        self.x_diag().wait_recv()
        self.y_diag().wait_recv()
        self.z_diag().wait_recv()
        self.c_part(3).start()

    def near(self, keep):
        self.c_own().wait_recv()
        if keep:
            self.local().wait()

    def far(self):
        for i in range(4):
            self.c_part(i).wait_recv()

    def sent(self):
        for copy in (self.x_main(), self.x_diag(), self.y_main(), self.z_main(), self.y_diag(), self.z_diag(), self.c_own()):
            copy.wait_send()
        for i in range(4):
            self.c_part(i).wait_send()


def window_start(h, j, own_blocks, row_blocks):
    g = own_blocks * h + j
    first = own_blocks * h - HALO
    row = row_blocks * (g // row_blocks)
    return jnp.clip(row, first, first + own_blocks + 2 * HALO - row_blocks) - first


def mask_of(keys, queries):
    down = jnp.broadcast_to(keys, (8, BLK)).T[:, 0:1]
    return jnp.where(down == queries, 0.0, -1e30).astype(F32)


ANY = pl.BlockSpec(memory_space=pl.ANY)
VM = pl.BlockSpec(memory_space=pltpu.VMEM)


def gelu_parts(u):
    bell = jnp.exp(-0.5 * u * u)
    base = 1.0 + (0.3275911 * 0.7071067811865476) * jnp.abs(u)
    t = pl.reciprocal(base, approx=True)
    t = t * (2.0 - base * t)
    poly = t * (0.127414796 + t * (-0.142248368 + t * (0.7107068705 + t * (-0.7265760135 + t * 0.5307027145))))
    tail = poly * bell
    cdf = jnp.where(u >= 0.0, 1.0 - tail, tail)
    return u * cdf, cdf + u * (bell * 0.3989422804014327)


class Sum:
    def __init__(self, n, bits, bufs, sems, at):
        self.n, self.bits, self.at = n, bits, at
        self.mine, self.rc, self.rx, self.ry, self.rz, self.rest = bufs
        self.send, self.recv, self.keep = sems
        r, h = place()
        self.y, self.z = r % 2, (r // 2) % 2
        self.by_x, self.by_c = (r, flip(h, 2)), (r, flip(h, 1))
        self.by_y, self.by_z = (flip(r, 1), h), (flip(r, 2), h)
        self.by_rest = [(flip(r, b), h) for b in bits]

    def copy(self, slot, src, dst, who):
        return remote(src, dst, self.send.at[self.at, slot], self.recv.at[self.at, slot], who)

    def core(self, i):
        return self.copy(i, self.mine.at[0], self.rc.at[i], self.by_c)

    def x(self):
        return self.copy(2, self.mine.at[1], self.rx, self.by_x)

    def half(self, which):
        return pl.ds(pl.multiple_of(which * (self.n // 2), 16), self.n // 2)

    def quarter(self, half, which):
        return pl.ds(pl.multiple_of(half * (self.n // 2) + which * (self.n // 4), 16), self.n // 4)

    def own(self):
        return self.mine.at[2, self.quarter(self.y, self.z), :]

    def landed(self, half, which):
        return self.rx.at[self.quarter(half, which), :]

    def y_down(self):
        return self.copy(3, self.mine.at[2, self.half(1 - self.y), :], self.ry, self.by_y)

    def z_down(self):
        return self.copy(4, self.mine.at[2, self.quarter(self.y, 1 - self.z), :], self.rz, self.by_z)

    def z_up(self):
        return self.copy(5, self.own(), self.landed(self.y, self.z), self.by_z)

    def y_up(self):
        return self.copy(6, self.own(), self.landed(self.y, self.z), self.by_y)

    def y_up2(self):
        return self.copy(7, self.landed(self.y, 1 - self.z), self.landed(self.y, 1 - self.z), self.by_y)

    def swap(self, i):
        return self.copy(8 + i, self.own(), self.rest.at[i], self.by_rest[i])

    def add(self, ref, got):
        ref[...] = (ref[...].astype(F32) + got[...].astype(F32)).astype(BF)

    def c0(self):
        self.core(0).start()

    def f(self):
        self.core(0).wait_recv()
        self.add(self.mine.at[1], self.rc.at[0])

    def xs(self):
        self.x().start()

    def c1(self):
        self.core(1).start()

    def s(self):
        self.core(1).wait_recv()
        self.add(self.mine.at[2], self.rc.at[1])

    def r(self):
        self.x().wait_recv()
        self.add(self.mine.at[2], self.rx)
        self.y_down().start()

    def yy(self):
        self.y_down().wait_recv()
        self.add(self.mine.at[2, self.half(self.y), :], self.ry)
        self.z_down().start()

    def zz(self):
        self.z_down().wait_recv()
        self.add(self.own(), self.rz)
        if self.bits:
            self.swap(0).start()

    def w(self):
        for i in range(len(self.bits)):
            self.swap(i).wait_recv()
            self.swap(i).wait_send()
            self.add(self.own(), self.rest.at[i])
            if i + 1 < len(self.bits):
                self.swap(i + 1).start()
        self.z_up().start()
        self.y_up().start()

    def u(self):
        self.z_up().wait_recv()
        self.y_up2().start()

    def outs(self, out, lo):
        def local(i, src, rows):
            start = pl.multiple_of(lo + rows.start, 16)
            return pltpu.make_async_copy(src, out.at[pl.ds(start, rows.size), :], self.keep.at[self.at, i])

        mine, beside, other = self.quarter(self.y, self.z), self.quarter(self.y, 1 - self.z), self.half(1 - self.y)
        return (
            local(0, self.own(), mine),
            local(1, self.rx.at[beside, :], beside),
            local(2, self.rx.at[other, :], other),
        )

    def e(self, out, lo):
        self.y_up().wait_recv()
        self.y_up2().wait_recv()
        for c in self.outs(out, lo):
            c.start()

    def sent(self, out, lo):
        for c in (self.core(1), self.x(), self.y_down(), self.z_down(), self.z_up(), self.y_up(), self.y_up2()):
            c.wait_send()
        for c in self.outs(out, lo):
            c.wait()


def other_bits(count):
    bits, b = [], 4
    while b < count:
        bits.append(b)
        b *= 2
    return tuple(bits)


def hooks_at(t, plan):
    for at, steps in plan.items():

        @pl.when(t == at)
        def _():
            for step in steps:
                step()


def layer_kernel(
    groups, row_blocks, bits, chunks,
    tok, cot, qkv_own, out_own, up_own, down_own, vec_own, lengths,
    mixed, o_down, o_up, o_out, o_qkv, o_tok, o_left, o_right, o_vec,
    out_w, up_w, down_w, ctxt, k_i, v_i, kt_i,
    w_v, x_v, q_v, ctx_v, lse, seg, vec_all, xhat, inv, g_hid, gx_side, vec_acc, vin, vacc, *scratch,
):
    r, h = place()
    own, width = tok.shape
    nb = own // BLK
    nw = nb + 2 * HALO
    halo = HALO * BLK
    shards = groups
    all_pairs = q_v.shape[0]
    pairs = all_pairs // 2
    half = pairs * 128
    shard_rows = half // 2
    x_half = (h // 2) % 2
    far_half = 1 - x_half
    core = h % 2
    rows = lambda b: pl.ds(pl.multiple_of(b * BLK, BLK), BLK)
    mean = lambda v: jnp.mean(v, axis=1, keepdims=True)
    n_chunks = len(chunks)
    (send, recv, keep, gsend, grecv, in_send, in_recv, side_send, side_recv, psend, precv, vsend, vrecv, loc) = scratch[6 * n_chunks :]
    sems = (send, recv, keep)
    outs = {"down": o_down, "up": o_up, "out": o_out, "q": o_qkv.at[0], "k": o_qkv.at[1], "v": o_qkv.at[2]}
    parts = [Sum(n, bits, scratch[6 * i : 6 * i + 6], sems, i) for i, (_, _, n) in enumerate(chunks)]
    by_name = {}
    for part, (name, lo, _) in zip(parts, chunks):
        part.end = functools.partial(part.e, outs[name], lo)
        part.done = functools.partial(part.sent, outs[name], lo)
        by_name.setdefault(name, []).append(part)
    downs, ups, (out_c,) = by_name["down"], by_name["up"], by_name["out"]
    q_c, k_c, v_c = (by_name[name][0] for name in "qkv")
    one = parts[0]
    gq = Gather(qkv_own, w_v, (gsend, grecv), 0)
    go = Gather(out_own, out_w, (gsend, grecv), 1)
    gu = Gather(up_own, up_w, (gsend, grecv), 2)
    gd = Gather(down_own, down_w, (gsend, grecv), 3)

    def shard_of(i):
        across = 1 - i // 2
        other = 1 - i % 2
        return h + across * (2 - 4 * x_half) + other * (1 - 2 * core)

    def slot_of(i):
        return (i % 2) * (1 + i // 2)

    def fetch(src, dst, i):
        return pltpu.make_async_copy(src, dst, loc.at[i])

    vec_ids = [one.by_c, one.by_x, one.by_y, one.by_z] + one.by_rest

    def vstep(i):
        src = vec_acc if i == 0 else vacc.at[i - 1]
        return remote(src, vin.at[i], vsend.at[i], vrecv.at[i], vec_ids[i])

    def vnext(i):
        vstep(i).wait_recv()
        vacc[i] = (vec_acc[...] if i == 0 else vacc[i - 1]) + vin[i]
        if i + 1 < len(vec_ids):
            vstep(i + 1).start()

    def project(vt, k_s, v_s, kt_s, bias, ctx_t):
        total_blocks = groups * nb
        def to_right(i):
            src, dst = pl.ds(own - halo + i * BLK, BLK), pl.ds(i * BLK, BLK)
            return remote(tok.at[src, :], x_v.at[dst, :], in_send.at[i], in_recv.at[i], (r, h + 1))

        def to_left(i):
            src, dst = pl.ds(i * BLK, BLK), pl.ds(halo + own + i * BLK, BLK)
            return remote(tok.at[src, :], x_v.at[dst, :], in_send.at[HALO + i], in_recv.at[HALO + i], (r, h - 1))

        def both(to, step):
            for i in range(HALO):
                step(to(i))

        start, arrived, gone = (lambda c: c.start()), (lambda c: c.wait_recv()), (lambda c: c.wait_send())
        even = h % 2 == 0
        slow_right = jnp.logical_and(h % 2 == 1, h < groups - 1)
        slow_left = jnp.logical_and(even, h > 0)

        odd = h % 2 == 1

        def par(i):
            who = (r, lax.rem(h + 1 + i, groups))
            return remote(vec_own, vec_all.at[h], psend.at[i], precv.at[groups - 2 - i], who)

        def par_from(i):
            return remote(vec_own, vec_all.at[h], psend.at[i], precv.at[i], (r, lax.rem(h + 1 + i, groups)))

        mine = fetch(tok, x_v.at[pl.ds(halo, own), :], 0)
        mine.start()
        greet(group_of(r, h, groups) + [one.by_y, one.by_z] + one.by_rest)

        @pl.when(slow_right)
        def _():
            to_right(HALO - 1).start()

        @pl.when(slow_left)
        def _():
            to_left(0).start()

        @pl.when(even)
        def _():
            both(to_right, start)

        @pl.when(odd)
        def _():
            both(to_left, start)

        gq.start_c(True)
        gq.start_main()
        for i in range(groups - 1):
            par(i).start()
        vec_all[h] = vec_own[...]

        @pl.when(h == 0)
        def _():
            x_v[pl.ds(0, halo), :] = jnp.zeros((halo, width), BF)

        @pl.when(h == groups - 1)
        def _():
            x_v[pl.ds(halo + own, halo), :] = jnp.zeros((halo, width), BF)

        packed, docs = lengths.shape
        down = lax.broadcasted_iota(jnp.int32, (docs, docs), 0)
        across = lax.broadcasted_iota(jnp.int32, (docs, docs), 1)
        for b in range(nw):
            g = nb * h - HALO + b
            row = jnp.clip(g // row_blocks, 0, packed - 1)
            sizes = lengths[pl.ds(row, 1), :].astype(F32)
            ends = jnp.sum(jnp.where(across <= down, jnp.broadcast_to(sizes, (docs, docs)), 0.0), axis=1, keepdims=True)
            at = (lax.broadcasted_iota(jnp.int32, (docs, BLK), 1) + (g % row_blocks) * BLK).astype(F32)
            ids = jnp.sum(jnp.where(at >= ends, 1.0, 0.0), axis=0, keepdims=True) + (row * docs).astype(F32)
            inside = jnp.logical_and(g >= 0, g < total_blocks)
            seg[b] = jnp.where(inside, ids, -1.0)
        for j in range(nb):
            ws = window_start(h, j, nb, row_blocks)
            for kb in range(row_blocks):
                bias[j, kb] = mask_of(seg[ws + kb], seg[HALO + j])

        def project_keys(hx, b):
            base = pl.multiple_of(hx * half, 128)
            xb = x_v[rows(b), :]
            wk = w_v[1, pl.ds(base, half), :]
            wv = w_v[2, pl.ds(base, half), :]
            key = nt(xb, wk).astype(BF)
            value = nt(xb, wv).astype(BF)
            for i in range(pairs):
                k_s[hx * pairs + i, rows(b), :] = key[:, i * 128 : (i + 1) * 128]
                v_s[hx * pairs + i, rows(b), :] = value[:, i * 128 : (i + 1) * 128]
            kt_s[b, pl.ds(base, half), :] = nt(wk, xb).astype(BF)
            vt[b, pl.ds(base, half), :] = nt(wv, xb).astype(BF)

        def project_query(hx, b):
            base = pl.multiple_of(hx * half, 128)
            xb = x_v[rows(b + HALO), :]
            query = nt(xb, w_v[0, pl.ds(base, half), :]).astype(BF) * BF(HEAD_WIDTH**-0.5)
            for i in range(pairs):
                q_v[hx * pairs + i, rows(b), :] = query[:, i * 128 : (i + 1) * 128]

        def side_keys(hx, first):
            def body(b, c):
                project_keys(hx, first + b)
                return c

            lax.fori_loop(0, HALO, body, 0)

        def attend(hx, t):
            j = jnp.where(odd, t // pairs, nb - 1 - t // pairs)
            p = hx * pairs + t % pairs
            ws = window_start(h, j, nb, row_blocks)
            q = q_v[p, rows(j), :]
            lane = lax.broadcasted_iota(jnp.int32, q.shape, 1)
            for hh in range(2):
                head = 2 * p + hh
                qm = jnp.where(lane // HEAD_WIDTH == hh, q, jnp.zeros_like(q))
                scores = []
                top = None
                for kb in range(row_blocks):
                    s = nt(k_s[p, rows(ws + kb), :], qm) + bias[j, kb]
                    m = jnp.max(s, axis=0, keepdims=True)
                    top = m if top is None else jnp.maximum(top, m)
                    scores.append(s)
                total = jnp.zeros_like(top)
                acc = jnp.zeros((HEAD_WIDTH, BLK), F32)
                at = pl.multiple_of(head * HEAD_WIDTH, HEAD_WIDTH)
                for kb in range(row_blocks):
                    e = jnp.exp(scores[kb] - top)
                    total = total + jnp.sum(e, axis=0, keepdims=True)
                    acc = acc + nn(vt[ws + kb, pl.ds(at, HEAD_WIDTH), :], e.astype(BF))
                ctx_t[j, pl.ds(at, HEAD_WIDTH), :] = acc / total
                lse[j, head] = top + jnp.log(total)

        def attend_all(hx, plan):
            def body(t, c):
                hooks_at(t, plan)
                attend(hx, t)
                return c

            lax.fori_loop(0, nb * pairs, body, 0)

        def slow_block(near):
            @pl.when(slow_right)
            def _():
                to_left(0 if near else 1).wait_recv()

            @pl.when(slow_left)
            def _():
                to_right(1 if near else 0).wait_recv()

            project_keys(x_half, jnp.where(odd, HALO + nb + (0 if near else 1), 1 if near else 0))

        def more_halo():
            @pl.when(slow_right)
            def _():
                to_right(0).start()

            @pl.when(slow_left)
            def _():
                to_left(1).start()

        mine.wait()
        gq.near(True)
        for b in range(nb):
            project_query(x_half, b)
        lax.fori_loop(HALO, HALO + nb, lambda b, c: (project_keys(x_half, b), c)[1], 0)

        @pl.when(odd)
        def _():
            both(to_right, arrived)

        @pl.when(even)
        def _():
            both(to_left, arrived)

        side_keys(x_half, jnp.where(odd, 0, HALO + nb))
        last = jnp.where(odd, nw - 1, 0)
        for i in range(all_pairs):
            k_s[i, rows(last), :] = jnp.zeros((BLK, 128), BF)
        vt[last] = jnp.zeros((width, BLK), BF)
        attend_all(x_half, {
            0: [lambda: go.start_c(True), lambda: gu.start_c(False)],
            3: [functools.partial(slow_block, True), gq.step_x, gq.start_diag, more_halo, lambda: gd.start_c(False)],
            6: [functools.partial(slow_block, False), go.start_x, gu.start_x], 8: [gq.step_yz],
        })
        go.step_x()
        gq.step_diag()
        gq.far()
        for b in range(nb):
            project_query(far_half, b)
        lax.fori_loop(0, nw, lambda b, c: (project_keys(far_half, b), c)[1], 0)
        keys_out = [fetch(a, b, i) for i, (a, b) in enumerate(((k_s, k_i), (v_s, v_i), (kt_s, kt_i)))]
        for c in keys_out:
            c.start()
        attend_all(far_half, {
            0: [gd.start_x], 1: [gu.step_x], 3: [go.step_yz], 7: [go.step_diag], 8: [gu.step_yz],
        })
        ctx_out = fetch(ctx_t, ctxt, 3)
        ctx_out.start()
        for j in range(nb):
            ctx_v[j * BLK : (j + 1) * BLK, :] = ctx_t[j].T.astype(BF)
        gd.step_x()
        go.near(True)
        go.far()
        for c in keys_out:
            c.wait()
        ctx_out.wait()
        for i in range(groups - 1):
            par(i).wait_send()
            par_from(i).wait_recv()

        @pl.when(h < groups - 1)
        def _():
            both(to_right, gone)

        @pl.when(h > 0)
        def _():
            both(to_left, gone)

    def dense(cot_v, out_v, up_v, down_v, hl, ht, act_t, slope):
        ffn, gup, mix_v, g_low = g_hid, hl, ctx_v, cot_v
        params = vec_all[0].astype(F32)
        for i in range(1, groups):
            params = params + vec_all[i].astype(F32)
        gain1, shift1, gain2, shift2 = (params[i : i + 1, :] for i in range(4))
        first = [fetch(a, b, i) for i, (a, b) in enumerate(((out_w.at[0], out_v), (cot, cot_v)))]
        for c in first:
            c.start()

        def weights(i, slot):
            if i == shards - 1:
                return fetch(up_own.at[0], up_v.at[slot], 4 + slot), fetch(down_own.at[0], down_v.at[slot], 6 + slot)
            here = pl.ds(pl.multiple_of(shard_of(i) * width, 16), width)
            return fetch(up_w.at[0, here, :], up_v.at[slot], 4 + slot), fetch(down_w.at[0, here, :], down_v.at[slot], 6 + slot)

        def start_weights(i, slot):
            for c in weights(i, slot):
                c.start()

        def wait_weights(i, slot):
            for c in weights(i, slot):
                c.wait()

        start_weights(3, 0)
        gu.near(False)
        gd.near(False)
        start_weights(2, 1)
        vec_acc[...] = jnp.zeros_like(vec_acc)
        for c in first:
            c.wait()

        def before(b, c):
            resid = x_v[rows(b + HALO), :].astype(F32) + nn(ctx_v[rows(b), :], out_v[...])
            cen = resid - mean(resid)
            rs = lax.rsqrt(mean(cen * cen) + NORM_EPS)
            n = cen * rs
            hidden = n * gain1 + shift1
            xhat[rows(b), :] = n
            inv[rows(b), :] = jnp.broadcast_to(rs, (BLK, 128))
            low = hidden.astype(BF)
            hl[rows(b), :] = low
            ht[b] = low.T
            ffn[rows(b), :] = hidden
            return c

        lax.fori_loop(0, nb, before, 0)
        gu.step_diag()
        gd.step_yz()

        def forward(i, c):
            slot = i % 2
            wait_weights(0, slot)
            for b in range(nb):
                up = nn(hl[rows(b), :], up_v[slot])
                active, deriv = gelu_parts(up)
                active = active.astype(BF)
                slope[i, rows(b), :] = deriv.astype(BF)
                act_t[i, b] = active.T
                ffn[rows(b), :] += nn(active, down_v[slot])
            return c

        def two(first, then):
            def body(i, c):
                forward(i, c)
                hooks_at(i, then)
                return c

            lax.fori_loop(first, first + 2, body, 0)

        two(0, {0: [gd.step_diag]})
        gu.far()
        gd.far()
        start_weights(1, 0)
        start_weights(0, 1)
        two(2, {})

        def middle(b, c):
            v = ffn[rows(b), :]
            cen = v - mean(v)
            rs = lax.rsqrt(mean(cen * cen) + NORM_EPS)
            n = cen * rs
            mix_v[rows(b), :] = (n * gain2 + shift2).astype(BF)
            ct = cot_v[rows(b), :].astype(F32)
            vec_acc[2:3, :] += jnp.sum(ct * n, axis=0, keepdims=True)
            vec_acc[3:4, :] += jnp.sum(ct, axis=0, keepdims=True)
            e = ct * gain2
            g = rs * (e - mean(e) - n * mean(e * n))
            g_hid[rows(b), :] = g
            g_low[rows(b), :] = g.astype(BF)
            return c

        lax.fori_loop(0, nb, middle, 0)
        mix_out = fetch(mix_v, mixed, 0)
        mix_out.start()

        def grad_rows(left, right, part, part_i, slot):
            n = part.n
            acc = jnp.zeros((n, width), F32)
            for b in range(nb):
                acc += nn(left(b, pl.ds(part_i * n, n)), right[b * BLK : (b + 1) * BLK, :])
            part.mine[slot] = acc.astype(BF)

        def down_grads(i, c):
            slot = slot_of(i)

            @pl.when(i == 2)
            def _():
                for p in downs:
                    p.core(0).wait_send()

            for k, p in enumerate(downs):
                grad_rows(lambda b, n: act_t[shards - 1 - i, b, n, :], g_low, p, k, slot)
            hooks_at(i, {
                0: [p.c0 for p in downs],
                1: [downs[0].f, downs[0].xs],
                2: [downs[1].f, *(p.c1 for p in downs)],
            })
            return c

        lax.fori_loop(0, shards, down_grads, 0)

        def backward(i, c):
            slot = 1 - i % 2

            @pl.when(i >= 2)
            def _():
                wait_weights(0, slot)

            def one_block(b, cc):
                ga = nt(g_low[rows(b), :], down_v[slot])
                gu = (slope[shards - 1 - i, rows(b), :].astype(F32) * ga).astype(BF)
                gup[rows(b), :] = gu
                g_hid[rows(b), :] += nt(gu, up_v[slot])
                return cc

            lax.fori_loop(0, nb, one_block, 0)

            for back in (0, 1):

                @pl.when(i == back)
                def _():
                    start_weights(back + 2, 1 - back)

            @pl.when(i == 2)
            def _():
                for p in ups:
                    p.core(0).wait_send()

            for k, p in enumerate(ups):
                grad_rows(lambda b, n: ht[b, n, :], gup, p, k, slot_of(i))
            hooks_at(i, {
                0: [p.c0 for p in ups] + [p.s for p in downs],
                1: [p.f for p in ups] + [downs[1].xs],
                2: [p.c1 for p in ups] + [downs[0].r],
                3: [p.s for p in ups],
            })
            return c

        lax.fori_loop(0, shards, backward, 0)
        mix_out.wait()

    pl.run_scoped(
        project,
        pltpu.VMEM((nw, width, BLK), BF),
        pltpu.VMEM((all_pairs, nw * BLK, 128), BF),
        pltpu.VMEM((all_pairs, nw * BLK, 128), BF),
        pltpu.VMEM((nw, width, BLK), BF),
        pltpu.VMEM((nb, row_blocks, BLK, BLK), F32),
        pltpu.VMEM((nb, width, BLK), F32),
    )
    pl.run_scoped(
        dense,
        pltpu.VMEM((own, width), BF),
        pltpu.VMEM((width, width), BF),
        pltpu.VMEM((2, width, width), BF),
        pltpu.VMEM((2, width, width), BF),
        pltpu.VMEM((own, width), BF),
        pltpu.VMEM((nb, width, BLK), BF),
        pltpu.VMEM((shards, nb, width, BLK), BF),
        pltpu.VMEM((shards, own, width), BF),
    )

    def attention(g_v, k_v, v_v, kt_v, delta, bias, dk, dv, dqt, dkt, dvt):
        gain1 = vec_all[0, 0:1, :].astype(F32)
        for i in range(1, groups):
            gain1 = gain1 + vec_all[i, 0:1, :].astype(F32)
        def keys(hf):
            base = pl.multiple_of(hf * half, 128)
            return (
                fetch(k_i.at[pl.ds(hf * pairs, pairs)], k_v, 0),
                fetch(v_i.at[pl.ds(hf * pairs, pairs)], v_v, 1),
                fetch(kt_i.at[:, pl.ds(base, half), :], kt_v, 2),
            )

        for c in keys(far_half):
            c.start()

        def between(out_v, ctxt_v):
            low_v = ctx_v
            o_in, c_in = fetch(out_w.at[0], out_v, 6), fetch(ctxt, ctxt_v, 7)
            o_in.start()
            c_in.start()
            o_in.wait()
            c_in.wait()

            def after(b, c):
                g = g_hid[rows(b), :]
                n = xhat[rows(b), :]
                vec_acc[0:1, :] += jnp.sum(g * n, axis=0, keepdims=True)
                vec_acc[1:2, :] += jnp.sum(g, axis=0, keepdims=True)
                e = g * gain1
                res = inv[rows(b), 0:1] * (e - mean(e) - n * mean(e * n))
                g_hid[rows(b), :] = res
                low = res.astype(BF)
                low_v[rows(b), :] = low
                gc = nt(low, out_v[...]).astype(BF)
                for i in range(all_pairs):
                    g_v[i, rows(b), :] = gc[:, i * 128 : (i + 1) * 128]
                prod = nt(out_v[...], low).astype(BF).astype(F32) * ctxt_v[b]
                for i in range(2 * all_pairs):
                    delta[b, i] = jnp.sum(prod[i * HEAD_WIDTH : (i + 1) * HEAD_WIDTH, :], axis=0, keepdims=True)
                return c

            lax.fori_loop(0, nb, after, 0)
            vstep(0).start()
            ups[0].xs()

            def grad_out(i, c):
                @pl.when(i == 2)
                def _():
                    out_c.core(0).wait_send()

                base = pl.multiple_of(shard_of(i) * shard_rows, 16)
                acc = jnp.zeros((shard_rows, width), F32)
                for b in range(nb):
                    acc += nn(ctxt_v[b, pl.ds(base, shard_rows), :].astype(BF), low_v[b * BLK : (b + 1) * BLK, :])
                out_c.mine[slot_of(i)] = acc.astype(BF)
                hooks_at(i, {0: [out_c.c0], 2: [out_c.c1]})
                return c

            lax.fori_loop(0, shards, grad_out, 0)
            downs[0].yy()
            downs[1].r()
            out_c.f()

        pl.run_scoped(
            between,
            pltpu.VMEM((width, width), BF),
            pltpu.VMEM((nb, width, BLK), F32),
        )
        def unit(hf, t):
            j, i = t // pairs, t % pairs
            p = hf * pairs + i
            ws = window_start(h, j, nb, row_blocks)

            @pl.when(i == 0)
            def _():
                for kb in range(row_blocks):
                    bias[kb] = mask_of(seg[ws + kb], seg[HALO + j])

            q = q_v[p, rows(j), :]
            g = g_v[p, rows(j), :]
            lane = lax.broadcasted_iota(jnp.int32, q.shape, 1)
            qm = [jnp.where(lane // HEAD_WIDTH == hh, q, jnp.zeros_like(q)) for hh in range(2)]
            gm = [jnp.where(lane // HEAD_WIDTH == hh, g, jnp.zeros_like(g)) for hh in range(2)]
            acc = [jnp.zeros((HEAD_WIDTH, BLK), F32) for _ in range(2)]
            for kb in range(row_blocks):
                kblk = k_v[i, rows(ws + kb), :]
                vblk = v_v[i, rows(ws + kb), :]
                add_k = None
                for hh in range(2):
                    head = 2 * p + hh
                    s = nt(kblk, qm[hh]) + bias[kb]
                    prob = jnp.exp(s - lse[j, head])
                    gp = nt(vblk, gm[hh])
                    gs = (prob * (gp - delta[j, head])).astype(BF)
                    one_v = nn(prob.astype(BF), gm[hh])
                    one_k = nn(gs, qm[hh])
                    add_k, add_v = (one_k, one_v) if add_k is None else (add_k + one_k, add_v + one_v)
                    at = pl.multiple_of((2 * i + hh) * HEAD_WIDTH, HEAD_WIDTH)
                    acc[hh] += nn(kt_v[ws + kb, pl.ds(at, HEAD_WIDTH), :], gs)
                dk[i, rows(ws + kb), :] += add_k
                dv[i, rows(ws + kb), :] += add_v
            for hh in range(2):
                at = pl.multiple_of((2 * i + hh) * HEAD_WIDTH, HEAD_WIDTH)
                dqt[j, pl.ds(at, HEAD_WIDTH), :] = (acc[hh] * HEAD_WIDTH**-0.5).astype(BF)

        def attend_half(hf, plan, then):
            dk[...] = jnp.zeros_like(dk)
            dv[...] = jnp.zeros_like(dv)

            def body(t, c):
                hooks_at(t, plan)
                unit(hf, t)
                return c

            lax.fori_loop(0, nb * pairs, body, 0)
            for step in then:
                step()
            for b in range(nw):
                lo, hi = b * BLK, (b + 1) * BLK
                dkt[b] = jnp.concatenate([dk[p, lo:hi, :].astype(BF) for p in range(pairs)], axis=1).T
                dvt[b] = jnp.concatenate([dv[p, lo:hi, :].astype(BF) for p in range(pairs)], axis=1).T

        def weight_grads(which, slot, then):
            at = pl.multiple_of(which * shard_rows, 16)
            for c, src, blocks in ((q_c, dqt, range(HALO, HALO + nb)), (k_c, dkt, range(nw)), (v_c, dvt, range(nw))):
                acc = jnp.zeros((shard_rows, width), F32)
                for b in blocks:
                    acc += nn(src[b - blocks[0], pl.ds(at, shard_rows), :], x_v[b * BLK : (b + 1) * BLK, :])
                c.mine[slot] = acc.astype(BF)
                then(c)

        def input_grads(hf, last):
            base = pl.multiple_of(hf * half, 128)
            wk, wv = w_v.at[1, pl.ds(base, half), :], w_v.at[2, pl.ds(base, half), :]

            def block(b):
                kb = jnp.concatenate([dk[p, rows(b), :].astype(BF) for p in range(pairs)], axis=1)
                vb = jnp.concatenate([dv[p, rows(b), :].astype(BF) for p in range(pairs)], axis=1)
                return nn(kb, wk[...]) + nn(vb, wv[...])

            def side(i, c):
                b = i + jnp.where(i >= HALO, nb, 0)
                total = block(b)
                if last:
                    total = total + gx_side[rows(i), :].astype(F32)
                gx_side[rows(i), :] = total.astype(BF)
                return c

            lax.fori_loop(0, 2 * HALO, side, 0)

            def inner(j, c):
                g_hid[rows(j), :] += block(j + HALO) + nn(dqt[j].T, w_v[0, pl.ds(base, half), :])
                return c

            return lambda: lax.fori_loop(0, nb, inner, 0)

        for c in keys(far_half):
            c.wait()
        d0, d1 = downs
        u0, u1 = ups
        vs = [functools.partial(vnext, i) for i in range(len(vec_ids))]
        vs = [functools.partial(vnext, i) for i in range(len(vec_ids))]
        attend_half(far_half, {
            1: [vs[0], out_c.s], 3: [d0.zz, u1.xs], 4: [d1.yy], 5: [u0.r], 7: [d0.w, d1.zz],
        }, [u0.yy, out_c.xs])
        for c in keys(x_half):
            c.start()
        weight_grads(1 - core, 0, lambda p: p.c0())
        u1.r()
        d0.u()
        d1.w()
        weight_grads(core, 1, lambda p: (p.f(), p.xs()))
        vs[1]()
        input_grads(far_half, False)()
        u0.zz()
        for c in keys(x_half):
            c.wait()
        attend_half(x_half, {
            0: [out_c.r], 1: [d1.u], 2: [u1.yy], 3: [vs[2]], 4: [u0.w, out_c.yy], 5: [u1.zz], 6: [vs[3], d0.end],
            7: [u0.u, d1.end], 8: [out_c.zz],
        }, [])
        u1.w()
        for p in (q_c, k_c, v_c):
            p.core(0).wait_send()
        weight_grads(1 - core, 0, lambda p: p.c1())
        out_c.w()
        weight_grads(core, 2, lambda p: None)
        for p in (q_c, k_c, v_c):
            p.s()
            p.r()
        u1.u()
        for step in vs[4:]:
            step()
        finish = input_grads(x_half, True)

        @pl.when(h > 0)
        def _():
            to_left.start()

        @pl.when(h < groups - 1)
        def _():
            to_right.start()

        out_c.u()
        for p in (q_c, k_c, v_c):
            p.yy()
        u0.end()
        for p in (q_c, k_c, v_c):
            p.zz()
        finish()
        tok_out = fetch(g_hid, o_tok, 3)
        tok_out.start()
        u1.end()
        out_c.end()
        for p in (q_c, k_c, v_c):
            p.w()
        for p in (q_c, k_c, v_c):
            p.u()
        for p in (q_c, k_c, v_c):
            p.end()
        tok_out.wait()

    to_left = remote(gx_side.at[pl.ds(0, halo), :], o_right, side_send.at[0], side_recv.at[0], (r, h - 1))
    to_right = remote(gx_side.at[pl.ds(halo, halo), :], o_left, side_send.at[1], side_recv.at[1], (r, h + 1))

    pl.run_scoped(
        attention,
        pltpu.VMEM((all_pairs, own, 128), BF),
        pltpu.VMEM((pairs, nw * BLK, 128), BF),
        pltpu.VMEM((pairs, nw * BLK, 128), BF),
        pltpu.VMEM((nw, half, BLK), BF),
        pltpu.VMEM((nb, 2 * all_pairs, 1, BLK), F32),
        pltpu.VMEM((row_blocks, BLK, BLK), F32),
        pltpu.VMEM((pairs, nw * BLK, 128), F32),
        pltpu.VMEM((pairs, nw * BLK, 128), F32),
        pltpu.VMEM((nb, half, BLK), BF),
        pltpu.VMEM((nw, half, BLK), BF),
        pltpu.VMEM((nw, half, BLK), BF),
    )

    o_vec[...] = vacc[len(vec_ids) - 1]
    for g in (gq, go, gu, gd):
        g.sent()
    for p in parts:
        p.done()
    for i in range(len(vec_ids)):
        vstep(i).wait_send()

    @pl.when(h > 0)
    def _():
        to_left.wait_send()
        to_right.wait_recv()

    @pl.when(h == 0)
    def _():
        gx_side[pl.ds(0, halo), :] = jnp.zeros((halo, width), BF)
        pltpu.sync_copy(gx_side.at[pl.ds(0, halo), :], o_left)

    @pl.when(h < groups - 1)
    def _():
        to_right.wait_send()
        to_left.wait_recv()

    @pl.when(h == groups - 1)
    def _():
        gx_side[pl.ds(halo, halo), :] = jnp.zeros((halo, width), BF)
        pltpu.sync_copy(gx_side.at[pl.ds(halo, halo), :], o_right)


def layer(groups, row_blocks, row_devices, tok, cot, qkv_own, out_own, up_own, down_own, vec_own, lengths):
    own, width = tok.shape
    shard_rows = width // groups
    nb = own // BLK
    nw = nb + 2 * HALO
    all_pairs = width // 128
    bits = other_bits(row_devices)
    split = width // 2
    chunks = [(name, lo, split) for name in ("down", "up") for lo in range(0, width, split)]
    chunks += [(name, 0, shard_rows) for name in ("out", "q", "k", "v")]
    hops = 4 + len(bits)
    scratch = [
        pltpu.VMEM((3, width, width), BF),
        pltpu.VMEM((nw * BLK, width), BF),
        pltpu.VMEM((all_pairs, own, 128), BF),
        pltpu.VMEM((own, width), BF),
        pltpu.VMEM((nb, 2 * all_pairs, 1, BLK), F32),
        pltpu.VMEM((nw, 1, BLK), F32),
        pltpu.VMEM((groups,) + vec_own.shape, BF),
        pltpu.VMEM((own, width), F32),
        pltpu.VMEM((own, 128), F32),
        pltpu.VMEM((own, width), F32),
        pltpu.VMEM((2 * HALO * BLK, width), BF),
        pltpu.VMEM((8, width), F32),
        pltpu.VMEM((hops, 8, width), F32),
        pltpu.VMEM((hops, 8, width), F32),
    ]
    for _, _, n in chunks:
        scratch += [
            pltpu.VMEM((3, n, width), BF),
            pltpu.VMEM((2, n, width), BF),
            pltpu.VMEM((n, width), BF),
            pltpu.VMEM((n // 2, width), BF),
            pltpu.VMEM((n // 4, width), BF),
            pltpu.VMEM((max(1, len(bits)), n // 4, width), BF),
        ]
    dma = pltpu.SemaphoreType.DMA
    scratch += [dma((len(chunks), 8 + len(bits)))] * 2 + [dma((len(chunks), 3))] + [dma((4, 12))] * 2
    scratch += [dma((2 * HALO,))] * 2 + [dma((2,))] * 2 + [dma((groups - 1,))] * 2 + [dma((hops,))] * 2 + [dma((8,))]
    s = jax.ShapeDtypeStruct
    side = s((HALO * BLK, width), BF)
    outs = [
        (s((own, width), BF), ANY),
        (s((width, width), BF), ANY),
        (s((width, width), BF), ANY),
        (s((shard_rows, width), BF), ANY),
        (s((3, shard_rows, width), BF), ANY),
        (s((own, width), F32), ANY),
        (side, ANY),
        (side, ANY),
        (s((8, width), F32), VM),
        (s((1, width, width), BF), ANY),
        (s((1, groups * width, width), BF), ANY),
        (s((1, groups * width, width), BF), ANY),
        (s((nb, width, BLK), F32), ANY),
        (s((all_pairs, nw * BLK, 128), BF), ANY),
        (s((all_pairs, nw * BLK, 128), BF), ANY),
        (s((nw, width, BLK), BF), ANY),
    ]
    return pl.pallas_call(
        functools.partial(layer_kernel, groups, row_blocks, bits, chunks),
        out_shape=[o[0] for o in outs],
        in_specs=[ANY] * 6 + [VM] * 2,
        out_specs=[o[1] for o in outs],
        scratch_shapes=scratch,
        compiler_params=pltpu.CompilerParams(collective_id=0, has_side_effects=True, vmem_limit_bytes=VMEM_LIMIT),
        name="layer",
    )(tok, cot, qkv_own, out_own, up_own, down_own, vec_own, lengths)


def local(
    groups, row_devices,
    tokens, lengths, w_query, w_key, w_value, w_out, w_up, w_down,
    gain_first, shift_first, gain_second, shift_second, cotangent,
):
    packed_rows = lengths.shape[0]
    own, width = tokens.shape
    row_length = groups * own // packed_rows
    row_blocks = row_length // BLK
    h = lax.axis_index("heads")
    n_vec = gain_first.shape[0]
    vec_own = jnp.stack([gain_first, shift_first, gain_second, shift_second])
    vec_own = lax.dynamic_update_slice(jnp.zeros((16, width), BF), vec_own, (0, n_vec * h))
    qkv_own = jnp.stack([w_query.T, w_key.T, w_value.T])
    mixed, o_down, o_up, o_out, o_qkv, gx, gx_left, gx_right, o_vec = layer(
        groups, row_blocks, row_devices, tokens, cotangent, qkv_own, w_out[None], w_up[None], w_down[None], vec_own, lengths
    )[:9]
    halo = HALO * BLK
    o_tok = gx + jnp.pad(gx_left.astype(F32), ((0, own - halo), (0, 0))) + jnp.pad(gx_right.astype(F32), ((own - halo, 0), (0, 0)))
    mine = lax.dynamic_slice(o_vec, (0, n_vec * h), (4, n_vec))
    wide = lambda a: a.astype(F32)
    return (
        mixed, o_tok, wide(o_qkv[0].T), wide(o_qkv[1].T), wide(o_qkv[2].T), wide(o_out), wide(o_up), wide(o_down),
        mine[0], mine[1], mine[2], mine[3],
    )


def solution(mesh):
    both, heads = P(("rows", "heads"), None), P("heads")
    cols, rows = P(None, "heads"), P("heads", None)
    return jax.shard_map(
        functools.partial(local, mesh.shape["heads"], mesh.shape["rows"]),
        mesh=mesh,
        in_specs=(both, P("rows", None), cols, cols, cols, rows, cols, rows, heads, heads, heads, heads, both),
        out_specs=(both, both, cols, cols, cols, rows, cols, rows, heads, heads, heads, heads),
        check_vma=False,
    )
```

```python
import functools

import jax
import jax.numpy as jnp
from jax import lax
from jax.experimental import pallas as pl
from jax.experimental.pallas import tpu as pltpu
from jax.sharding import PartitionSpec as P

MESH = pl.DeviceIdType.MESH
BF = jnp.bfloat16
F32 = jnp.float32
HEAD_WIDTH = 64
LONGEST_DOC = 512
BLK = 256
HALO = LONGEST_DOC // BLK
NORM_EPS = 1e-12
VMEM_LIMIT = 62 * 1024 * 1024


def nt(left, right):
    return lax.dot_general(left, right, (((1,), (1,)), ((), ())), preferred_element_type=F32)


def nn(left, right):
    return lax.dot_general(left, right, (((1,), (0,)), ((), ())), preferred_element_type=F32)


def flip(index, bit):
    return index + bit - 2 * bit * ((index // bit) % 2)


def place():
    r, h = lax.axis_index("rows"), lax.axis_index("heads")
    return r, h


def greet(ids):
    barrier = pltpu.get_barrier_semaphore()
    for who in ids:
        pl.semaphore_signal(barrier, inc=1, device_id=who, device_id_type=MESH)
    pl.semaphore_wait(barrier, len(ids))


def group_of(r, h, groups):
    return [(r, lax.rem(h + i, groups)) for i in range(1, groups)]


def remote(src, dst, send, recv, who):
    return pltpu.make_async_remote_copy(
        src_ref=src, dst_ref=dst, send_sem=send, recv_sem=recv, device_id=who, device_id_type=MESH
    )


class Gather:
    def __init__(self, own, full, sems, at):
        self.own, self.full, self.sems, self.at = own, full, sems, at
        self.n = own.shape[1]
        self.u = self.n // 12
        r, h = place()
        self.r, self.h = r, h
        y, z = r % 2, (r // 2) % 2
        self.k = 2 * z + y
        self.ky = 2 * z + 1 - y
        self.kz = 2 * (1 - z) + y
        self.kd = 3 - self.k
        self.hx = flip(h, 2)
        self.hc = flip(h, 1)
        self.by_x = (r, self.hx)
        self.by_c = (r, self.hc)
        self.by_y = (flip(r, 1), h)
        self.by_z = (flip(r, 2), h)

    def rows(self, shard, sub, count):
        u = self.u
        return pl.ds(pl.multiple_of(shard * self.n + sub * u, 16), count * u)

    def part(self, slot, who, shard, sub, count, own=False):
        dst = self.full.at[:, self.rows(shard, sub, count), :]
        src = self.own.at[:, self.rows(0, sub, count), :] if own else dst
        send, recv = self.sems
        return remote(src, dst, send.at[self.at, slot], recv.at[self.at, slot], who)

    def x_main(self):
        return self.part(0, self.by_x, self.h, 3 * self.k, 3, own=True)

    def x_diag(self):
        return self.part(1, self.by_x, self.h, 3 * self.kd, 1, own=True)

    def y_main(self):
        return self.part(2, self.by_y, self.hx, 3 * self.k, 3)

    def z_main(self):
        return self.part(3, self.by_z, self.hx, 3 * self.k, 3)

    def y_diag(self):
        return self.part(4, self.by_y, self.hx, 3 * self.kz + 1, 1)

    def z_diag(self):
        return self.part(5, self.by_z, self.hx, 3 * self.ky + 2, 1)

    def c_own(self):
        return self.part(6, self.by_c, self.h, 0, 12, own=True)

    def c_part(self, i):
        return self.part(7 + i, self.by_c, self.hx, 3 * (self.k, self.ky, self.kz, self.kd)[i], 3)

    def local(self):
        send, _ = self.sems
        return pltpu.make_async_copy(
            self.own, self.full.at[:, self.rows(self.h, 0, 12), :], send.at[self.at, 11]
        )

    def start_x(self):
        self.x_main().start()
        self.x_diag().start()

    def start_main(self):
        self.x_main().start()

    def start_diag(self):
        self.x_diag().start()

    def start_c(self, keep):
        self.c_own().start()
        if keep:
            self.local().start()

    def step_x(self):
        self.x_main().wait_recv()
        self.y_main().start()
        self.z_main().start()
        self.c_part(0).start()

    def step_yz(self):
        self.y_main().wait_recv()
        self.z_diag().start()
        self.c_part(1).start()
        self.z_main().wait_recv()
        self.y_diag().start()
        self.c_part(2).start()

    def step_diag(self):
        self.x_diag().wait_recv()
        self.y_diag().wait_recv()
        self.z_diag().wait_recv()
        self.c_part(3).start()

    def near(self, keep):
        self.c_own().wait_recv()
        if keep:
            self.local().wait()

    def far(self):
        for i in range(4):
            self.c_part(i).wait_recv()

    def sent(self):
        for copy in (self.x_main(), self.x_diag(), self.y_main(), self.z_main(), self.y_diag(), self.z_diag(), self.c_own()):
            copy.wait_send()
        for i in range(4):
            self.c_part(i).wait_send()


def window_start(h, j, own_blocks, row_blocks):
    g = own_blocks * h + j
    first = own_blocks * h - HALO
    row = row_blocks * (g // row_blocks)
    return jnp.clip(row, first, first + own_blocks + 2 * HALO - row_blocks) - first


def mask_of(keys, queries):
    down = jnp.broadcast_to(keys, (8, BLK)).T[:, 0:1]
    return jnp.where(down == queries, 0.0, -1e30).astype(F32)


ANY = pl.BlockSpec(memory_space=pl.ANY)
VM = pl.BlockSpec(memory_space=pltpu.VMEM)


def gelu_parts(u):
    bell = jnp.exp(-0.5 * u * u)
    base = 1.0 + (0.3275911 * 0.7071067811865476) * jnp.abs(u)
    t = pl.reciprocal(base, approx=True)
    t = t * (2.0 - base * t)
    poly = t * (0.127414796 + t * (-0.142248368 + t * (0.7107068705 + t * (-0.7265760135 + t * 0.5307027145))))
    tail = poly * bell
    cdf = jnp.where(u >= 0.0, 1.0 - tail, tail)
    return u * cdf, cdf + u * (bell * 0.3989422804014327)


class Sum:
    def __init__(self, n, bits, bufs, sems, at):
        self.n, self.bits, self.at = n, bits, at
        self.mine, self.rc, self.rx, self.ry, self.rz, self.rest = bufs
        self.send, self.recv, self.keep = sems
        r, h = place()
        self.y, self.z = r % 2, (r // 2) % 2
        self.by_x, self.by_c = (r, flip(h, 2)), (r, flip(h, 1))
        self.by_y, self.by_z = (flip(r, 1), h), (flip(r, 2), h)
        self.by_rest = [(flip(r, b), h) for b in bits]

    def copy(self, slot, src, dst, who):
        return remote(src, dst, self.send.at[self.at, slot], self.recv.at[self.at, slot], who)

    def core(self, i):
        return self.copy(i, self.mine.at[0], self.rc.at[i], self.by_c)

    def x(self):
        return self.copy(2, self.mine.at[1], self.rx, self.by_x)

    def half(self, which):
        return pl.ds(pl.multiple_of(which * (self.n // 2), 16), self.n // 2)

    def quarter(self, half, which):
        return pl.ds(pl.multiple_of(half * (self.n // 2) + which * (self.n // 4), 16), self.n // 4)

    def own(self):
        return self.mine.at[2, self.quarter(self.y, self.z), :]

    def landed(self, half, which):
        return self.rx.at[self.quarter(half, which), :]

    def y_down(self):
        return self.copy(3, self.mine.at[2, self.half(1 - self.y), :], self.ry, self.by_y)

    def z_down(self):
        return self.copy(4, self.mine.at[2, self.quarter(self.y, 1 - self.z), :], self.rz, self.by_z)

    def z_up(self):
        return self.copy(5, self.own(), self.landed(self.y, self.z), self.by_z)

    def y_up(self):
        return self.copy(6, self.own(), self.landed(self.y, self.z), self.by_y)

    def y_up2(self):
        return self.copy(7, self.landed(self.y, 1 - self.z), self.landed(self.y, 1 - self.z), self.by_y)

    def swap(self, i):
        return self.copy(8 + i, self.own(), self.rest.at[i], self.by_rest[i])

    def add(self, ref, got):
        ref[...] = (ref[...].astype(F32) + got[...].astype(F32)).astype(BF)

    def c0(self):
        self.core(0).start()

    def f(self):
        self.core(0).wait_recv()
        self.add(self.mine.at[1], self.rc.at[0])

    def xs(self):
        self.x().start()

    def c1(self):
        self.core(1).start()

    def s(self):
        self.core(1).wait_recv()
        self.add(self.mine.at[2], self.rc.at[1])

    def r(self):
        self.x().wait_recv()
        self.add(self.mine.at[2], self.rx)
        self.y_down().start()

    def yy(self):
        self.y_down().wait_recv()
        self.add(self.mine.at[2, self.half(self.y), :], self.ry)
        self.z_down().start()

    def zz(self):
        self.z_down().wait_recv()
        self.add(self.own(), self.rz)
        if self.bits:
            self.swap(0).start()

    def w(self):
        for i in range(len(self.bits)):
            self.swap(i).wait_recv()
            self.swap(i).wait_send()
            self.add(self.own(), self.rest.at[i])
            if i + 1 < len(self.bits):
                self.swap(i + 1).start()
        self.z_up().start()
        self.y_up().start()

    def u(self):
        self.z_up().wait_recv()
        self.y_up2().start()

    def outs(self, out, lo):
        def local(i, src, rows):
            start = pl.multiple_of(lo + rows.start, 16)
            return pltpu.make_async_copy(src, out.at[pl.ds(start, rows.size), :], self.keep.at[self.at, i])

        mine, beside, other = self.quarter(self.y, self.z), self.quarter(self.y, 1 - self.z), self.half(1 - self.y)
        return (
            local(0, self.own(), mine),
            local(1, self.rx.at[beside, :], beside),
            local(2, self.rx.at[other, :], other),
        )

    def e(self, out, lo):
        self.y_up().wait_recv()
        self.y_up2().wait_recv()
        for c in self.outs(out, lo):
            c.start()

    def sent(self, out, lo):
        for c in (self.core(1), self.x(), self.y_down(), self.z_down(), self.z_up(), self.y_up(), self.y_up2()):
            c.wait_send()
        for c in self.outs(out, lo):
            c.wait()


def other_bits(count):
    bits, b = [], 4
    while b < count:
        bits.append(b)
        b *= 2
    return tuple(bits)


def hooks_at(t, plan):
    for at, steps in plan.items():

        @pl.when(t == at)
        def _():
            for step in steps:
                step()


def layer_kernel(
    groups, row_blocks, bits, chunks,
    tok, cot, qkv_own, out_own, up_own, down_own, vec_own, lengths,
    mixed, o_down, o_up, o_out, o_qkv, o_tok, o_left, o_right, o_vec,
    out_w, up_w, down_w, ctxt, k_i, v_i, kt_i,
    w_v, x_v, q_v, ctx_v, lse, seg, vec_all, xhat, inv, g_hid, gx_side, vec_acc, vin, vacc, *scratch,
):
    r, h = place()
    own, width = tok.shape
    nb = own // BLK
    nw = nb + 2 * HALO
    halo = HALO * BLK
    shards = groups
    all_pairs = q_v.shape[0]
    pairs = all_pairs // 2
    half = pairs * 128
    shard_rows = half // 2
    x_half = (h // 2) % 2
    far_half = 1 - x_half
    core = h % 2
    rows = lambda b: pl.ds(pl.multiple_of(b * BLK, BLK), BLK)
    mean = lambda v: jnp.mean(v, axis=1, keepdims=True)
    n_chunks = len(chunks)
    (send, recv, keep, gsend, grecv, in_send, in_recv, side_send, side_recv, psend, precv, vsend, vrecv, loc) = scratch[6 * n_chunks :]
    sems = (send, recv, keep)
    outs = {"down": o_down, "up": o_up, "out": o_out, "q": o_qkv.at[0], "k": o_qkv.at[1], "v": o_qkv.at[2]}
    parts = [Sum(n, bits, scratch[6 * i : 6 * i + 6], sems, i) for i, (_, _, n) in enumerate(chunks)]
    by_name = {}
    for part, (name, lo, _) in zip(parts, chunks):
        part.end = functools.partial(part.e, outs[name], lo)
        part.done = functools.partial(part.sent, outs[name], lo)
        by_name.setdefault(name, []).append(part)
    downs, ups, (out_c,) = by_name["down"], by_name["up"], by_name["out"]
    q_c, k_c, v_c = (by_name[name][0] for name in "qkv")
    one = parts[0]
    gq = Gather(qkv_own, w_v, (gsend, grecv), 0)
    go = Gather(out_own, out_w, (gsend, grecv), 1)
    gu = Gather(up_own, up_w, (gsend, grecv), 2)
    gd = Gather(down_own, down_w, (gsend, grecv), 3)

    def shard_of(i):
        across = 1 - i // 2
        other = 1 - i % 2
        return h + across * (2 - 4 * x_half) + other * (1 - 2 * core)

    def slot_of(i):
        return (i % 2) * (1 + i // 2)

    def fetch(src, dst, i):
        return pltpu.make_async_copy(src, dst, loc.at[i])

    vec_ids = [one.by_c, one.by_x, one.by_y, one.by_z] + one.by_rest

    def vstep(i):
        src = vec_acc if i == 0 else vacc.at[i - 1]
        return remote(src, vin.at[i], vsend.at[i], vrecv.at[i], vec_ids[i])

    def vnext(i):
        vstep(i).wait_recv()
        vacc[i] = (vec_acc[...] if i == 0 else vacc[i - 1]) + vin[i]
        if i + 1 < len(vec_ids):
            vstep(i + 1).start()

    def parameter(i):
        n = width // groups
        return jnp.concatenate([vec_all[s].astype(F32)[0:1, i * n : (i + 1) * n] for s in range(groups)], axis=1)

    def project(vt, k_s, v_s, kt_s, bias, ctx_t):
        total_blocks = groups * nb
        def to_right(i):
            src, dst = pl.ds(own - halo + i * BLK, BLK), pl.ds(i * BLK, BLK)
            return remote(tok.at[src, :], x_v.at[dst, :], in_send.at[i], in_recv.at[i], (r, h + 1))

        def to_left(i):
            src, dst = pl.ds(i * BLK, BLK), pl.ds(halo + own + i * BLK, BLK)
            return remote(tok.at[src, :], x_v.at[dst, :], in_send.at[HALO + i], in_recv.at[HALO + i], (r, h - 1))

        def both(to, step):
            for i in range(HALO):
                step(to(i))

        start, arrived, gone = (lambda c: c.start()), (lambda c: c.wait_recv()), (lambda c: c.wait_send())
        even = h % 2 == 0
        slow_right = jnp.logical_and(h % 2 == 1, h < groups - 1)
        slow_left = jnp.logical_and(even, h > 0)

        odd = h % 2 == 1

        def par(i):
            who = (r, lax.rem(h + 1 + i, groups))
            return remote(vec_own, vec_all.at[h], psend.at[i], precv.at[groups - 2 - i], who)

        def par_from(i):
            return remote(vec_own, vec_all.at[h], psend.at[i], precv.at[i], (r, lax.rem(h + 1 + i, groups)))

        mine = fetch(tok, x_v.at[pl.ds(halo, own), :], 0)
        mine.start()
        greet(group_of(r, h, groups) + [one.by_y, one.by_z] + one.by_rest)

        @pl.when(slow_right)
        def _():
            to_right(HALO - 1).start()

        @pl.when(slow_left)
        def _():
            to_left(0).start()

        @pl.when(even)
        def _():
            both(to_right, start)

        @pl.when(odd)
        def _():
            both(to_left, start)

        gq.start_c(True)
        gq.start_main()
        for i in range(groups - 1):
            par(i).start()
        vec_all[h] = vec_own[...]

        @pl.when(h == 0)
        def _():
            x_v[pl.ds(0, halo), :] = jnp.zeros((halo, width), BF)

        @pl.when(h == groups - 1)
        def _():
            x_v[pl.ds(halo + own, halo), :] = jnp.zeros((halo, width), BF)

        packed, docs = lengths.shape
        down = lax.broadcasted_iota(jnp.int32, (docs, docs), 0)
        across = lax.broadcasted_iota(jnp.int32, (docs, docs), 1)
        for b in range(nw):
            g = nb * h - HALO + b
            row = jnp.clip(g // row_blocks, 0, packed - 1)
            sizes = lengths[pl.ds(row, 1), :].astype(F32)
            ends = jnp.sum(jnp.where(across <= down, jnp.broadcast_to(sizes, (docs, docs)), 0.0), axis=1, keepdims=True)
            at = (lax.broadcasted_iota(jnp.int32, (docs, BLK), 1) + (g % row_blocks) * BLK).astype(F32)
            ids = jnp.sum(jnp.where(at >= ends, 1.0, 0.0), axis=0, keepdims=True) + (row * docs).astype(F32)
            inside = jnp.logical_and(g >= 0, g < total_blocks)
            seg[b] = jnp.where(inside, ids, -1.0)
        for j in range(nb):
            ws = window_start(h, j, nb, row_blocks)
            for kb in range(row_blocks):
                bias[j, kb] = mask_of(seg[ws + kb], seg[HALO + j])

        def project_keys(hx, b):
            base = pl.multiple_of(hx * half, 128)
            xb = x_v[rows(b), :]
            wk = w_v[1, pl.ds(base, half), :]
            wv = w_v[2, pl.ds(base, half), :]
            key = nt(xb, wk).astype(BF)
            value = nt(xb, wv).astype(BF)
            for i in range(pairs):
                k_s[hx * pairs + i, rows(b), :] = key[:, i * 128 : (i + 1) * 128]
                v_s[hx * pairs + i, rows(b), :] = value[:, i * 128 : (i + 1) * 128]
            kt_s[b, pl.ds(base, half), :] = nt(wk, xb).astype(BF)
            vt[b, pl.ds(base, half), :] = nt(wv, xb).astype(BF)

        def project_query(hx, b):
            base = pl.multiple_of(hx * half, 128)
            xb = x_v[rows(b + HALO), :]
            query = nt(xb, w_v[0, pl.ds(base, half), :]).astype(BF) * BF(HEAD_WIDTH**-0.5)
            for i in range(pairs):
                q_v[hx * pairs + i, rows(b), :] = query[:, i * 128 : (i + 1) * 128]

        def side_keys(hx, first):
            def body(b, c):
                project_keys(hx, first + b)
                return c

            lax.fori_loop(0, HALO, body, 0)

        def attend(hx, t):
            j = jnp.where(odd, t // pairs, nb - 1 - t // pairs)
            p = hx * pairs + t % pairs
            ws = window_start(h, j, nb, row_blocks)
            q = q_v[p, rows(j), :]
            lane = lax.broadcasted_iota(jnp.int32, q.shape, 1)
            q_both = jnp.concatenate([jnp.where(lane // HEAD_WIDTH == hh, q, jnp.zeros_like(q)) for hh in range(2)], axis=0)
            scores, tops = [[], []], [None, None]
            for kb in range(row_blocks):
                both_s = nt(k_s[p, rows(ws + kb), :], q_both)
                for hh in range(2):
                    s = both_s[:, hh * BLK : (hh + 1) * BLK] + bias[j, kb]
                    m = jnp.max(s.reshape(BLK // 8, 8, BLK), axis=0)
                    tops[hh] = m if kb == 0 else jnp.maximum(tops[hh], m)
                    scores[hh].append(s)
            tops = [jnp.max(m, axis=0, keepdims=True) for m in tops]
            totals = [jnp.zeros((8, BLK), F32) for _ in range(2)]
            accs = [jnp.zeros((HEAD_WIDTH, BLK), F32) for _ in range(2)]
            at = [pl.ds(pl.multiple_of((2 * p + hh) * HEAD_WIDTH, HEAD_WIDTH), HEAD_WIDTH) for hh in range(2)]
            for kb in range(row_blocks):
                for hh in range(2):
                    e = jnp.exp(scores[hh][kb] - tops[hh])
                    totals[hh] = totals[hh] + jnp.sum(e.reshape(BLK // 8, 8, BLK), axis=0)
                    accs[hh] = accs[hh] + nn(vt[ws + kb, at[hh], :], e.astype(BF))
            for hh in range(2):
                total = jnp.sum(totals[hh], axis=0, keepdims=True)
                ctx_t[j, at[hh], :] = accs[hh] / total
                lse[j, 2 * p + hh] = tops[hh] + jnp.log(total)

        def attend_all(hx, plan):
            def body(t, c):
                hooks_at(t, plan)
                attend(hx, t)
                return c

            lax.fori_loop(0, nb * pairs, body, 0)

        def slow_block(near):
            @pl.when(slow_right)
            def _():
                to_left(0 if near else 1).wait_recv()

            @pl.when(slow_left)
            def _():
                to_right(1 if near else 0).wait_recv()

            project_keys(x_half, jnp.where(odd, HALO + nb + (0 if near else 1), 1 if near else 0))

        def more_halo():
            @pl.when(slow_right)
            def _():
                to_right(0).start()

            @pl.when(slow_left)
            def _():
                to_left(1).start()

        mine.wait()
        gq.near(True)
        for b in range(nb):
            project_query(x_half, b)
        lax.fori_loop(HALO, HALO + nb, lambda b, c: (project_keys(x_half, b), c)[1], 0)

        @pl.when(odd)
        def _():
            both(to_right, arrived)

        @pl.when(even)
        def _():
            both(to_left, arrived)

        side_keys(x_half, jnp.where(odd, 0, HALO + nb))
        last = jnp.where(odd, nw - 1, 0)
        for i in range(all_pairs):
            k_s[i, rows(last), :] = jnp.zeros((BLK, 128), BF)
        vt[last] = jnp.zeros((width, BLK), BF)
        attend_all(x_half, {
            0: [lambda: go.start_c(True), lambda: gu.start_c(False)],
            3: [functools.partial(slow_block, True), gq.step_x, gq.start_diag, more_halo, lambda: gd.start_c(False)],
            6: [functools.partial(slow_block, False), go.start_x, gu.start_x], 8: [gq.step_yz],
        })
        go.step_x()
        gq.step_diag()
        gq.far()
        for b in range(nb):
            project_query(far_half, b)
        lax.fori_loop(0, nw, lambda b, c: (project_keys(far_half, b), c)[1], 0)
        keys_out = [fetch(a, b, i) for i, (a, b) in enumerate(((k_s, k_i), (v_s, v_i), (kt_s, kt_i)))]
        for c in keys_out:
            c.start()
        attend_all(far_half, {
            0: [gd.start_x], 1: [gu.step_x], 3: [go.step_yz], 7: [go.step_diag], 8: [gu.step_yz],
        })
        ctx_out = fetch(ctx_t, ctxt, 3)
        ctx_out.start()
        for j in range(nb):
            ctx_v[j * BLK : (j + 1) * BLK, :] = ctx_t[j].T.astype(BF)
        gd.step_x()
        go.near(True)
        go.far()
        for c in keys_out:
            c.wait()
        ctx_out.wait()
        for i in range(groups - 1):
            par(i).wait_send()
            par_from(i).wait_recv()

        @pl.when(h < groups - 1)
        def _():
            both(to_right, gone)

        @pl.when(h > 0)
        def _():
            both(to_left, gone)

    def dense(cot_v, out_v, up_v, down_v, hl, ht, act_t, slope):
        ffn, gup, mix_v, g_low = g_hid, hl, ctx_v, cot_v
        gain1, shift1, gain2, shift2 = (parameter(i) for i in range(4))
        first = [fetch(a, b, i) for i, (a, b) in enumerate(((out_w.at[0], out_v), (cot, cot_v)))]
        for c in first:
            c.start()

        def weights(i, slot):
            if i == shards - 1:
                return fetch(up_own.at[0], up_v.at[slot], 4 + slot), fetch(down_own.at[0], down_v.at[slot], 6 + slot)
            here = pl.ds(pl.multiple_of(shard_of(i) * width, 16), width)
            return fetch(up_w.at[0, here, :], up_v.at[slot], 4 + slot), fetch(down_w.at[0, here, :], down_v.at[slot], 6 + slot)

        def start_weights(i, slot):
            for c in weights(i, slot):
                c.start()

        def wait_weights(i, slot):
            for c in weights(i, slot):
                c.wait()

        start_weights(3, 0)
        gu.near(False)
        gd.near(False)
        start_weights(2, 1)
        vec_acc[...] = jnp.zeros_like(vec_acc)
        for c in first:
            c.wait()

        def before(b, c):
            resid = x_v[rows(b + HALO), :].astype(F32) + nn(ctx_v[rows(b), :], out_v[...])
            cen = resid - mean(resid)
            rs = lax.rsqrt(mean(cen * cen) + NORM_EPS)
            n = cen * rs
            hidden = n * gain1 + shift1
            xhat[rows(b), :] = n
            inv[rows(b), :] = jnp.broadcast_to(rs, (BLK, 128))
            low = hidden.astype(BF)
            hl[rows(b), :] = low
            ht[b] = low.T
            ffn[rows(b), :] = hidden
            return c

        lax.fori_loop(0, nb, before, 0)
        gu.step_diag()
        gd.step_yz()

        def forward(i, c):
            slot = i % 2
            wait_weights(0, slot)
            for b in range(nb):
                up = nn(hl[rows(b), :], up_v[slot])
                active, deriv = gelu_parts(up)
                active = active.astype(BF)
                slope[i, rows(b), :] = deriv.astype(BF)
                act_t[i, b] = active.T
                ffn[rows(b), :] += nn(active, down_v[slot])
            return c

        def two(first, then):
            def body(i, c):
                forward(i, c)
                hooks_at(i, then)
                return c

            lax.fori_loop(first, first + 2, body, 0)

        two(0, {0: [gd.step_diag]})
        gu.far()
        gd.far()
        start_weights(1, 0)
        start_weights(0, 1)
        two(2, {})

        def middle(b, c):
            v = ffn[rows(b), :]
            cen = v - mean(v)
            rs = lax.rsqrt(mean(cen * cen) + NORM_EPS)
            n = cen * rs
            mix_v[rows(b), :] = (n * gain2 + shift2).astype(BF)
            ct = cot_v[rows(b), :].astype(F32)
            vec_acc[2:3, :] += jnp.sum(ct * n, axis=0, keepdims=True)
            vec_acc[3:4, :] += jnp.sum(ct, axis=0, keepdims=True)
            e = ct * gain2
            g = rs * (e - mean(e) - n * mean(e * n))
            g_hid[rows(b), :] = g
            g_low[rows(b), :] = g.astype(BF)
            return c

        lax.fori_loop(0, nb, middle, 0)
        mix_out = fetch(mix_v, mixed, 0)
        mix_out.start()

        def grad_rows(left, right, part, part_i, slot):
            n = part.n
            acc = jnp.zeros((n, width), F32)
            for b in range(nb):
                acc += nn(left(b, pl.ds(part_i * n, n)), right[b * BLK : (b + 1) * BLK, :])
            part.mine[slot] = acc.astype(BF)

        def down_grads(i, c):
            slot = slot_of(i)

            @pl.when(i == 2)
            def _():
                for p in downs:
                    p.core(0).wait_send()

            for k, p in enumerate(downs):
                grad_rows(lambda b, n: act_t[shards - 1 - i, b, n, :], g_low, p, k, slot)
            hooks_at(i, {
                0: [p.c0 for p in downs],
                1: [downs[0].f, downs[0].xs],
                2: [downs[1].f, *(p.c1 for p in downs)],
            })
            return c

        lax.fori_loop(0, shards, down_grads, 0)

        def backward(i, c):
            slot = 1 - i % 2

            @pl.when(i >= 2)
            def _():
                wait_weights(0, slot)

            def one_block(b, cc):
                ga = nt(g_low[rows(b), :], down_v[slot])
                gu = (slope[shards - 1 - i, rows(b), :].astype(F32) * ga).astype(BF)
                gup[rows(b), :] = gu
                g_hid[rows(b), :] += nt(gu, up_v[slot])
                return cc

            lax.fori_loop(0, nb, one_block, 0)

            for back in (0, 1):

                @pl.when(i == back)
                def _():
                    start_weights(back + 2, 1 - back)

            @pl.when(i == 2)
            def _():
                for p in ups:
                    p.core(0).wait_send()

            for k, p in enumerate(ups):
                grad_rows(lambda b, n: ht[b, n, :], gup, p, k, slot_of(i))
            hooks_at(i, {
                0: [p.c0 for p in ups] + [p.s for p in downs],
                1: [p.f for p in ups] + [downs[1].xs],
                2: [p.c1 for p in ups] + [downs[0].r],
                3: [p.s for p in ups],
            })
            return c

        lax.fori_loop(0, shards, backward, 0)
        mix_out.wait()

    pl.run_scoped(
        project,
        pltpu.VMEM((nw, width, BLK), BF),
        pltpu.VMEM((all_pairs, nw * BLK, 128), BF),
        pltpu.VMEM((all_pairs, nw * BLK, 128), BF),
        pltpu.VMEM((nw, width, BLK), BF),
        pltpu.VMEM((nb, row_blocks, BLK, BLK), F32),
        pltpu.VMEM((nb, width, BLK), F32),
    )
    pl.run_scoped(
        dense,
        pltpu.VMEM((own, width), BF),
        pltpu.VMEM((width, width), BF),
        pltpu.VMEM((2, width, width), BF),
        pltpu.VMEM((2, width, width), BF),
        pltpu.VMEM((own, width), BF),
        pltpu.VMEM((nb, width, BLK), BF),
        pltpu.VMEM((shards, nb, width, BLK), BF),
        pltpu.VMEM((shards, own, width), BF),
    )

    def attention(g_v, k_v, v_v, kt_v, delta, bias, dk, dv, dqt, dkt, dvt):
        gain1 = parameter(0)
        def keys(hf):
            base = pl.multiple_of(hf * half, 128)
            return (
                fetch(k_i.at[pl.ds(hf * pairs, pairs)], k_v, 0),
                fetch(v_i.at[pl.ds(hf * pairs, pairs)], v_v, 1),
                fetch(kt_i.at[:, pl.ds(base, half), :], kt_v, 2),
            )

        for c in keys(far_half):
            c.start()

        def between(out_v, ctxt_v):
            low_v = ctx_v
            o_in, c_in = fetch(out_w.at[0], out_v, 6), fetch(ctxt, ctxt_v, 7)
            o_in.start()
            c_in.start()

            def norm_back(b, c):
                g = g_hid[rows(b), :]
                n = xhat[rows(b), :]
                vec_acc[0:1, :] += jnp.sum(g * n, axis=0, keepdims=True)
                vec_acc[1:2, :] += jnp.sum(g, axis=0, keepdims=True)
                e = g * gain1
                res = inv[rows(b), 0:1] * (e - mean(e) - n * mean(e * n))
                g_hid[rows(b), :] = res
                low_v[rows(b), :] = res.astype(BF)
                return c

            lax.fori_loop(0, nb, norm_back, 0)
            o_in.wait()
            c_in.wait()

            def after(b, c):
                low = low_v[rows(b), :]
                gc = nt(low, out_v[...]).astype(BF)
                for i in range(all_pairs):
                    g_v[i, rows(b), :] = gc[:, i * 128 : (i + 1) * 128]
                prod = nt(out_v[...], low).astype(BF).astype(F32) * ctxt_v[b]
                for i in range(2 * all_pairs):
                    delta[b, i] = jnp.sum(prod[i * HEAD_WIDTH : (i + 1) * HEAD_WIDTH, :], axis=0, keepdims=True)
                return c

            lax.fori_loop(0, nb, after, 0)
            vstep(0).start()
            ups[0].xs()

            def grad_out(i, c):
                @pl.when(i == 2)
                def _():
                    out_c.core(0).wait_send()

                base = pl.multiple_of(shard_of(i) * shard_rows, 16)
                acc = jnp.zeros((shard_rows, width), F32)
                for b in range(nb):
                    acc += nn(ctxt_v[b, pl.ds(base, shard_rows), :].astype(BF), low_v[b * BLK : (b + 1) * BLK, :])
                out_c.mine[slot_of(i)] = acc.astype(BF)
                hooks_at(i, {0: [out_c.c0], 2: [out_c.c1]})
                return c

            lax.fori_loop(0, shards, grad_out, 0)
            downs[0].yy()
            downs[1].r()
            out_c.f()

        pl.run_scoped(
            between,
            pltpu.VMEM((width, width), BF),
            pltpu.VMEM((nb, width, BLK), F32),
        )
        def unit(hf, t):
            j, i = t // pairs, t % pairs
            p = hf * pairs + i
            ws = window_start(h, j, nb, row_blocks)

            @pl.when(i == 0)
            def _():
                for kb in range(row_blocks):
                    bias[kb * BLK : (kb + 1) * BLK, :] = mask_of(seg[ws + kb], seg[HALO + j])

            q = q_v[p, rows(j), :]
            g = g_v[p, rows(j), :]
            lane = lax.broadcasted_iota(jnp.int32, q.shape, 1)
            qm = [jnp.where(lane // HEAD_WIDTH == hh, q, jnp.zeros_like(q)) for hh in range(2)]
            gm = [jnp.where(lane // HEAD_WIDTH == hh, g, jnp.zeros_like(g)) for hh in range(2)]
            window = pl.ds(pl.multiple_of(ws * BLK, BLK), row_blocks * BLK)
            scores = nt(k_v[i, window, :], jnp.concatenate(qm, axis=0))
            g_probs = nt(v_v[i, window, :], jnp.concatenate(gm, axis=0))
            probs, g_scores = [], []
            for hh in range(2):
                cols = slice(hh * BLK, (hh + 1) * BLK)
                prob = jnp.exp(scores[:, cols] + bias[...] - lse[j, 2 * p + hh])
                g_scores.append((prob * (g_probs[:, cols] - delta[j, 2 * p + hh])).astype(BF))
                probs.append(prob.astype(BF))
            dv[i, window, :] += nn(probs[0], gm[0]) + nn(probs[1], gm[1])
            dk[i, window, :] += nn(g_scores[0], qm[0]) + nn(g_scores[1], qm[1])
            for hh in range(2):
                at = pl.ds(pl.multiple_of((2 * i + hh) * HEAD_WIDTH, HEAD_WIDTH), HEAD_WIDTH)
                acc = jnp.zeros((HEAD_WIDTH, BLK), F32)
                for kb in range(row_blocks):
                    acc += nn(kt_v[ws + kb, at, :], g_scores[hh][kb * BLK : (kb + 1) * BLK, :])
                dqt[j, at, :] = (acc * HEAD_WIDTH**-0.5).astype(BF)

        def attend_half(hf, plan, then):
            dk[...] = jnp.zeros_like(dk)
            dv[...] = jnp.zeros_like(dv)

            def body(t, c):
                hooks_at(t, plan)
                unit(hf, t)
                return c

            lax.fori_loop(0, nb * pairs, body, 0)
            for step in then:
                step()
            for b in range(nw):
                lo, hi = b * BLK, (b + 1) * BLK
                dkt[b] = jnp.concatenate([dk[p, lo:hi, :].astype(BF) for p in range(pairs)], axis=1).T
                dvt[b] = jnp.concatenate([dv[p, lo:hi, :].astype(BF) for p in range(pairs)], axis=1).T

        def weight_grads(which, slot, then):
            at = pl.multiple_of(which * shard_rows, 16)
            for c, src, blocks in ((q_c, dqt, range(HALO, HALO + nb)), (k_c, dkt, range(nw)), (v_c, dvt, range(nw))):
                acc = jnp.zeros((shard_rows, width), F32)
                for b in blocks:
                    acc += nn(src[b - blocks[0], pl.ds(at, shard_rows), :], x_v[b * BLK : (b + 1) * BLK, :])
                c.mine[slot] = acc.astype(BF)
                then(c)

        def input_grads(hf, last):
            base = pl.multiple_of(hf * half, 128)
            wk, wv = w_v.at[1, pl.ds(base, half), :], w_v.at[2, pl.ds(base, half), :]

            def block(b):
                kb = jnp.concatenate([dk[p, rows(b), :].astype(BF) for p in range(pairs)], axis=1)
                vb = jnp.concatenate([dv[p, rows(b), :].astype(BF) for p in range(pairs)], axis=1)
                return nn(kb, wk[...]) + nn(vb, wv[...])

            def side(i, c):
                b = i + jnp.where(i >= HALO, nb, 0)
                total = block(b)
                if last:
                    total = total + gx_side[rows(i), :].astype(F32)
                gx_side[rows(i), :] = total.astype(BF)
                return c

            lax.fori_loop(0, 2 * HALO, side, 0)

            def inner(j, c):
                g_hid[rows(j), :] += block(j + HALO) + nn(dqt[j].T, w_v[0, pl.ds(base, half), :])
                return c

            return lambda: lax.fori_loop(0, nb, inner, 0)

        for c in keys(far_half):
            c.wait()
        d0, d1 = downs
        u0, u1 = ups
        vs = [functools.partial(vnext, i) for i in range(len(vec_ids))]
        vs = [functools.partial(vnext, i) for i in range(len(vec_ids))]
        attend_half(far_half, {
            1: [vs[0], out_c.s], 3: [d0.zz, u1.xs], 4: [d1.yy], 5: [u0.r], 7: [d0.w, d1.zz],
        }, [u0.yy, out_c.xs])
        for c in keys(x_half):
            c.start()
        weight_grads(1 - core, 0, lambda p: p.c0())
        u1.r()
        d0.u()
        d1.w()
        weight_grads(core, 1, lambda p: (p.f(), p.xs()))
        vs[1]()
        input_grads(far_half, False)()
        u0.zz()
        for c in keys(x_half):
            c.wait()
        attend_half(x_half, {
            0: [out_c.r], 1: [d1.u], 2: [u1.yy], 3: [vs[2]], 4: [u0.w, out_c.yy], 5: [u1.zz], 6: [vs[3], d0.end],
            7: [u0.u, d1.end], 8: [out_c.zz],
        }, [])
        u1.w()
        for p in (q_c, k_c, v_c):
            p.core(0).wait_send()
        weight_grads(1 - core, 0, lambda p: p.c1())
        out_c.w()
        weight_grads(core, 2, lambda p: None)
        for p in (q_c, k_c, v_c):
            p.s()
            p.r()
        u1.u()
        for step in vs[4:]:
            step()
        finish = input_grads(x_half, True)

        @pl.when(h > 0)
        def _():
            to_left.start()

        @pl.when(h < groups - 1)
        def _():
            to_right.start()

        out_c.u()
        for p in (q_c, k_c, v_c):
            p.yy()
        u0.end()
        for p in (q_c, k_c, v_c):
            p.zz()
        finish()
        u1.end()
        out_c.end()
        for p in (q_c, k_c, v_c):
            p.w()
        from_right, from_left = pl.ds(halo + own, halo), pl.ds(0, halo)

        @pl.when(h < groups - 1)
        def _():
            to_left.wait_recv()
            fetch(o_left, x_v.at[from_right, :], 0).start()

        @pl.when(h > 0)
        def _():
            to_right.wait_recv()
            fetch(o_right, x_v.at[from_left, :], 1).start()

        for p in (q_c, k_c, v_c):
            p.u()

        @pl.when(h < groups - 1)
        def _():
            fetch(o_left, x_v.at[from_right, :], 0).wait()
            g_hid[own - halo :, :] += x_v[from_right, :].astype(F32)

        @pl.when(h > 0)
        def _():
            fetch(o_right, x_v.at[from_left, :], 1).wait()
            g_hid[:halo, :] += x_v[from_left, :].astype(F32)

        tok_out = fetch(g_hid, o_tok, 3)
        tok_out.start()
        for p in (q_c, k_c, v_c):
            p.end()
        tok_out.wait()

    to_left = remote(gx_side.at[pl.ds(0, halo), :], o_left, side_send.at[0], side_recv.at[0], (r, h - 1))
    to_right = remote(gx_side.at[pl.ds(halo, halo), :], o_right, side_send.at[1], side_recv.at[1], (r, h + 1))

    pl.run_scoped(
        attention,
        pltpu.VMEM((all_pairs, own, 128), BF),
        pltpu.VMEM((pairs, nw * BLK, 128), BF),
        pltpu.VMEM((pairs, nw * BLK, 128), BF),
        pltpu.VMEM((nw, half, BLK), BF),
        pltpu.VMEM((nb, 2 * all_pairs, 1, BLK), F32),
        pltpu.VMEM((row_blocks * BLK, BLK), F32),
        pltpu.VMEM((pairs, nw * BLK, 128), F32),
        pltpu.VMEM((pairs, nw * BLK, 128), F32),
        pltpu.VMEM((nb, half, BLK), BF),
        pltpu.VMEM((nw, half, BLK), BF),
        pltpu.VMEM((nw, half, BLK), BF),
    )

    o_vec[...] = vacc[len(vec_ids) - 1]
    for g in (gq, go, gu, gd):
        g.sent()
    for p in parts:
        p.done()
    for i in range(len(vec_ids)):
        vstep(i).wait_send()

    @pl.when(h > 0)
    def _():
        to_left.wait_send()

    @pl.when(h < groups - 1)
    def _():
        to_right.wait_send()


def layer(groups, row_blocks, row_devices, tok, cot, qkv_own, out_own, up_own, down_own, vec_own, lengths):
    own, width = tok.shape
    shard_rows = width // groups
    nb = own // BLK
    nw = nb + 2 * HALO
    all_pairs = width // 128
    bits = other_bits(row_devices)
    split = width // 2
    chunks = [(name, lo, split) for name in ("down", "up") for lo in range(0, width, split)]
    chunks += [(name, 0, shard_rows) for name in ("out", "q", "k", "v")]
    hops = 4 + len(bits)
    scratch = [
        pltpu.VMEM((3, width, width), BF),
        pltpu.VMEM((nw * BLK, width), BF),
        pltpu.VMEM((all_pairs, own, 128), BF),
        pltpu.VMEM((own, width), BF),
        pltpu.VMEM((nb, 2 * all_pairs, 1, BLK), F32),
        pltpu.VMEM((nw, 1, BLK), F32),
        pltpu.VMEM((groups,) + vec_own.shape, BF),
        pltpu.VMEM((own, width), F32),
        pltpu.VMEM((own, 128), F32),
        pltpu.VMEM((own, width), F32),
        pltpu.VMEM((2 * HALO * BLK, width), BF),
        pltpu.VMEM((8, width), F32),
        pltpu.VMEM((hops, 8, width), F32),
        pltpu.VMEM((hops, 8, width), F32),
    ]
    for _, _, n in chunks:
        scratch += [
            pltpu.VMEM((3, n, width), BF),
            pltpu.VMEM((2, n, width), BF),
            pltpu.VMEM((n, width), BF),
            pltpu.VMEM((n // 2, width), BF),
            pltpu.VMEM((n // 4, width), BF),
            pltpu.VMEM((max(1, len(bits)), n // 4, width), BF),
        ]
    dma = pltpu.SemaphoreType.DMA
    scratch += [dma((len(chunks), 8 + len(bits)))] * 2 + [dma((len(chunks), 3))] + [dma((4, 12))] * 2
    scratch += [dma((2 * HALO,))] * 2 + [dma((2,))] * 2 + [dma((groups - 1,))] * 2 + [dma((hops,))] * 2 + [dma((8,))]
    s = jax.ShapeDtypeStruct
    side = s((HALO * BLK, width), BF)
    outs = [
        (s((own, width), BF), ANY),
        (s((width, width), BF), ANY),
        (s((width, width), BF), ANY),
        (s((shard_rows, width), BF), ANY),
        (s((3, shard_rows, width), BF), ANY),
        (s((own, width), F32), ANY),
        (side, ANY),
        (side, ANY),
        (s((8, width), F32), VM),
        (s((1, width, width), BF), ANY),
        (s((1, groups * width, width), BF), ANY),
        (s((1, groups * width, width), BF), ANY),
        (s((nb, width, BLK), F32), ANY),
        (s((all_pairs, nw * BLK, 128), BF), ANY),
        (s((all_pairs, nw * BLK, 128), BF), ANY),
        (s((nw, width, BLK), BF), ANY),
    ]
    return pl.pallas_call(
        functools.partial(layer_kernel, groups, row_blocks, bits, chunks),
        out_shape=[o[0] for o in outs],
        in_specs=[ANY] * 6 + [VM] * 2,
        out_specs=[o[1] for o in outs],
        scratch_shapes=scratch,
        compiler_params=pltpu.CompilerParams(collective_id=0, has_side_effects=True, vmem_limit_bytes=VMEM_LIMIT),
        name="layer",
    )(tok, cot, qkv_own, out_own, up_own, down_own, vec_own, lengths)


def local(
    groups, row_devices,
    tokens, lengths, w_query, w_key, w_value, w_out, w_up, w_down,
    gain_first, shift_first, gain_second, shift_second, cotangent,
):
    packed_rows = lengths.shape[0]
    own, width = tokens.shape
    row_length = groups * own // packed_rows
    row_blocks = row_length // BLK
    h = lax.axis_index("heads")
    n_vec = gain_first.shape[0]
    vec_own = jnp.concatenate([gain_first, shift_first, gain_second, shift_second])
    vec_own = jnp.broadcast_to(vec_own[None, :], (16, width))
    qkv_own = jnp.stack([w_query.T, w_key.T, w_value.T])
    mixed, o_down, o_up, o_out, o_qkv, o_tok, _, _, o_vec = layer(
        groups, row_blocks, row_devices, tokens, cotangent, qkv_own, w_out[None], w_up[None], w_down[None], vec_own, lengths
    )[:9]
    mine = lax.dynamic_slice(o_vec, (0, n_vec * h), (4, n_vec))
    wide = lambda a: a.astype(F32)
    return (
        mixed, o_tok, wide(o_qkv[0].T), wide(o_qkv[1].T), wide(o_qkv[2].T), wide(o_out), wide(o_up), wide(o_down),
        mine[0], mine[1], mine[2], mine[3],
    )


def solution(mesh):
    both, heads = P(("rows", "heads"), None), P("heads")
    cols, rows = P(None, "heads"), P("heads", None)
    return jax.shard_map(
        functools.partial(local, mesh.shape["heads"], mesh.shape["rows"]),
        mesh=mesh,
        in_specs=(both, P("rows", None), cols, cols, cols, rows, cols, rows, heads, heads, heads, heads, both),
        out_specs=(both, both, cols, cols, cols, rows, cols, rows, heads, heads, heads, heads),
        check_vma=False,
    )
```

```python
import functools

import jax
import jax.numpy as jnp
from jax import lax
from jax.experimental import pallas as pl
from jax.experimental.pallas import tpu as pltpu
from jax.sharding import PartitionSpec as P

MESH = pl.DeviceIdType.MESH
BF = jnp.bfloat16
F32 = jnp.float32
HEAD_WIDTH = 64
LONGEST_DOC = 512
BLK = 256
HALO = LONGEST_DOC // BLK
NORM_EPS = 1e-12
VMEM_LIMIT = 62 * 1024 * 1024


def nt(left, right):
    return lax.dot_general(left, right, (((1,), (1,)), ((), ())), preferred_element_type=F32)


def nn(left, right):
    return lax.dot_general(left, right, (((1,), (0,)), ((), ())), preferred_element_type=F32)


def flip(index, bit):
    return index + bit - 2 * bit * ((index // bit) % 2)


def place():
    r, h = lax.axis_index("rows"), lax.axis_index("heads")
    return r, h


def greet(ids):
    barrier = pltpu.get_barrier_semaphore()
    for who in ids:
        pl.semaphore_signal(barrier, inc=1, device_id=who, device_id_type=MESH)
    pl.semaphore_wait(barrier, len(ids))


def group_of(r, h, groups):
    return [(r, lax.rem(h + i, groups)) for i in range(1, groups)]


def remote(src, dst, send, recv, who):
    return pltpu.make_async_remote_copy(
        src_ref=src, dst_ref=dst, send_sem=send, recv_sem=recv, device_id=who, device_id_type=MESH
    )


class Gather:
    def __init__(self, own, full, sems, at):
        self.own, self.full, self.sems, self.at = own, full, sems, at
        self.n = own.shape[1]
        self.u = self.n // 12
        r, h = place()
        self.r, self.h = r, h
        y, z = r % 2, (r // 2) % 2
        self.k = 2 * z + y
        self.ky = 2 * z + 1 - y
        self.kz = 2 * (1 - z) + y
        self.kd = 3 - self.k
        self.hx = flip(h, 2)
        self.hc = flip(h, 1)
        self.by_x = (r, self.hx)
        self.by_c = (r, self.hc)
        self.by_y = (flip(r, 1), h)
        self.by_z = (flip(r, 2), h)

    def rows(self, shard, sub, count):
        u = self.u
        return pl.ds(pl.multiple_of(shard * self.n + sub * u, 16), count * u)

    def part(self, slot, who, shard, sub, count, own=False):
        dst = self.full.at[:, self.rows(shard, sub, count), :]
        src = self.own.at[:, self.rows(0, sub, count), :] if own else dst
        send, recv = self.sems
        return remote(src, dst, send.at[self.at, slot], recv.at[self.at, slot], who)

    def x_main(self):
        return self.part(0, self.by_x, self.h, 3 * self.k, 3, own=True)

    def x_diag(self):
        return self.part(1, self.by_x, self.h, 3 * self.kd, 1, own=True)

    def y_main(self):
        return self.part(2, self.by_y, self.hx, 3 * self.k, 3)

    def z_main(self):
        return self.part(3, self.by_z, self.hx, 3 * self.k, 3)

    def y_diag(self):
        return self.part(4, self.by_y, self.hx, 3 * self.kz + 1, 1)

    def z_diag(self):
        return self.part(5, self.by_z, self.hx, 3 * self.ky + 2, 1)

    def c_own(self):
        return self.part(6, self.by_c, self.h, 0, 12, own=True)

    def c_part(self, i):
        return self.part(7 + i, self.by_c, self.hx, 3 * (self.k, self.ky, self.kz, self.kd)[i], 3)

    def local(self):
        send, _ = self.sems
        return pltpu.make_async_copy(
            self.own, self.full.at[:, self.rows(self.h, 0, 12), :], send.at[self.at, 11]
        )

    def start_x(self):
        self.x_main().start()
        self.x_diag().start()

    def start_main(self):
        self.x_main().start()

    def start_diag(self):
        self.x_diag().start()

    def start_c(self, keep):
        self.c_own().start()
        if keep:
            self.local().start()

    def step_x(self):
        self.x_main().wait_recv()
        self.y_main().start()
        self.z_main().start()
        self.c_part(0).start()

    def step_yz(self):
        self.y_main().wait_recv()
        self.z_diag().start()
        self.c_part(1).start()
        self.z_main().wait_recv()
        self.y_diag().start()
        self.c_part(2).start()

    def step_diag(self):
        self.x_diag().wait_recv()
        self.y_diag().wait_recv()
        self.z_diag().wait_recv()
        self.c_part(3).start()

    def near(self, keep):
        self.c_own().wait_recv()
        if keep:
            self.local().wait()

    def far(self):
        for i in range(4):
            self.c_part(i).wait_recv()

    def sent(self):
        for copy in (self.x_main(), self.x_diag(), self.y_main(), self.z_main(), self.y_diag(), self.z_diag(), self.c_own()):
            copy.wait_send()
        for i in range(4):
            self.c_part(i).wait_send()


def window_start(h, j, own_blocks, row_blocks):
    g = own_blocks * h + j
    first = own_blocks * h - HALO
    row = row_blocks * (g // row_blocks)
    return jnp.clip(row, first, first + own_blocks + 2 * HALO - row_blocks) - first


def mask_of(keys, queries):
    down = jnp.broadcast_to(keys, (8, BLK)).T[:, 0:1]
    return jnp.where(down == queries, 0.0, -1e30).astype(F32)


ANY = pl.BlockSpec(memory_space=pl.ANY)
VM = pl.BlockSpec(memory_space=pltpu.VMEM)


def gelu_parts(u):
    bell = jnp.exp(-0.5 * u * u)
    base = 1.0 + (0.3275911 * 0.7071067811865476) * jnp.abs(u)
    t = pl.reciprocal(base, approx=True)
    t = t * (2.0 - base * t)
    poly = t * (0.127414796 + t * (-0.142248368 + t * (0.7107068705 + t * (-0.7265760135 + t * 0.5307027145))))
    tail = poly * bell
    cdf = jnp.where(u >= 0.0, 1.0 - tail, tail)
    return u * cdf, cdf + u * (bell * 0.3989422804014327)


class Sum:
    def __init__(self, n, bits, bufs, sems, at, turned):
        self.n, self.bits, self.at = n, bits, at
        self.mine, self.rc, self.rx, self.ry, self.rz, self.rest = bufs
        self.send, self.recv, self.keep = sems
        r, h = place()
        self.y, self.z = r % 2, (r // 2) % 2
        self.by_x, self.by_c = (r, flip(h, 2)), (r, flip(h, 1))
        self.by_y, self.by_z = (flip(r, 1), h), (flip(r, 2), h)
        if turned:
            self.y, self.z, self.by_y, self.by_z = self.z, self.y, self.by_z, self.by_y
        self.by_rest = [(flip(r, b), h) for b in bits]

    def copy(self, slot, src, dst, who):
        return remote(src, dst, self.send.at[self.at, slot], self.recv.at[self.at, slot], who)

    def core(self, i):
        return self.copy(i, self.mine.at[0], self.rc.at[i], self.by_c)

    def x(self):
        return self.copy(2, self.mine.at[1], self.rx, self.by_x)

    def half(self, which):
        return pl.ds(pl.multiple_of(which * (self.n // 2), 16), self.n // 2)

    def quarter(self, half, which):
        return pl.ds(pl.multiple_of(half * (self.n // 2) + which * (self.n // 4), 16), self.n // 4)

    def own(self):
        return self.mine.at[2, self.quarter(self.y, self.z), :]

    def landed(self, half, which):
        return self.rx.at[self.quarter(half, which), :]

    def y_down(self):
        return self.copy(3, self.mine.at[2, self.half(1 - self.y), :], self.ry, self.by_y)

    def z_down(self):
        return self.copy(4, self.mine.at[2, self.quarter(self.y, 1 - self.z), :], self.rz, self.by_z)

    def z_up(self):
        return self.copy(5, self.own(), self.landed(self.y, self.z), self.by_z)

    def y_up(self):
        return self.copy(6, self.own(), self.landed(self.y, self.z), self.by_y)

    def y_up2(self):
        return self.copy(7, self.landed(self.y, 1 - self.z), self.landed(self.y, 1 - self.z), self.by_y)

    def swap(self, i):
        return self.copy(8 + i, self.own(), self.rest.at[i], self.by_rest[i])

    def add(self, ref, got):
        ref[...] = (ref[...].astype(F32) + got[...].astype(F32)).astype(BF)

    def c0(self):
        self.core(0).start()

    def f(self):
        self.core(0).wait_recv()
        self.add(self.mine.at[1], self.rc.at[0])

    def xs(self):
        self.x().start()

    def c1(self):
        self.core(1).start()

    def s(self):
        self.core(1).wait_recv()
        self.add(self.mine.at[2], self.rc.at[1])

    def r(self):
        self.x().wait_recv()
        self.add(self.mine.at[2], self.rx)
        self.y_down().start()

    def yy(self):
        self.y_down().wait_recv()
        self.add(self.mine.at[2, self.half(self.y), :], self.ry)
        self.z_down().start()

    def zz(self):
        self.z_down().wait_recv()
        self.add(self.own(), self.rz)
        if self.bits:
            self.swap(0).start()

    def w(self):
        for i in range(len(self.bits)):
            self.swap(i).wait_recv()
            self.swap(i).wait_send()
            self.add(self.own(), self.rest.at[i])
            if i + 1 < len(self.bits):
                self.swap(i + 1).start()
        self.z_up().start()
        self.y_up().start()

    def u(self):
        self.z_up().wait_recv()
        self.y_up2().start()

    def outs(self, out, lo):
        def local(i, src, rows):
            start = pl.multiple_of(lo + rows.start, 16)
            return pltpu.make_async_copy(src, out.at[pl.ds(start, rows.size), :], self.keep.at[self.at, i])

        mine, beside, other = self.quarter(self.y, self.z), self.quarter(self.y, 1 - self.z), self.half(1 - self.y)
        return (
            local(0, self.own(), mine),
            local(1, self.rx.at[beside, :], beside),
            local(2, self.rx.at[other, :], other),
        )

    def e(self, out, lo):
        self.y_up().wait_recv()
        self.y_up2().wait_recv()
        for c in self.outs(out, lo):
            c.start()

    def sent(self, out, lo):
        for c in (self.core(1), self.x(), self.y_down(), self.z_down(), self.z_up(), self.y_up(), self.y_up2()):
            c.wait_send()
        for c in self.outs(out, lo):
            c.wait()


def other_bits(count):
    bits, b = [], 4
    while b < count:
        bits.append(b)
        b *= 2
    return tuple(bits)


def hooks_at(t, plan):
    for at, steps in plan.items():

        @pl.when(t == at)
        def _():
            for step in steps:
                step()


def layer_kernel(
    groups, row_blocks, bits, chunks,
    tok, cot, qkv_own, out_own, up_own, down_own, vec_own, lengths,
    mixed, o_down, o_up, o_out, o_qkv, o_tok, o_left, o_right, o_vec,
    out_w, up_w, down_w, ctxt, k_i, v_i, kt_i,
    w_v, x_v, q_v, ctx_v, lse, seg, vec_all, xhat, inv, g_hid, gx_side, vec_acc, vin, vacc, *scratch,
):
    r, h = place()
    own, width = tok.shape
    nb = own // BLK
    nw = nb + 2 * HALO
    halo = HALO * BLK
    shards = groups
    all_pairs = q_v.shape[0]
    pairs = all_pairs // 2
    half = pairs * 128
    shard_rows = half // 2
    x_half = (h // 2) % 2
    far_half = 1 - x_half
    core = h % 2
    rows = lambda b: pl.ds(pl.multiple_of(b * BLK, BLK), BLK)
    mean = lambda v: jnp.mean(v, axis=1, keepdims=True)
    n_chunks = len(chunks)
    (send, recv, keep, gsend, grecv, in_send, in_recv, side_send, side_recv, psend, precv, vsend, vrecv, loc) = scratch[6 * n_chunks :]
    sems = (send, recv, keep)
    turned = (1, 3, 6)
    outs = {"down": o_down, "up": o_up, "out": o_out, "q": o_qkv.at[0], "k": o_qkv.at[1], "v": o_qkv.at[2]}
    parts = [Sum(n, bits, scratch[6 * i : 6 * i + 6], sems, i, i in turned) for i, (_, _, n) in enumerate(chunks)]
    by_name = {}
    for part, (name, lo, _) in zip(parts, chunks):
        part.end = functools.partial(part.e, outs[name], lo)
        part.done = functools.partial(part.sent, outs[name], lo)
        by_name.setdefault(name, []).append(part)
    downs, ups, (out_c,) = by_name["down"], by_name["up"], by_name["out"]
    q_c, k_c, v_c = (by_name[name][0] for name in "qkv")
    one = parts[0]
    gq = Gather(qkv_own, w_v, (gsend, grecv), 0)
    go = Gather(out_own, out_w, (gsend, grecv), 1)
    gu = Gather(up_own, up_w, (gsend, grecv), 2)
    gd = Gather(down_own, down_w, (gsend, grecv), 3)

    def shard_of(i):
        across = 1 - i // 2
        other = 1 - i % 2
        return h + across * (2 - 4 * x_half) + other * (1 - 2 * core)

    def slot_of(i):
        return (i % 2) * (1 + i // 2)

    def fetch(src, dst, i):
        return pltpu.make_async_copy(src, dst, loc.at[i])

    vec_ids = [one.by_c, one.by_x, one.by_y, one.by_z] + one.by_rest

    def vstep(i):
        src = vec_acc if i == 0 else vacc.at[i - 1]
        return remote(src, vin.at[i], vsend.at[i], vrecv.at[i], vec_ids[i])

    def vnext(i):
        vstep(i).wait_recv()
        vacc[i] = (vec_acc[...] if i == 0 else vacc[i - 1]) + vin[i]
        if i + 1 < len(vec_ids):
            vstep(i + 1).start()

    def parameter(i):
        n = width // groups
        return jnp.concatenate([vec_all[s].astype(F32)[0:1, i * n : (i + 1) * n] for s in range(groups)], axis=1)

    def project(vt, k_s, v_s, kt_s, bias, ctx_t):
        total_blocks = groups * nb
        def to_right(i):
            src, dst = pl.ds(own - halo + i * BLK, BLK), pl.ds(i * BLK, BLK)
            return remote(tok.at[src, :], x_v.at[dst, :], in_send.at[i], in_recv.at[i], (r, h + 1))

        def to_left(i):
            src, dst = pl.ds(i * BLK, BLK), pl.ds(halo + own + i * BLK, BLK)
            return remote(tok.at[src, :], x_v.at[dst, :], in_send.at[HALO + i], in_recv.at[HALO + i], (r, h - 1))

        def both(to, step):
            for i in range(HALO):
                step(to(i))

        start, arrived, gone = (lambda c: c.start()), (lambda c: c.wait_recv()), (lambda c: c.wait_send())
        even = h % 2 == 0
        slow_right = jnp.logical_and(h % 2 == 1, h < groups - 1)
        slow_left = jnp.logical_and(even, h > 0)

        odd = h % 2 == 1

        def par(i):
            who = (r, lax.rem(h + 1 + i, groups))
            return remote(vec_own, vec_all.at[h], psend.at[i], precv.at[groups - 2 - i], who)

        def par_from(i):
            return remote(vec_own, vec_all.at[h], psend.at[i], precv.at[i], (r, lax.rem(h + 1 + i, groups)))

        mine = fetch(tok, x_v.at[pl.ds(halo, own), :], 0)
        mine.start()
        greet(group_of(r, h, groups) + [one.by_y, one.by_z] + one.by_rest)

        @pl.when(slow_right)
        def _():
            to_right(HALO - 1).start()

        @pl.when(slow_left)
        def _():
            to_left(0).start()

        @pl.when(even)
        def _():
            both(to_right, start)

        @pl.when(odd)
        def _():
            both(to_left, start)

        gq.start_c(True)
        gq.start_x()
        for i in range(groups - 1):
            par(i).start()
        vec_all[h] = vec_own[...]

        @pl.when(h == 0)
        def _():
            x_v[pl.ds(0, halo), :] = jnp.zeros((halo, width), BF)

        @pl.when(h == groups - 1)
        def _():
            x_v[pl.ds(halo + own, halo), :] = jnp.zeros((halo, width), BF)

        packed, docs = lengths.shape
        down = lax.broadcasted_iota(jnp.int32, (docs, docs), 0)
        across = lax.broadcasted_iota(jnp.int32, (docs, docs), 1)
        for b in range(nw):
            g = nb * h - HALO + b
            row = jnp.clip(g // row_blocks, 0, packed - 1)
            sizes = lengths[pl.ds(row, 1), :].astype(F32)
            ends = jnp.sum(jnp.where(across <= down, jnp.broadcast_to(sizes, (docs, docs)), 0.0), axis=1, keepdims=True)
            at = (lax.broadcasted_iota(jnp.int32, (docs, BLK), 1) + (g % row_blocks) * BLK).astype(F32)
            ids = jnp.sum(jnp.where(at >= ends, 1.0, 0.0), axis=0, keepdims=True) + (row * docs).astype(F32)
            inside = jnp.logical_and(g >= 0, g < total_blocks)
            seg[b] = jnp.where(inside, ids, -1.0)
        for j in range(nb):
            ws = window_start(h, j, nb, row_blocks)
            for kb in range(row_blocks):
                bias[j, kb] = mask_of(seg[ws + kb], seg[HALO + j])

        def project_keys(hx, b):
            base = pl.multiple_of(hx * half, 128)
            xb = x_v[rows(b), :]
            wk = w_v[1, pl.ds(base, half), :]
            wv = w_v[2, pl.ds(base, half), :]
            key = nt(xb, wk).astype(BF)
            value = nt(xb, wv).astype(BF)
            for i in range(pairs):
                k_s[hx * pairs + i, rows(b), :] = key[:, i * 128 : (i + 1) * 128]
                v_s[hx * pairs + i, rows(b), :] = value[:, i * 128 : (i + 1) * 128]
            kt_s[b, pl.ds(base, half), :] = nt(wk, xb).astype(BF)
            vt[b, pl.ds(base, half), :] = nt(wv, xb).astype(BF)

        def project_query(hx, b):
            base = pl.multiple_of(hx * half, 128)
            xb = x_v[rows(b + HALO), :]
            query = nt(xb, w_v[0, pl.ds(base, half), :]).astype(BF) * BF(HEAD_WIDTH**-0.5)
            for i in range(pairs):
                q_v[hx * pairs + i, rows(b), :] = query[:, i * 128 : (i + 1) * 128]

        def side_keys(hx, first):
            def body(b, c):
                project_keys(hx, first + b)
                return c

            lax.fori_loop(0, HALO, body, 0)

        def attend(hx, t):
            j = jnp.where(odd, t // pairs, nb - 1 - t // pairs)
            p = hx * pairs + t % pairs
            ws = window_start(h, j, nb, row_blocks)
            q = q_v[p, rows(j), :]
            lane = lax.broadcasted_iota(jnp.int32, q.shape, 1)
            q_both = jnp.concatenate([jnp.where(lane // HEAD_WIDTH == hh, q, jnp.zeros_like(q)) for hh in range(2)], axis=0)
            scores, tops = [[], []], [None, None]
            for kb in range(row_blocks):
                both_s = nt(k_s[p, rows(ws + kb), :], q_both)
                for hh in range(2):
                    s = both_s[:, hh * BLK : (hh + 1) * BLK] + bias[j, kb]
                    m = jnp.max(s.reshape(BLK // 8, 8, BLK), axis=0)
                    tops[hh] = m if kb == 0 else jnp.maximum(tops[hh], m)
                    scores[hh].append(s)
            tops = [jnp.max(m, axis=0, keepdims=True) for m in tops]
            totals = [jnp.zeros((8, BLK), F32) for _ in range(2)]
            accs = [jnp.zeros((HEAD_WIDTH, BLK), F32) for _ in range(2)]
            at = [pl.ds(pl.multiple_of((2 * p + hh) * HEAD_WIDTH, HEAD_WIDTH), HEAD_WIDTH) for hh in range(2)]
            for kb in range(row_blocks):
                for hh in range(2):
                    e = jnp.exp(scores[hh][kb] - tops[hh])
                    totals[hh] = totals[hh] + jnp.sum(e.reshape(BLK // 8, 8, BLK), axis=0)
                    accs[hh] = accs[hh] + nn(vt[ws + kb, at[hh], :], e.astype(BF))
            for hh in range(2):
                total = jnp.sum(totals[hh], axis=0, keepdims=True)
                ctx_t[j, at[hh], :] = accs[hh] / total
                lse[j, 2 * p + hh] = tops[hh] + jnp.log(total)

        def attend_all(hx, plan):
            def body(t, c):
                hooks_at(t, plan)
                attend(hx, t)
                return c

            lax.fori_loop(0, nb * pairs, body, 0)

        def slow_block(near):
            @pl.when(slow_right)
            def _():
                to_left(0 if near else 1).wait_recv()

            @pl.when(slow_left)
            def _():
                to_right(1 if near else 0).wait_recv()

            project_keys(x_half, jnp.where(odd, HALO + nb + (0 if near else 1), 1 if near else 0))

        def more_halo():
            @pl.when(slow_right)
            def _():
                to_right(0).start()

            @pl.when(slow_left)
            def _():
                to_left(1).start()

        mine.wait()
        gq.near(True)
        for b in range(nb):
            project_query(x_half, b)
        lax.fori_loop(HALO, HALO + nb, lambda b, c: (project_keys(x_half, b), c)[1], 0)

        @pl.when(odd)
        def _():
            both(to_right, arrived)

        @pl.when(even)
        def _():
            both(to_left, arrived)

        side_keys(x_half, jnp.where(odd, 0, HALO + nb))
        last = jnp.where(odd, nw - 1, 0)
        for i in range(all_pairs):
            k_s[i, rows(last), :] = jnp.zeros((BLK, 128), BF)
        vt[last] = jnp.zeros((width, BLK), BF)
        attend_all(x_half, {
            0: [lambda: go.start_c(True), lambda: gu.start_c(False)],
            2: [more_halo], 3: [gq.step_x, functools.partial(slow_block, True), lambda: gd.start_c(False)],
            6: [functools.partial(slow_block, False), go.start_x, gu.start_x], 7: [gq.step_yz],
        })
        gd.start_x()
        gq.step_diag()
        go.step_x()
        gq.far()
        for b in range(nb):
            project_query(far_half, b)
        lax.fori_loop(0, nw, lambda b, c: (project_keys(far_half, b), c)[1], 0)
        keys_out = [fetch(a, b, i) for i, (a, b) in enumerate(((k_s, k_i), (v_s, v_i), (kt_s, kt_i)))]
        for c in keys_out:
            c.start()
        attend_all(far_half, {
            0: [gu.step_x], 3: [go.step_yz], 7: [go.step_diag], 8: [gd.step_x, gu.step_yz],
        })
        ctx_out = fetch(ctx_t, ctxt, 3)
        ctx_out.start()
        for j in range(nb):
            ctx_v[j * BLK : (j + 1) * BLK, :] = ctx_t[j].T.astype(BF)
        go.near(True)
        go.far()
        for c in keys_out:
            c.wait()
        ctx_out.wait()
        for i in range(groups - 1):
            par(i).wait_send()
            par_from(i).wait_recv()

        @pl.when(h < groups - 1)
        def _():
            both(to_right, gone)

        @pl.when(h > 0)
        def _():
            both(to_left, gone)

    def dense(cot_v, out_v, up_v, down_v, hl, ht, act_t, slope):
        ffn, gup, mix_v, g_low = g_hid, hl, ctx_v, cot_v
        gain1, shift1, gain2, shift2 = (parameter(i) for i in range(4))
        first = [fetch(a, b, i) for i, (a, b) in enumerate(((out_w.at[0], out_v), (cot, cot_v)))]
        for c in first:
            c.start()

        def weights(i, slot):
            if i == shards - 1:
                return fetch(up_own.at[0], up_v.at[slot], 4 + slot), fetch(down_own.at[0], down_v.at[slot], 6 + slot)
            here = pl.ds(pl.multiple_of(shard_of(i) * width, 16), width)
            return fetch(up_w.at[0, here, :], up_v.at[slot], 4 + slot), fetch(down_w.at[0, here, :], down_v.at[slot], 6 + slot)

        def start_weights(i, slot):
            for c in weights(i, slot):
                c.start()

        def wait_weights(i, slot):
            for c in weights(i, slot):
                c.wait()

        start_weights(3, 0)
        gu.near(False)
        gd.near(False)
        start_weights(2, 1)
        vec_acc[...] = jnp.zeros_like(vec_acc)
        for c in first:
            c.wait()

        def before(b, c):
            resid = x_v[rows(b + HALO), :].astype(F32) + nn(ctx_v[rows(b), :], out_v[...])
            cen = resid - mean(resid)
            rs = lax.rsqrt(mean(cen * cen) + NORM_EPS)
            n = cen * rs
            hidden = n * gain1 + shift1
            xhat[rows(b), :] = n
            inv[rows(b), :] = jnp.broadcast_to(rs, (BLK, 128))
            low = hidden.astype(BF)
            hl[rows(b), :] = low
            ht[b] = low.T
            ffn[rows(b), :] = hidden
            return c

        lax.fori_loop(0, nb, before, 0)

        def forward(i, c):
            slot = i % 2
            wait_weights(0, slot)
            for b in range(nb):
                up = nn(hl[rows(b), :], up_v[slot])
                active, deriv = gelu_parts(up)
                active = active.astype(BF)
                slope[i, rows(b), :] = deriv.astype(BF)
                act_t[i, b] = active.T
                ffn[rows(b), :] += nn(active, down_v[slot])
            return c

        def forward_then(i, c):
            forward(i, c)
            hooks_at(i, {
                0: [gu.step_diag, gd.step_yz],
                1: [gd.step_diag, lambda: start_weights(1, 0)],
                2: [gu.far, gd.far, lambda: start_weights(0, 1)],
            })
            return c

        lax.fori_loop(0, shards, forward_then, 0)

        def middle(b, c):
            v = ffn[rows(b), :]
            cen = v - mean(v)
            rs = lax.rsqrt(mean(cen * cen) + NORM_EPS)
            n = cen * rs
            mix_v[rows(b), :] = (n * gain2 + shift2).astype(BF)
            ct = cot_v[rows(b), :].astype(F32)
            vec_acc[2:3, :] += jnp.sum(ct * n, axis=0, keepdims=True)
            vec_acc[3:4, :] += jnp.sum(ct, axis=0, keepdims=True)
            e = ct * gain2
            g = rs * (e - mean(e) - n * mean(e * n))
            g_hid[rows(b), :] = g
            g_low[rows(b), :] = g.astype(BF)
            return c

        lax.fori_loop(0, nb, middle, 0)
        mix_out = fetch(mix_v, mixed, 0)
        mix_out.start()

        def grad_rows(left, right, part, part_i, slot):
            n = part.n
            acc = jnp.zeros((n, width), F32)
            for b in range(nb):
                acc += nn(left(b, pl.ds(part_i * n, n)), right[b * BLK : (b + 1) * BLK, :])
            part.mine[slot] = acc.astype(BF)

        def down_grads(i, c):
            slot = slot_of(i)

            @pl.when(i == 2)
            def _():
                for p in downs:
                    p.core(0).wait_send()

            for k, p in enumerate(downs):
                grad_rows(lambda b, n: act_t[shards - 1 - i, b, n, :], g_low, p, k, slot)
            hooks_at(i, {
                0: [p.c0 for p in downs],
                1: [downs[0].f, downs[0].xs],
                2: [downs[1].f, *(p.c1 for p in downs)],
            })
            return c

        lax.fori_loop(0, shards, down_grads, 0)

        def backward(i, c):
            slot = 1 - i % 2

            @pl.when(i >= 2)
            def _():
                wait_weights(0, slot)

            def one_block(b, cc):
                ga = nt(g_low[rows(b), :], down_v[slot])
                gu = (slope[shards - 1 - i, rows(b), :].astype(F32) * ga).astype(BF)
                gup[rows(b), :] = gu
                g_hid[rows(b), :] += nt(gu, up_v[slot])
                return cc

            lax.fori_loop(0, nb, one_block, 0)

            for back in (0, 1):

                @pl.when(i == back)
                def _():
                    start_weights(back + 2, 1 - back)

            @pl.when(i == 2)
            def _():
                for p in ups:
                    p.core(0).wait_send()

            for k, p in enumerate(ups):
                grad_rows(lambda b, n: ht[b, n, :], gup, p, k, slot_of(i))
            hooks_at(i, {
                0: [p.c0 for p in ups] + [p.s for p in downs],
                1: [p.f for p in ups] + [downs[1].xs],
                2: [p.c1 for p in ups] + [downs[0].r],
                3: [p.s for p in ups],
            })
            return c

        lax.fori_loop(0, shards, backward, 0)
        mix_out.wait()

    pl.run_scoped(
        project,
        pltpu.VMEM((nw, width, BLK), BF),
        pltpu.VMEM((all_pairs, nw * BLK, 128), BF),
        pltpu.VMEM((all_pairs, nw * BLK, 128), BF),
        pltpu.VMEM((nw, width, BLK), BF),
        pltpu.VMEM((nb, row_blocks, BLK, BLK), F32),
        pltpu.VMEM((nb, width, BLK), F32),
    )
    pl.run_scoped(
        dense,
        pltpu.VMEM((own, width), BF),
        pltpu.VMEM((width, width), BF),
        pltpu.VMEM((2, width, width), BF),
        pltpu.VMEM((2, width, width), BF),
        pltpu.VMEM((own, width), BF),
        pltpu.VMEM((nb, width, BLK), BF),
        pltpu.VMEM((shards, nb, width, BLK), BF),
        pltpu.VMEM((shards, own, width), BF),
    )

    def attention(g_v, k_v, v_v, kt_v, delta, bias, dk, dv, dqt, dkt, dvt):
        gain1 = parameter(0)
        def keys(hf):
            base = pl.multiple_of(hf * half, 128)
            return (
                fetch(k_i.at[pl.ds(hf * pairs, pairs)], k_v, 0),
                fetch(v_i.at[pl.ds(hf * pairs, pairs)], v_v, 1),
                fetch(kt_i.at[:, pl.ds(base, half), :], kt_v, 2),
            )

        for c in keys(far_half):
            c.start()

        def between(out_v, ctxt_v):
            low_v = ctx_v
            o_in, c_in = fetch(out_w.at[0], out_v, 6), fetch(ctxt, ctxt_v, 7)
            o_in.start()
            c_in.start()

            def norm_back(b, c):
                g = g_hid[rows(b), :]
                n = xhat[rows(b), :]
                vec_acc[0:1, :] += jnp.sum(g * n, axis=0, keepdims=True)
                vec_acc[1:2, :] += jnp.sum(g, axis=0, keepdims=True)
                e = g * gain1
                res = inv[rows(b), 0:1] * (e - mean(e) - n * mean(e * n))
                g_hid[rows(b), :] = res
                low_v[rows(b), :] = res.astype(BF)
                return c

            lax.fori_loop(0, nb, norm_back, 0)
            o_in.wait()
            c_in.wait()

            def after(b, c):
                low = low_v[rows(b), :]
                gc = nt(low, out_v[...]).astype(BF)
                for i in range(all_pairs):
                    g_v[i, rows(b), :] = gc[:, i * 128 : (i + 1) * 128]
                prod = nt(out_v[...], low).astype(BF).astype(F32) * ctxt_v[b]
                for i in range(2 * all_pairs):
                    delta[b, i] = jnp.sum(prod[i * HEAD_WIDTH : (i + 1) * HEAD_WIDTH, :], axis=0, keepdims=True)
                return c

            lax.fori_loop(0, nb, after, 0)
            vstep(0).start()
            ups[0].xs()

            def grad_out(i, c):
                @pl.when(i == 2)
                def _():
                    out_c.core(0).wait_send()

                base = pl.multiple_of(shard_of(i) * shard_rows, 16)
                acc = jnp.zeros((shard_rows, width), F32)
                for b in range(nb):
                    acc += nn(ctxt_v[b, pl.ds(base, shard_rows), :].astype(BF), low_v[b * BLK : (b + 1) * BLK, :])
                out_c.mine[slot_of(i)] = acc.astype(BF)
                hooks_at(i, {0: [out_c.c0], 2: [out_c.c1]})
                return c

            lax.fori_loop(0, shards, grad_out, 0)
            downs[0].yy()
            downs[1].r()
            out_c.f()

        pl.run_scoped(
            between,
            pltpu.VMEM((width, width), BF),
            pltpu.VMEM((nb, width, BLK), F32),
        )
        def unit(hf, t):
            j, i = t // pairs, t % pairs
            p = hf * pairs + i
            ws = window_start(h, j, nb, row_blocks)

            @pl.when(i == 0)
            def _():
                for kb in range(row_blocks):
                    bias[kb * BLK : (kb + 1) * BLK, :] = mask_of(seg[ws + kb], seg[HALO + j])

            q = q_v[p, rows(j), :]
            g = g_v[p, rows(j), :]
            lane = lax.broadcasted_iota(jnp.int32, q.shape, 1)
            qm = [jnp.where(lane // HEAD_WIDTH == hh, q, jnp.zeros_like(q)) for hh in range(2)]
            gm = [jnp.where(lane // HEAD_WIDTH == hh, g, jnp.zeros_like(g)) for hh in range(2)]
            window = pl.ds(pl.multiple_of(ws * BLK, BLK), row_blocks * BLK)
            scores = nt(k_v[i, window, :], jnp.concatenate(qm, axis=0))
            g_probs = nt(v_v[i, window, :], jnp.concatenate(gm, axis=0))
            probs, g_scores = [], []
            for hh in range(2):
                cols = slice(hh * BLK, (hh + 1) * BLK)
                prob = jnp.exp(scores[:, cols] + bias[...] - lse[j, 2 * p + hh])
                g_scores.append((prob * (g_probs[:, cols] - delta[j, 2 * p + hh])).astype(BF))
                probs.append(prob.astype(BF))
            dv[i, window, :] += nn(probs[0], gm[0]) + nn(probs[1], gm[1])
            dk[i, window, :] += nn(g_scores[0], qm[0]) + nn(g_scores[1], qm[1])
            for hh in range(2):
                at = pl.ds(pl.multiple_of((2 * i + hh) * HEAD_WIDTH, HEAD_WIDTH), HEAD_WIDTH)
                acc = jnp.zeros((HEAD_WIDTH, BLK), F32)
                for kb in range(row_blocks):
                    acc += nn(kt_v[ws + kb, at, :], g_scores[hh][kb * BLK : (kb + 1) * BLK, :])
                dqt[j, at, :] = (acc * HEAD_WIDTH**-0.5).astype(BF)

        def attend_half(hf, plan, then):
            dk[...] = jnp.zeros_like(dk)
            dv[...] = jnp.zeros_like(dv)

            def body(t, c):
                hooks_at(t, plan)
                unit(hf, t)
                return c

            lax.fori_loop(0, nb * pairs, body, 0)
            for step in then:
                step()
            for b in range(nw):
                lo, hi = b * BLK, (b + 1) * BLK
                dkt[b] = jnp.concatenate([dk[p, lo:hi, :].astype(BF) for p in range(pairs)], axis=1).T
                dvt[b] = jnp.concatenate([dv[p, lo:hi, :].astype(BF) for p in range(pairs)], axis=1).T

        def weight_grads(which, slot, then):
            at = pl.multiple_of(which * shard_rows, 16)
            for c, src, blocks in ((q_c, dqt, range(HALO, HALO + nb)), (k_c, dkt, range(nw)), (v_c, dvt, range(nw))):
                acc = jnp.zeros((shard_rows, width), F32)
                for b in blocks:
                    acc += nn(src[b - blocks[0], pl.ds(at, shard_rows), :], x_v[b * BLK : (b + 1) * BLK, :])
                c.mine[slot] = acc.astype(BF)
                then(c)

        def input_grads(hf, last):
            base = pl.multiple_of(hf * half, 128)
            wk, wv = w_v.at[1, pl.ds(base, half), :], w_v.at[2, pl.ds(base, half), :]

            def block(b):
                kb = jnp.concatenate([dk[p, rows(b), :].astype(BF) for p in range(pairs)], axis=1)
                vb = jnp.concatenate([dv[p, rows(b), :].astype(BF) for p in range(pairs)], axis=1)
                return nn(kb, wk[...]) + nn(vb, wv[...])

            def side(i, c):
                b = i + jnp.where(i >= HALO, nb, 0)
                total = block(b)
                if last:
                    total = total + gx_side[rows(i), :].astype(F32)
                gx_side[rows(i), :] = total.astype(BF)
                return c

            lax.fori_loop(0, 2 * HALO, side, 0)

            def inner(j, c):
                g_hid[rows(j), :] += block(j + HALO) + nn(dqt[j].T, w_v[0, pl.ds(base, half), :])
                return c

            return lambda: lax.fori_loop(0, nb, inner, 0)

        for c in keys(far_half):
            c.wait()
        d0, d1 = downs
        u0, u1 = ups
        vs = [functools.partial(vnext, i) for i in range(len(vec_ids))]
        vs = [functools.partial(vnext, i) for i in range(len(vec_ids))]
        attend_half(far_half, {
            1: [vs[0], out_c.s], 3: [d0.zz], 5: [u1.xs], 6: [d1.yy], 7: [u0.r], 8: [d0.w],
        }, [d1.zz])
        for c in keys(x_half):
            c.start()
        weight_grads(1 - core, 0, lambda p: p.c0())
        out_c.xs()
        weight_grads(core, 1, lambda p: (p.f(), p.xs()))
        u0.yy()
        d0.u()
        input_grads(far_half, False)()
        u1.r()
        for c in keys(x_half):
            c.wait()
        attend_half(x_half, {
            1: [u0.zz, d1.w], 3: [out_c.r, vs[1]], 5: [u1.yy], 6: [u0.w], 7: [d0.end, d1.u], 8: [u1.zz, out_c.yy],
        }, [])
        for p in (q_c, k_c, v_c):
            p.core(0).wait_send()
        weight_grads(1 - core, 0, lambda p: p.c1())
        u0.u()
        out_c.zz()
        vs[2]()
        weight_grads(core, 2, lambda p: None)
        for p in (q_c, k_c, v_c):
            p.s()
            p.r()
        u1.w()
        finish = input_grads(x_half, True)

        @pl.when(h > 0)
        def _():
            to_left.start()

        @pl.when(h < groups - 1)
        def _():
            to_right.start()

        finish()
        q_c.yy()
        k_c.yy()
        out_c.w()
        q_c.zz()
        v_c.yy()
        k_c.zz()
        u1.u()
        v_c.zz()
        q_c.w()
        vs[3]()
        out_c.u()
        k_c.w()
        v_c.w()
        q_c.u()
        from_right, from_left = pl.ds(halo + own, halo), pl.ds(0, halo)

        @pl.when(h < groups - 1)
        def _():
            to_left.wait_recv()
            fetch(o_left, x_v.at[from_right, :], 0).start()

        @pl.when(h > 0)
        def _():
            to_right.wait_recv()
            fetch(o_right, x_v.at[from_left, :], 1).start()

        k_c.u()
        v_c.u()
        d1.end()
        u0.end()
        u1.end()
        out_c.end()
        for step in vs[4:]:
            step()

        @pl.when(h < groups - 1)
        def _():
            fetch(o_left, x_v.at[from_right, :], 0).wait()
            g_hid[own - halo :, :] += x_v[from_right, :].astype(F32)

        @pl.when(h > 0)
        def _():
            fetch(o_right, x_v.at[from_left, :], 1).wait()
            g_hid[:halo, :] += x_v[from_left, :].astype(F32)

        tok_out = fetch(g_hid, o_tok, 3)
        tok_out.start()
        for p in (q_c, k_c, v_c):
            p.end()
        tok_out.wait()

    to_left = remote(gx_side.at[pl.ds(0, halo), :], o_left, side_send.at[0], side_recv.at[0], (r, h - 1))
    to_right = remote(gx_side.at[pl.ds(halo, halo), :], o_right, side_send.at[1], side_recv.at[1], (r, h + 1))

    pl.run_scoped(
        attention,
        pltpu.VMEM((all_pairs, own, 128), BF),
        pltpu.VMEM((pairs, nw * BLK, 128), BF),
        pltpu.VMEM((pairs, nw * BLK, 128), BF),
        pltpu.VMEM((nw, half, BLK), BF),
        pltpu.VMEM((nb, 2 * all_pairs, 1, BLK), F32),
        pltpu.VMEM((row_blocks * BLK, BLK), F32),
        pltpu.VMEM((pairs, nw * BLK, 128), F32),
        pltpu.VMEM((pairs, nw * BLK, 128), F32),
        pltpu.VMEM((nb, half, BLK), BF),
        pltpu.VMEM((nw, half, BLK), BF),
        pltpu.VMEM((nw, half, BLK), BF),
    )

    o_vec[...] = vacc[len(vec_ids) - 1]
    for g in (gq, go, gu, gd):
        g.sent()
    for p in parts:
        p.done()
    for i in range(len(vec_ids)):
        vstep(i).wait_send()

    @pl.when(h > 0)
    def _():
        to_left.wait_send()

    @pl.when(h < groups - 1)
    def _():
        to_right.wait_send()


def layer(groups, row_blocks, row_devices, tok, cot, qkv_own, out_own, up_own, down_own, vec_own, lengths):
    own, width = tok.shape
    shard_rows = width // groups
    nb = own // BLK
    nw = nb + 2 * HALO
    all_pairs = width // 128
    bits = other_bits(row_devices)
    split = width // 2
    chunks = [(name, lo, split) for name in ("down", "up") for lo in range(0, width, split)]
    chunks += [(name, 0, shard_rows) for name in ("out", "q", "k", "v")]
    hops = 4 + len(bits)
    scratch = [
        pltpu.VMEM((3, width, width), BF),
        pltpu.VMEM((nw * BLK, width), BF),
        pltpu.VMEM((all_pairs, own, 128), BF),
        pltpu.VMEM((own, width), BF),
        pltpu.VMEM((nb, 2 * all_pairs, 1, BLK), F32),
        pltpu.VMEM((nw, 1, BLK), F32),
        pltpu.VMEM((groups,) + vec_own.shape, BF),
        pltpu.VMEM((own, width), F32),
        pltpu.VMEM((own, 128), F32),
        pltpu.VMEM((own, width), F32),
        pltpu.VMEM((2 * HALO * BLK, width), BF),
        pltpu.VMEM((8, width), F32),
        pltpu.VMEM((hops, 8, width), F32),
        pltpu.VMEM((hops, 8, width), F32),
    ]
    for _, _, n in chunks:
        scratch += [
            pltpu.VMEM((3, n, width), BF),
            pltpu.VMEM((2, n, width), BF),
            pltpu.VMEM((n, width), BF),
            pltpu.VMEM((n // 2, width), BF),
            pltpu.VMEM((n // 4, width), BF),
            pltpu.VMEM((max(1, len(bits)), n // 4, width), BF),
        ]
    dma = pltpu.SemaphoreType.DMA
    scratch += [dma((len(chunks), 8 + len(bits)))] * 2 + [dma((len(chunks), 3))] + [dma((4, 12))] * 2
    scratch += [dma((2 * HALO,))] * 2 + [dma((2,))] * 2 + [dma((groups - 1,))] * 2 + [dma((hops,))] * 2 + [dma((8,))]
    s = jax.ShapeDtypeStruct
    side = s((HALO * BLK, width), BF)
    outs = [
        (s((own, width), BF), ANY),
        (s((width, width), BF), ANY),
        (s((width, width), BF), ANY),
        (s((shard_rows, width), BF), ANY),
        (s((3, shard_rows, width), BF), ANY),
        (s((own, width), F32), ANY),
        (side, ANY),
        (side, ANY),
        (s((8, width), F32), VM),
        (s((1, width, width), BF), ANY),
        (s((1, groups * width, width), BF), ANY),
        (s((1, groups * width, width), BF), ANY),
        (s((nb, width, BLK), F32), ANY),
        (s((all_pairs, nw * BLK, 128), BF), ANY),
        (s((all_pairs, nw * BLK, 128), BF), ANY),
        (s((nw, width, BLK), BF), ANY),
    ]
    return pl.pallas_call(
        functools.partial(layer_kernel, groups, row_blocks, bits, chunks),
        out_shape=[o[0] for o in outs],
        in_specs=[ANY] * 6 + [VM] * 2,
        out_specs=[o[1] for o in outs],
        scratch_shapes=scratch,
        compiler_params=pltpu.CompilerParams(collective_id=0, has_side_effects=True, vmem_limit_bytes=VMEM_LIMIT),
        name="layer",
    )(tok, cot, qkv_own, out_own, up_own, down_own, vec_own, lengths)


def local(
    groups, row_devices,
    tokens, lengths, w_query, w_key, w_value, w_out, w_up, w_down,
    gain_first, shift_first, gain_second, shift_second, cotangent,
):
    packed_rows = lengths.shape[0]
    own, width = tokens.shape
    row_length = groups * own // packed_rows
    row_blocks = row_length // BLK
    h = lax.axis_index("heads")
    n_vec = gain_first.shape[0]
    vec_own = jnp.concatenate([gain_first, shift_first, gain_second, shift_second])
    vec_own = jnp.broadcast_to(vec_own[None, :], (16, width))
    qkv_own = jnp.stack([w_query.T, w_key.T, w_value.T])
    mixed, o_down, o_up, o_out, o_qkv, o_tok, _, _, o_vec = layer(
        groups, row_blocks, row_devices, tokens, cotangent, qkv_own, w_out[None], w_up[None], w_down[None], vec_own, lengths
    )[:9]
    mine = lax.dynamic_slice(o_vec, (0, n_vec * h), (4, n_vec))
    wide = lambda a: a.astype(F32)
    return (
        mixed, o_tok, wide(o_qkv[0].T), wide(o_qkv[1].T), wide(o_qkv[2].T), wide(o_out), wide(o_up), wide(o_down),
        mine[0], mine[1], mine[2], mine[3],
    )


def solution(mesh):
    both, heads = P(("rows", "heads"), None), P("heads")
    cols, rows = P(None, "heads"), P("heads", None)
    return jax.shard_map(
        functools.partial(local, mesh.shape["heads"], mesh.shape["rows"]),
        mesh=mesh,
        in_specs=(both, P("rows", None), cols, cols, cols, rows, cols, rows, heads, heads, heads, heads, both),
        out_specs=(both, both, cols, cols, cols, rows, cols, rows, heads, heads, heads, heads),
        check_vma=False,
    )
```

```python
import functools

import jax
import jax.numpy as jnp
from jax import lax
from jax.experimental import pallas as pl
from jax.experimental.pallas import tpu as pltpu
from jax.sharding import PartitionSpec as P

MESH = pl.DeviceIdType.MESH
BF = jnp.bfloat16
F32 = jnp.float32
HEAD_WIDTH = 64
LONGEST_DOC = 512
BLK = 256
HALO = LONGEST_DOC // BLK
NORM_EPS = 1e-12
VMEM_LIMIT = 62 * 1024 * 1024


def nt(left, right):
    return lax.dot_general(left, right, (((1,), (1,)), ((), ())), preferred_element_type=F32)


def nn(left, right):
    return lax.dot_general(left, right, (((1,), (0,)), ((), ())), preferred_element_type=F32)


def flip(index, bit):
    return index + bit - 2 * bit * ((index // bit) % 2)


def place():
    r, h = lax.axis_index("rows"), lax.axis_index("heads")
    return r, h


def greet(ids):
    barrier = pltpu.get_barrier_semaphore()
    for who in ids:
        pl.semaphore_signal(barrier, inc=1, device_id=who, device_id_type=MESH)
    pl.semaphore_wait(barrier, len(ids))


def group_of(r, h, groups):
    return [(r, lax.rem(h + i, groups)) for i in range(1, groups)]


def remote(src, dst, send, recv, who):
    return pltpu.make_async_remote_copy(
        src_ref=src, dst_ref=dst, send_sem=send, recv_sem=recv, device_id=who, device_id_type=MESH
    )


class Gather:
    def __init__(self, own, full, sems, at):
        self.own, self.full, self.sems, self.at = own, full, sems, at
        self.n = own.shape[1]
        self.u = self.n // 12
        r, h = place()
        self.r, self.h = r, h
        y, z = r % 2, (r // 2) % 2
        self.k = 2 * z + y
        self.ky = 2 * z + 1 - y
        self.kz = 2 * (1 - z) + y
        self.kd = 3 - self.k
        self.hx = flip(h, 2)
        self.hc = flip(h, 1)
        self.by_x = (r, self.hx)
        self.by_c = (r, self.hc)
        self.by_y = (flip(r, 1), h)
        self.by_z = (flip(r, 2), h)

    def rows(self, shard, sub, count):
        u = self.u
        return pl.ds(pl.multiple_of(shard * self.n + sub * u, 16), count * u)

    def part(self, slot, who, shard, sub, count, own=False):
        dst = self.full.at[:, self.rows(shard, sub, count), :]
        src = self.own.at[:, self.rows(0, sub, count), :] if own else dst
        send, recv = self.sems
        return remote(src, dst, send.at[self.at, slot], recv.at[self.at, slot], who)

    def x_main(self):
        return self.part(0, self.by_x, self.h, 3 * self.k, 3, own=True)

    def x_diag(self):
        return self.part(1, self.by_x, self.h, 3 * self.kd, 1, own=True)

    def y_main(self):
        return self.part(2, self.by_y, self.hx, 3 * self.k, 3)

    def z_main(self):
        return self.part(3, self.by_z, self.hx, 3 * self.k, 3)

    def y_diag(self):
        return self.part(4, self.by_y, self.hx, 3 * self.kz + 1, 1)

    def z_diag(self):
        return self.part(5, self.by_z, self.hx, 3 * self.ky + 2, 1)

    def c_own(self):
        return self.part(6, self.by_c, self.h, 0, 12, own=True)

    def c_part(self, i):
        return self.part(7 + i, self.by_c, self.hx, 3 * (self.k, self.ky, self.kz, self.kd)[i], 3)

    def local(self):
        send, _ = self.sems
        return pltpu.make_async_copy(
            self.own, self.full.at[:, self.rows(self.h, 0, 12), :], send.at[self.at, 11]
        )

    def start_x(self):
        self.x_main().start()
        self.x_diag().start()

    def start_main(self):
        self.x_main().start()

    def start_diag(self):
        self.x_diag().start()

    def start_c(self, keep):
        self.c_own().start()
        if keep:
            self.local().start()

    def step_x(self):
        self.x_main().wait_recv()
        self.y_main().start()
        self.z_main().start()
        self.c_part(0).start()

    def step_yz(self):
        self.y_main().wait_recv()
        self.z_diag().start()
        self.c_part(1).start()
        self.z_main().wait_recv()
        self.y_diag().start()
        self.c_part(2).start()

    def step_diag(self):
        self.x_diag().wait_recv()
        self.y_diag().wait_recv()
        self.z_diag().wait_recv()
        self.c_part(3).start()

    def near(self, keep):
        self.c_own().wait_recv()
        if keep:
            self.local().wait()

    def far(self):
        for i in range(4):
            self.c_part(i).wait_recv()

    def sent(self):
        for copy in (self.x_main(), self.x_diag(), self.y_main(), self.z_main(), self.y_diag(), self.z_diag(), self.c_own()):
            copy.wait_send()
        for i in range(4):
            self.c_part(i).wait_send()


def window_start(h, j, own_blocks, row_blocks):
    g = own_blocks * h + j
    first = own_blocks * h - HALO
    row = row_blocks * (g // row_blocks)
    return jnp.clip(row, first, first + own_blocks + 2 * HALO - row_blocks) - first


def mask_of(keys, queries):
    down = jnp.broadcast_to(keys, (8, BLK)).T[:, 0:1]
    return jnp.where(down == queries, 0.0, -1e30).astype(F32)


ANY = pl.BlockSpec(memory_space=pl.ANY)
VM = pl.BlockSpec(memory_space=pltpu.VMEM)


def gelu_parts(u):
    bell = jnp.exp(-0.5 * u * u)
    base = 1.0 + (0.3275911 * 0.7071067811865476) * jnp.abs(u)
    t = pl.reciprocal(base, approx=True)
    t = t * (2.0 - base * t)
    poly = t * (0.127414796 + t * (-0.142248368 + t * (0.7107068705 + t * (-0.7265760135 + t * 0.5307027145))))
    tail = poly * bell
    cdf = jnp.where(u >= 0.0, 1.0 - tail, tail)
    return u * cdf, cdf + u * (bell * 0.3989422804014327)


class Sum:
    def __init__(self, n, bits, bufs, sems, at, turned):
        self.n, self.bits, self.at = n, bits, at
        self.mine, self.rc, self.rx, self.ry, self.rz, self.rest = bufs
        self.send, self.recv, self.keep = sems
        r, h = place()
        self.y, self.z = r % 2, (r // 2) % 2
        self.by_x, self.by_c = (r, flip(h, 2)), (r, flip(h, 1))
        self.by_y, self.by_z = (flip(r, 1), h), (flip(r, 2), h)
        if turned:
            self.y, self.z, self.by_y, self.by_z = self.z, self.y, self.by_z, self.by_y
        self.by_rest = [(flip(r, b), h) for b in bits]

    def copy(self, slot, src, dst, who):
        return remote(src, dst, self.send.at[self.at, slot], self.recv.at[self.at, slot], who)

    def core(self, i):
        return self.copy(i, self.mine.at[0], self.rc.at[i], self.by_c)

    def x(self):
        return self.copy(2, self.mine.at[1], self.rx, self.by_x)

    def half(self, which):
        return pl.ds(pl.multiple_of(which * (self.n // 2), 16), self.n // 2)

    def quarter(self, half, which):
        return pl.ds(pl.multiple_of(half * (self.n // 2) + which * (self.n // 4), 16), self.n // 4)

    def own(self):
        return self.mine.at[2, self.quarter(self.y, self.z), :]

    def landed(self, half, which):
        return self.rx.at[self.quarter(half, which), :]

    def y_down(self):
        return self.copy(3, self.mine.at[2, self.half(1 - self.y), :], self.ry, self.by_y)

    def z_down(self):
        return self.copy(4, self.mine.at[2, self.quarter(self.y, 1 - self.z), :], self.rz, self.by_z)

    def z_up(self):
        return self.copy(5, self.own(), self.landed(self.y, self.z), self.by_z)

    def y_up(self):
        return self.copy(6, self.own(), self.landed(self.y, self.z), self.by_y)

    def y_up2(self):
        return self.copy(7, self.landed(self.y, 1 - self.z), self.landed(self.y, 1 - self.z), self.by_y)

    def swap(self, i):
        return self.copy(8 + i, self.own(), self.rest.at[i], self.by_rest[i])

    def add(self, ref, got):
        step = self.n // 4

        def some(i, c):
            at = pl.ds(pl.multiple_of(i * step, 16), step)
            ref[at, :] = (ref[at, :].astype(F32) + got[at, :].astype(F32)).astype(BF)
            return c

        lax.fori_loop(0, ref.shape[0] // step, some, 0)

    def c0(self):
        self.core(0).start()

    def f(self):
        self.core(0).wait_recv()
        self.add(self.mine.at[1], self.rc.at[0])

    def xs(self):
        self.x().start()

    def c1(self):
        self.core(1).start()

    def s(self):
        self.core(1).wait_recv()
        self.add(self.mine.at[2], self.rc.at[1])

    def r(self):
        self.x().wait_recv()
        self.add(self.mine.at[2], self.rx)
        self.y_down().start()

    def yy(self):
        self.y_down().wait_recv()
        self.add(self.mine.at[2, self.half(self.y), :], self.ry)
        self.z_down().start()

    def zz(self):
        self.z_down().wait_recv()
        self.add(self.own(), self.rz)
        if self.bits:
            self.swap(0).start()

    def w(self):
        for i in range(len(self.bits)):
            self.swap(i).wait_recv()
            self.swap(i).wait_send()
            self.add(self.own(), self.rest.at[i])
            if i + 1 < len(self.bits):
                self.swap(i + 1).start()
        self.z_up().start()
        self.y_up().start()

    def u(self):
        self.z_up().wait_recv()
        self.y_up2().start()

    def outs(self, out, lo):
        def local(i, src, rows):
            start = pl.multiple_of(lo + rows.start, 16)
            return pltpu.make_async_copy(src, out.at[pl.ds(start, rows.size), :], self.keep.at[self.at, i])

        mine, beside, other = self.quarter(self.y, self.z), self.quarter(self.y, 1 - self.z), self.half(1 - self.y)
        return (
            local(0, self.own(), mine),
            local(1, self.rx.at[beside, :], beside),
            local(2, self.rx.at[other, :], other),
        )

    def e(self, out, lo):
        self.y_up().wait_recv()
        self.y_up2().wait_recv()
        for c in self.outs(out, lo):
            c.start()

    def sent(self, out, lo):
        for c in (self.core(1), self.x(), self.y_down(), self.z_down(), self.z_up(), self.y_up(), self.y_up2()):
            c.wait_send()
        for c in self.outs(out, lo):
            c.wait()


def other_bits(count):
    bits, b = [], 4
    while b < count:
        bits.append(b)
        b *= 2
    return tuple(bits)


def hooks_at(t, plan):
    for at, steps in plan.items():

        @pl.when(t == at)
        def _():
            for step in steps:
                step()


def layer_kernel(
    groups, row_blocks, bits, chunks,
    tok, cot, qkv_own, out_own, up_own, down_own, vec_own, lengths,
    mixed, o_down, o_up, o_out, o_qkv, o_tok, o_left, o_right, o_vec,
    out_w, up_w, down_w, ctxt, k_i, v_i, kt_i,
    w_v, x_v, q_v, ctx_v, lse, seg, vec_all, xhat, inv, g_hid, gx_side, vec_acc, vin, vacc, *scratch,
):
    r, h = place()
    own, width = tok.shape
    nb = own // BLK
    nw = nb + 2 * HALO
    halo = HALO * BLK
    shards = groups
    all_pairs = q_v.shape[0]
    pairs = all_pairs // 2
    half = pairs * 128
    shard_rows = half // 2
    x_half = (h // 2) % 2
    far_half = 1 - x_half
    core = h % 2
    rows = lambda b: pl.ds(pl.multiple_of(b * BLK, BLK), BLK)
    mean = lambda v: jnp.mean(v, axis=1, keepdims=True)
    n_chunks = len(chunks)
    (send, recv, keep, gsend, grecv, in_send, in_recv, side_send, side_recv, psend, precv, vsend, vrecv, loc) = scratch[6 * n_chunks :]
    sems = (send, recv, keep)
    turned = (1, 3, 6)
    outs = {"down": o_down, "up": o_up, "out": o_out, "q": o_qkv.at[0], "k": o_qkv.at[1], "v": o_qkv.at[2]}
    parts = [Sum(n, bits, scratch[6 * i : 6 * i + 6], sems, i, i in turned) for i, (_, _, n) in enumerate(chunks)]
    by_name = {}
    for part, (name, lo, _) in zip(parts, chunks):
        part.end = functools.partial(part.e, outs[name], lo)
        part.done = functools.partial(part.sent, outs[name], lo)
        by_name.setdefault(name, []).append(part)
    downs, ups, (out_c,) = by_name["down"], by_name["up"], by_name["out"]
    q_c, k_c, v_c = (by_name[name][0] for name in "qkv")
    one = parts[0]
    gq = Gather(qkv_own, w_v, (gsend, grecv), 0)
    go = Gather(out_own, out_w, (gsend, grecv), 1)
    gu = Gather(up_own, up_w, (gsend, grecv), 2)
    gd = Gather(down_own, down_w, (gsend, grecv), 3)

    def shard_of(i):
        across = 1 - i // 2
        other = 1 - i % 2
        return h + across * (2 - 4 * x_half) + other * (1 - 2 * core)

    def slot_of(i):
        return (i % 2) * (1 + i // 2)

    def fetch(src, dst, i):
        return pltpu.make_async_copy(src, dst, loc.at[i])

    vec_ids = [one.by_c, one.by_x, one.by_y, one.by_z] + one.by_rest

    def vstep(i):
        src = vec_acc if i == 0 else vacc.at[i - 1]
        return remote(src, vin.at[i], vsend.at[i], vrecv.at[i], vec_ids[i])

    def vnext(i):
        vstep(i).wait_recv()
        vacc[i] = (vec_acc[...] if i == 0 else vacc[i - 1]) + vin[i]
        if i + 1 < len(vec_ids):
            vstep(i + 1).start()

    def parameter(i):
        n = width // groups
        return jnp.concatenate([vec_all[s].astype(F32)[0:1, i * n : (i + 1) * n] for s in range(groups)], axis=1)

    def project(vt, k_s, v_s, kt_s, bias, ctx_t):
        total_blocks = groups * nb
        def to_right(i):
            src, dst = pl.ds(own - halo + i * BLK, BLK), pl.ds(i * BLK, BLK)
            return remote(tok.at[src, :], x_v.at[dst, :], in_send.at[i], in_recv.at[i], (r, h + 1))

        def to_left(i):
            src, dst = pl.ds(i * BLK, BLK), pl.ds(halo + own + i * BLK, BLK)
            return remote(tok.at[src, :], x_v.at[dst, :], in_send.at[HALO + i], in_recv.at[HALO + i], (r, h - 1))

        def both(to, step):
            for i in range(HALO):
                step(to(i))

        start, arrived, gone = (lambda c: c.start()), (lambda c: c.wait_recv()), (lambda c: c.wait_send())
        even = h % 2 == 0
        slow_right = jnp.logical_and(h % 2 == 1, h < groups - 1)
        slow_left = jnp.logical_and(even, h > 0)

        odd = h % 2 == 1

        def par(i):
            who = (r, lax.rem(h + 1 + i, groups))
            return remote(vec_own, vec_all.at[h], psend.at[i], precv.at[groups - 2 - i], who)

        def par_from(i):
            return remote(vec_own, vec_all.at[h], psend.at[i], precv.at[i], (r, lax.rem(h + 1 + i, groups)))

        mine = fetch(tok, x_v.at[pl.ds(halo, own), :], 0)
        mine.start()
        greet(group_of(r, h, groups) + [one.by_y, one.by_z] + one.by_rest)

        @pl.when(slow_right)
        def _():
            to_right(HALO - 1).start()

        @pl.when(slow_left)
        def _():
            to_left(0).start()

        @pl.when(even)
        def _():
            both(to_right, start)

        @pl.when(odd)
        def _():
            both(to_left, start)

        gq.start_c(True)
        gq.start_x()
        for i in range(groups - 1):
            par(i).start()
        vec_all[h] = vec_own[...]

        @pl.when(h == 0)
        def _():
            x_v[pl.ds(0, halo), :] = jnp.zeros((halo, width), BF)

        @pl.when(h == groups - 1)
        def _():
            x_v[pl.ds(halo + own, halo), :] = jnp.zeros((halo, width), BF)

        packed, docs = lengths.shape
        down = lax.broadcasted_iota(jnp.int32, (docs, docs), 0)
        across = lax.broadcasted_iota(jnp.int32, (docs, docs), 1)
        for b in range(nw):
            g = nb * h - HALO + b
            row = jnp.clip(g // row_blocks, 0, packed - 1)
            sizes = lengths[pl.ds(row, 1), :].astype(F32)
            ends = jnp.sum(jnp.where(across <= down, jnp.broadcast_to(sizes, (docs, docs)), 0.0), axis=1, keepdims=True)
            at = (lax.broadcasted_iota(jnp.int32, (docs, BLK), 1) + (g % row_blocks) * BLK).astype(F32)
            ids = jnp.sum(jnp.where(at >= ends, 1.0, 0.0), axis=0, keepdims=True) + (row * docs).astype(F32)
            inside = jnp.logical_and(g >= 0, g < total_blocks)
            seg[b] = jnp.where(inside, ids, -1.0)
        for j in range(nb):
            ws = window_start(h, j, nb, row_blocks)
            for kb in range(row_blocks):
                bias[j, kb] = mask_of(seg[ws + kb], seg[HALO + j])

        def project_keys(hx, b):
            base = pl.multiple_of(hx * half, 128)
            xb = x_v[rows(b), :]
            wk = w_v[1, pl.ds(base, half), :]
            wv = w_v[2, pl.ds(base, half), :]
            key = nt(xb, wk).astype(BF)
            value = nt(xb, wv).astype(BF)
            for i in range(pairs):
                k_s[hx * pairs + i, rows(b), :] = key[:, i * 128 : (i + 1) * 128]
                v_s[hx * pairs + i, rows(b), :] = value[:, i * 128 : (i + 1) * 128]
            kt_s[b, pl.ds(base, half), :] = nt(wk, xb).astype(BF)
            vt[b, pl.ds(base, half), :] = nt(wv, xb).astype(BF)

        def project_query(hx, b):
            base = pl.multiple_of(hx * half, 128)
            xb = x_v[rows(b + HALO), :]
            query = nt(xb, w_v[0, pl.ds(base, half), :]).astype(BF) * BF(HEAD_WIDTH**-0.5)
            for i in range(pairs):
                q_v[hx * pairs + i, rows(b), :] = query[:, i * 128 : (i + 1) * 128]

        def side_keys(hx, first):
            def body(b, c):
                project_keys(hx, first + b)
                return c

            lax.fori_loop(0, HALO, body, 0)

        def attend(hx, t):
            j = jnp.where(odd, t // pairs, nb - 1 - t // pairs)
            p = hx * pairs + t % pairs
            ws = window_start(h, j, nb, row_blocks)
            q = q_v[p, rows(j), :]
            lane = lax.broadcasted_iota(jnp.int32, q.shape, 1)
            q_both = jnp.concatenate([jnp.where(lane // HEAD_WIDTH == hh, q, jnp.zeros_like(q)) for hh in range(2)], axis=0)
            scores, tops = [[], []], [None, None]
            for kb in range(row_blocks):
                both_s = nt(k_s[p, rows(ws + kb), :], q_both)
                for hh in range(2):
                    s = both_s[:, hh * BLK : (hh + 1) * BLK] + bias[j, kb]
                    m = jnp.max(s.reshape(BLK // 8, 8, BLK), axis=0)
                    tops[hh] = m if kb == 0 else jnp.maximum(tops[hh], m)
                    scores[hh].append(s)
            tops = [jnp.max(m, axis=0, keepdims=True) for m in tops]
            totals = [jnp.zeros((8, BLK), F32) for _ in range(2)]
            accs = [jnp.zeros((HEAD_WIDTH, BLK), F32) for _ in range(2)]
            at = [pl.ds(pl.multiple_of((2 * p + hh) * HEAD_WIDTH, HEAD_WIDTH), HEAD_WIDTH) for hh in range(2)]
            for kb in range(row_blocks):
                for hh in range(2):
                    e = jnp.exp(scores[hh][kb] - tops[hh])
                    totals[hh] = totals[hh] + jnp.sum(e.reshape(BLK // 8, 8, BLK), axis=0)
                    accs[hh] = accs[hh] + nn(vt[ws + kb, at[hh], :], e.astype(BF))
            for hh in range(2):
                total = jnp.sum(totals[hh], axis=0, keepdims=True)
                ctx_t[j, at[hh], :] = accs[hh] / total
                lse[j, 2 * p + hh] = tops[hh] + jnp.log(total)

        def attend_all(hx, plan):
            def body(t, c):
                hooks_at(t, plan)
                attend(hx, t)
                return c

            lax.fori_loop(0, nb * pairs, body, 0)

        def slow_block(near):
            @pl.when(slow_right)
            def _():
                to_left(0 if near else 1).wait_recv()

            @pl.when(slow_left)
            def _():
                to_right(1 if near else 0).wait_recv()

            project_keys(x_half, jnp.where(odd, HALO + nb + (0 if near else 1), 1 if near else 0))

        def more_halo():
            @pl.when(slow_right)
            def _():
                to_right(0).start()

            @pl.when(slow_left)
            def _():
                to_left(1).start()

        mine.wait()
        gq.near(True)
        lax.fori_loop(0, nb, lambda b, c: (project_query(x_half, b), c)[1], 0)
        lax.fori_loop(HALO, HALO + nb, lambda b, c: (project_keys(x_half, b), c)[1], 0)

        @pl.when(odd)
        def _():
            both(to_right, arrived)

        @pl.when(even)
        def _():
            both(to_left, arrived)

        side_keys(x_half, jnp.where(odd, 0, HALO + nb))
        last = jnp.where(odd, nw - 1, 0)
        for i in range(all_pairs):
            k_s[i, rows(last), :] = jnp.zeros((BLK, 128), BF)
        vt[last] = jnp.zeros((width, BLK), BF)
        attend_all(x_half, {
            0: [lambda: go.start_c(True), lambda: gu.start_c(False)],
            2: [more_halo], 3: [gq.step_x, functools.partial(slow_block, True), lambda: gd.start_c(False)],
            6: [functools.partial(slow_block, False), go.start_x, gu.start_x], 7: [gq.step_yz],
        })
        gd.start_x()
        gq.step_diag()
        go.step_x()
        gq.far()
        lax.fori_loop(0, nb, lambda b, c: (project_query(far_half, b), c)[1], 0)
        lax.fori_loop(0, nw, lambda b, c: (project_keys(far_half, b), c)[1], 0)
        keys_out = [fetch(a, b, i) for i, (a, b) in enumerate(((k_s, k_i), (v_s, v_i), (kt_s, kt_i)))]
        for c in keys_out:
            c.start()
        attend_all(far_half, {
            0: [gu.step_x], 3: [go.step_yz], 7: [go.step_diag], 8: [gd.step_x, gu.step_yz],
        })
        ctx_out = fetch(ctx_t, ctxt, 3)
        ctx_out.start()
        for j in range(nb):
            ctx_v[j * BLK : (j + 1) * BLK, :] = ctx_t[j].T.astype(BF)
        go.near(True)
        go.far()
        for c in keys_out:
            c.wait()
        ctx_out.wait()
        for i in range(groups - 1):
            par(i).wait_send()
            par_from(i).wait_recv()

        @pl.when(h < groups - 1)
        def _():
            both(to_right, gone)

        @pl.when(h > 0)
        def _():
            both(to_left, gone)

    def dense(cot_v, out_v, up_v, down_v, hl, ht, act_t, slope):
        ffn, gup, mix_v, g_low = g_hid, hl, ctx_v, cot_v
        gain1, shift1, gain2, shift2 = (parameter(i) for i in range(4))
        first = [fetch(a, b, i) for i, (a, b) in enumerate(((out_w.at[0], out_v), (cot, cot_v)))]
        for c in first:
            c.start()

        def weights(i, slot):
            if i == shards - 1:
                return fetch(up_own.at[0], up_v.at[slot], 4 + slot), fetch(down_own.at[0], down_v.at[slot], 6 + slot)
            here = pl.ds(pl.multiple_of(shard_of(i) * width, 16), width)
            return fetch(up_w.at[0, here, :], up_v.at[slot], 4 + slot), fetch(down_w.at[0, here, :], down_v.at[slot], 6 + slot)

        def start_weights(i, slot):
            for c in weights(i, slot):
                c.start()

        def wait_weights(i, slot):
            for c in weights(i, slot):
                c.wait()

        start_weights(3, 0)
        gu.near(False)
        gd.near(False)
        start_weights(2, 1)
        vec_acc[...] = jnp.zeros_like(vec_acc)
        for c in first:
            c.wait()

        def before(b, c):
            resid = x_v[rows(b + HALO), :].astype(F32) + nn(ctx_v[rows(b), :], out_v[...])
            cen = resid - mean(resid)
            rs = lax.rsqrt(mean(cen * cen) + NORM_EPS)
            n = cen * rs
            hidden = n * gain1 + shift1
            xhat[rows(b), :] = n
            inv[rows(b), :] = jnp.broadcast_to(rs, (BLK, 128))
            low = hidden.astype(BF)
            hl[rows(b), :] = low
            ht[b] = low.T
            ffn[rows(b), :] = hidden
            return c

        lax.fori_loop(0, nb, before, 0)

        def forward(i, c):
            slot = i % 2
            wait_weights(0, slot)
            for b in range(nb):
                up = nn(hl[rows(b), :], up_v[slot])
                active, deriv = gelu_parts(up)
                active = active.astype(BF)
                slope[i, rows(b), :] = deriv.astype(BF)
                act_t[i, b] = active.T
                ffn[rows(b), :] += nn(active, down_v[slot])
            return c

        def forward_then(i, c):
            forward(i, c)
            hooks_at(i, {
                0: [gu.step_diag, gd.step_yz],
                1: [gd.step_diag, lambda: start_weights(1, 0)],
                2: [gu.far, gd.far, lambda: start_weights(0, 1)],
            })
            return c

        lax.fori_loop(0, shards, forward_then, 0)

        def middle(b, c):
            v = ffn[rows(b), :]
            cen = v - mean(v)
            rs = lax.rsqrt(mean(cen * cen) + NORM_EPS)
            n = cen * rs
            mix_v[rows(b), :] = (n * gain2 + shift2).astype(BF)
            ct = cot_v[rows(b), :].astype(F32)
            vec_acc[2:3, :] += jnp.sum(ct * n, axis=0, keepdims=True)
            vec_acc[3:4, :] += jnp.sum(ct, axis=0, keepdims=True)
            e = ct * gain2
            g = rs * (e - mean(e) - n * mean(e * n))
            g_hid[rows(b), :] = g
            g_low[rows(b), :] = g.astype(BF)
            return c

        lax.fori_loop(0, nb, middle, 0)
        mix_out = fetch(mix_v, mixed, 0)
        mix_out.start()

        def grad_rows(left, right, part, part_i, slot):
            n = part.n
            acc = jnp.zeros((n, width), F32)
            for b in range(nb):
                acc += nn(left(b, pl.ds(part_i * n, n)), right[b * BLK : (b + 1) * BLK, :])
            part.mine[slot] = acc.astype(BF)

        def down_grads(i, c):
            slot = slot_of(i)

            @pl.when(i == 2)
            def _():
                for p in downs:
                    p.core(0).wait_send()

            for k, p in enumerate(downs):
                grad_rows(lambda b, n: act_t[shards - 1 - i, b, n, :], g_low, p, k, slot)
            hooks_at(i, {
                0: [p.c0 for p in downs],
                1: [downs[0].f, downs[0].xs],
                2: [downs[1].f, *(p.c1 for p in downs)],
            })
            return c

        lax.fori_loop(0, shards, down_grads, 0)

        def backward(i, c):
            slot = 1 - i % 2

            @pl.when(i >= 2)
            def _():
                wait_weights(0, slot)

            def one_block(b, cc):
                ga = nt(g_low[rows(b), :], down_v[slot])
                gu = (slope[shards - 1 - i, rows(b), :].astype(F32) * ga).astype(BF)
                gup[rows(b), :] = gu
                g_hid[rows(b), :] += nt(gu, up_v[slot])
                return cc

            lax.fori_loop(0, nb, one_block, 0)

            for back in (0, 1):

                @pl.when(i == back)
                def _():
                    start_weights(back + 2, 1 - back)

            @pl.when(i == 2)
            def _():
                for p in ups:
                    p.core(0).wait_send()

            for k, p in enumerate(ups):
                grad_rows(lambda b, n: ht[b, n, :], gup, p, k, slot_of(i))
            hooks_at(i, {
                0: [p.c0 for p in ups] + [p.s for p in downs],
                1: [p.f for p in ups] + [downs[1].xs],
                2: [p.c1 for p in ups] + [downs[0].r],
                3: [p.s for p in ups],
            })
            return c

        lax.fori_loop(0, shards, backward, 0)
        mix_out.wait()

    pl.run_scoped(
        project,
        pltpu.VMEM((nw, width, BLK), BF),
        pltpu.VMEM((all_pairs, nw * BLK, 128), BF),
        pltpu.VMEM((all_pairs, nw * BLK, 128), BF),
        pltpu.VMEM((nw, width, BLK), BF),
        pltpu.VMEM((nb, row_blocks, BLK, BLK), F32),
        pltpu.VMEM((nb, width, BLK), F32),
    )
    pl.run_scoped(
        dense,
        pltpu.VMEM((own, width), BF),
        pltpu.VMEM((width, width), BF),
        pltpu.VMEM((2, width, width), BF),
        pltpu.VMEM((2, width, width), BF),
        pltpu.VMEM((own, width), BF),
        pltpu.VMEM((nb, width, BLK), BF),
        pltpu.VMEM((shards, nb, width, BLK), BF),
        pltpu.VMEM((shards, own, width), BF),
    )

    def attention(g_v, k_v, v_v, kt_v, delta, bias, dk, dv, dqt, dkt, dvt):
        gain1 = parameter(0)
        def keys(hf):
            base = pl.multiple_of(hf * half, 128)
            return (
                fetch(k_i.at[pl.ds(hf * pairs, pairs)], k_v, 0),
                fetch(v_i.at[pl.ds(hf * pairs, pairs)], v_v, 1),
                fetch(kt_i.at[:, pl.ds(base, half), :], kt_v, 2),
            )

        for c in keys(far_half):
            c.start()

        def between(out_v, ctxt_v):
            low_v = ctx_v
            o_in, c_in = fetch(out_w.at[0], out_v, 6), fetch(ctxt, ctxt_v, 7)
            o_in.start()
            c_in.start()

            def norm_back(b, c):
                g = g_hid[rows(b), :]
                n = xhat[rows(b), :]
                vec_acc[0:1, :] += jnp.sum(g * n, axis=0, keepdims=True)
                vec_acc[1:2, :] += jnp.sum(g, axis=0, keepdims=True)
                e = g * gain1
                res = inv[rows(b), 0:1] * (e - mean(e) - n * mean(e * n))
                g_hid[rows(b), :] = res
                low_v[rows(b), :] = res.astype(BF)
                return c

            lax.fori_loop(0, nb, norm_back, 0)
            o_in.wait()
            c_in.wait()

            def after(b, c):
                low = low_v[rows(b), :]
                gc = nt(low, out_v[...]).astype(BF)
                for i in range(all_pairs):
                    g_v[i, rows(b), :] = gc[:, i * 128 : (i + 1) * 128]
                prod = nt(out_v[...], low).astype(BF).astype(F32) * ctxt_v[b]
                for i in range(2 * all_pairs):
                    delta[b, i] = jnp.sum(prod[i * HEAD_WIDTH : (i + 1) * HEAD_WIDTH, :], axis=0, keepdims=True)
                return c

            lax.fori_loop(0, nb, after, 0)
            vstep(0).start()
            ups[0].xs()

            def grad_out(i, c):
                @pl.when(i == 2)
                def _():
                    out_c.core(0).wait_send()

                base = pl.multiple_of(shard_of(i) * shard_rows, 16)
                acc = jnp.zeros((shard_rows, width), F32)
                for b in range(nb):
                    acc += nn(ctxt_v[b, pl.ds(base, shard_rows), :].astype(BF), low_v[b * BLK : (b + 1) * BLK, :])
                out_c.mine[slot_of(i)] = acc.astype(BF)
                hooks_at(i, {0: [out_c.c0], 2: [out_c.c1]})
                return c

            lax.fori_loop(0, shards, grad_out, 0)
            downs[0].yy()
            downs[1].r()
            out_c.f()

        pl.run_scoped(
            between,
            pltpu.VMEM((width, width), BF),
            pltpu.VMEM((nb, width, BLK), F32),
        )
        def unit(hf, t):
            j, i = t // pairs, t % pairs
            p = hf * pairs + i
            ws = window_start(h, j, nb, row_blocks)

            @pl.when(i == 0)
            def _():
                for kb in range(row_blocks):
                    bias[kb * BLK : (kb + 1) * BLK, :] = mask_of(seg[ws + kb], seg[HALO + j])

            q = q_v[p, rows(j), :]
            g = g_v[p, rows(j), :]
            lane = lax.broadcasted_iota(jnp.int32, q.shape, 1)
            qm = [jnp.where(lane // HEAD_WIDTH == hh, q, jnp.zeros_like(q)) for hh in range(2)]
            gm = [jnp.where(lane // HEAD_WIDTH == hh, g, jnp.zeros_like(g)) for hh in range(2)]
            window = pl.ds(pl.multiple_of(ws * BLK, BLK), row_blocks * BLK)
            scores = nt(k_v[i, window, :], jnp.concatenate(qm, axis=0))
            g_probs = nt(v_v[i, window, :], jnp.concatenate(gm, axis=0))
            probs, g_scores = [], []
            for hh in range(2):
                cols = slice(hh * BLK, (hh + 1) * BLK)
                prob = jnp.exp(scores[:, cols] + bias[...] - lse[j, 2 * p + hh])
                g_scores.append((prob * (g_probs[:, cols] - delta[j, 2 * p + hh])).astype(BF))
                probs.append(prob.astype(BF))
            dv[i, window, :] += nn(probs[0], gm[0]) + nn(probs[1], gm[1])
            dk[i, window, :] += nn(g_scores[0], qm[0]) + nn(g_scores[1], qm[1])
            for hh in range(2):
                at = pl.ds(pl.multiple_of((2 * i + hh) * HEAD_WIDTH, HEAD_WIDTH), HEAD_WIDTH)
                acc = jnp.zeros((HEAD_WIDTH, BLK), F32)
                for kb in range(row_blocks):
                    acc += nn(kt_v[ws + kb, at, :], g_scores[hh][kb * BLK : (kb + 1) * BLK, :])
                dqt[j, at, :] = (acc * HEAD_WIDTH**-0.5).astype(BF)

        def attend_half(hf, plan, then):
            dk[...] = jnp.zeros_like(dk)
            dv[...] = jnp.zeros_like(dv)

            def body(t, c):
                hooks_at(t, plan)
                unit(hf, t)
                return c

            lax.fori_loop(0, nb * pairs, body, 0)
            for step in then:
                step()

            def turn(b, c):
                dkt[b] = jnp.concatenate([dk[p, rows(b), :].astype(BF) for p in range(pairs)], axis=1).T
                dvt[b] = jnp.concatenate([dv[p, rows(b), :].astype(BF) for p in range(pairs)], axis=1).T
                return c

            lax.fori_loop(0, nw, turn, 0)

        def weight_grads(which, slot, then):
            at = pl.multiple_of(which * shard_rows, 16)
            for c, src, blocks in ((q_c, dqt, range(HALO, HALO + nb)), (k_c, dkt, range(nw)), (v_c, dvt, range(nw))):
                acc = jnp.zeros((shard_rows, width), F32)
                for b in blocks:
                    acc += nn(src[b - blocks[0], pl.ds(at, shard_rows), :], x_v[b * BLK : (b + 1) * BLK, :])
                c.mine[slot] = acc.astype(BF)
                then(c)

        def input_grads(hf, last):
            base = pl.multiple_of(hf * half, 128)
            wk, wv = w_v.at[1, pl.ds(base, half), :], w_v.at[2, pl.ds(base, half), :]

            def block(b):
                kb = jnp.concatenate([dk[p, rows(b), :].astype(BF) for p in range(pairs)], axis=1)
                vb = jnp.concatenate([dv[p, rows(b), :].astype(BF) for p in range(pairs)], axis=1)
                return nn(kb, wk[...]) + nn(vb, wv[...])

            def side(i, c):
                b = i + jnp.where(i >= HALO, nb, 0)
                total = block(b)
                if last:
                    total = total + gx_side[rows(i), :].astype(F32)
                gx_side[rows(i), :] = total.astype(BF)
                return c

            lax.fori_loop(0, 2 * HALO, side, 0)

            def inner(j, c):
                g_hid[rows(j), :] += block(j + HALO) + nn(dqt[j].T, w_v[0, pl.ds(base, half), :])
                return c

            return lambda: lax.fori_loop(0, nb, inner, 0)

        for c in keys(far_half):
            c.wait()
        d0, d1 = downs
        u0, u1 = ups
        vs = [functools.partial(vnext, i) for i in range(len(vec_ids))]
        vs = [functools.partial(vnext, i) for i in range(len(vec_ids))]
        attend_half(far_half, {
            1: [vs[0], out_c.s], 3: [d0.zz], 5: [u1.xs], 6: [d1.yy], 7: [u0.r], 8: [d0.w],
        }, [d1.zz])
        for c in keys(x_half):
            c.start()
        weight_grads(1 - core, 0, lambda p: p.c0())
        out_c.xs()
        weight_grads(core, 1, lambda p: (p.f(), p.xs()))
        u0.yy()
        d0.u()
        input_grads(far_half, False)()
        u1.r()
        for c in keys(x_half):
            c.wait()
        attend_half(x_half, {
            1: [u0.zz, d1.w], 3: [out_c.r, vs[1]], 5: [u1.yy], 6: [u0.w], 7: [d0.end, d1.u], 8: [u1.zz, out_c.yy],
        }, [])
        for p in (q_c, k_c, v_c):
            p.core(0).wait_send()
        weight_grads(1 - core, 0, lambda p: p.c1())
        u0.u()
        out_c.zz()
        vs[2]()
        weight_grads(core, 2, lambda p: None)
        for p in (q_c, k_c, v_c):
            p.s()
            p.r()
        u1.w()
        finish = input_grads(x_half, True)

        @pl.when(h > 0)
        def _():
            to_left.start()

        @pl.when(h < groups - 1)
        def _():
            to_right.start()

        finish()
        q_c.yy()
        k_c.yy()
        out_c.w()
        q_c.zz()
        v_c.yy()
        k_c.zz()
        u1.u()
        v_c.zz()
        q_c.w()
        vs[3]()
        out_c.u()
        k_c.w()
        v_c.w()
        q_c.u()
        from_right, from_left = pl.ds(halo + own, halo), pl.ds(0, halo)

        @pl.when(h < groups - 1)
        def _():
            to_left.wait_recv()
            fetch(o_left, x_v.at[from_right, :], 0).start()

        @pl.when(h > 0)
        def _():
            to_right.wait_recv()
            fetch(o_right, x_v.at[from_left, :], 1).start()

        k_c.u()
        v_c.u()
        d1.end()
        u0.end()
        u1.end()
        out_c.end()
        for step in vs[4:]:
            step()

        @pl.when(h < groups - 1)
        def _():
            fetch(o_left, x_v.at[from_right, :], 0).wait()
            g_hid[own - halo :, :] += x_v[from_right, :].astype(F32)

        @pl.when(h > 0)
        def _():
            fetch(o_right, x_v.at[from_left, :], 1).wait()
            g_hid[:halo, :] += x_v[from_left, :].astype(F32)

        tok_out = fetch(g_hid, o_tok, 3)
        tok_out.start()
        for p in (q_c, k_c, v_c):
            p.end()
        tok_out.wait()

    to_left = remote(gx_side.at[pl.ds(0, halo), :], o_left, side_send.at[0], side_recv.at[0], (r, h - 1))
    to_right = remote(gx_side.at[pl.ds(halo, halo), :], o_right, side_send.at[1], side_recv.at[1], (r, h + 1))

    pl.run_scoped(
        attention,
        pltpu.VMEM((all_pairs, own, 128), BF),
        pltpu.VMEM((pairs, nw * BLK, 128), BF),
        pltpu.VMEM((pairs, nw * BLK, 128), BF),
        pltpu.VMEM((nw, half, BLK), BF),
        pltpu.VMEM((nb, 2 * all_pairs, 1, BLK), F32),
        pltpu.VMEM((row_blocks * BLK, BLK), F32),
        pltpu.VMEM((pairs, nw * BLK, 128), F32),
        pltpu.VMEM((pairs, nw * BLK, 128), F32),
        pltpu.VMEM((nb, half, BLK), BF),
        pltpu.VMEM((nw, half, BLK), BF),
        pltpu.VMEM((nw, half, BLK), BF),
    )

    o_vec[...] = vacc[len(vec_ids) - 1]
    for g in (gq, go, gu, gd):
        g.sent()
    for p in parts:
        p.done()
    for i in range(len(vec_ids)):
        vstep(i).wait_send()

    @pl.when(h > 0)
    def _():
        to_left.wait_send()

    @pl.when(h < groups - 1)
    def _():
        to_right.wait_send()


def layer(groups, row_blocks, row_devices, tok, cot, qkv_own, out_own, up_own, down_own, vec_own, lengths):
    own, width = tok.shape
    shard_rows = width // groups
    nb = own // BLK
    nw = nb + 2 * HALO
    all_pairs = width // 128
    bits = other_bits(row_devices)
    split = width // 2
    chunks = [(name, lo, split) for name in ("down", "up") for lo in range(0, width, split)]
    chunks += [(name, 0, shard_rows) for name in ("out", "q", "k", "v")]
    hops = 4 + len(bits)
    scratch = [
        pltpu.VMEM((3, width, width), BF),
        pltpu.VMEM((nw * BLK, width), BF),
        pltpu.VMEM((all_pairs, own, 128), BF),
        pltpu.VMEM((own, width), BF),
        pltpu.VMEM((nb, 2 * all_pairs, 1, BLK), F32),
        pltpu.VMEM((nw, 1, BLK), F32),
        pltpu.VMEM((groups,) + vec_own.shape, BF),
        pltpu.VMEM((own, width), F32),
        pltpu.VMEM((own, 128), F32),
        pltpu.VMEM((own, width), F32),
        pltpu.VMEM((2 * HALO * BLK, width), BF),
        pltpu.VMEM((8, width), F32),
        pltpu.VMEM((hops, 8, width), F32),
        pltpu.VMEM((hops, 8, width), F32),
    ]
    for _, _, n in chunks:
        scratch += [
            pltpu.VMEM((3, n, width), BF),
            pltpu.VMEM((2, n, width), BF),
            pltpu.VMEM((n, width), BF),
            pltpu.VMEM((n // 2, width), BF),
            pltpu.VMEM((n // 4, width), BF),
            pltpu.VMEM((max(1, len(bits)), n // 4, width), BF),
        ]
    dma = pltpu.SemaphoreType.DMA
    scratch += [dma((len(chunks), 8 + len(bits)))] * 2 + [dma((len(chunks), 3))] + [dma((4, 12))] * 2
    scratch += [dma((2 * HALO,))] * 2 + [dma((2,))] * 2 + [dma((groups - 1,))] * 2 + [dma((hops,))] * 2 + [dma((8,))]
    s = jax.ShapeDtypeStruct
    side = s((HALO * BLK, width), BF)
    outs = [
        (s((own, width), BF), ANY),
        (s((width, width), BF), ANY),
        (s((width, width), BF), ANY),
        (s((shard_rows, width), BF), ANY),
        (s((3, shard_rows, width), BF), ANY),
        (s((own, width), F32), ANY),
        (side, ANY),
        (side, ANY),
        (s((8, width), F32), VM),
        (s((1, width, width), BF), ANY),
        (s((1, groups * width, width), BF), ANY),
        (s((1, groups * width, width), BF), ANY),
        (s((nb, width, BLK), F32), ANY),
        (s((all_pairs, nw * BLK, 128), BF), ANY),
        (s((all_pairs, nw * BLK, 128), BF), ANY),
        (s((nw, width, BLK), BF), ANY),
    ]
    return pl.pallas_call(
        functools.partial(layer_kernel, groups, row_blocks, bits, chunks),
        out_shape=[o[0] for o in outs],
        in_specs=[ANY] * 6 + [VM] * 2,
        out_specs=[o[1] for o in outs],
        scratch_shapes=scratch,
        compiler_params=pltpu.CompilerParams(collective_id=0, has_side_effects=True, vmem_limit_bytes=VMEM_LIMIT),
        name="layer",
    )(tok, cot, qkv_own, out_own, up_own, down_own, vec_own, lengths)


def local(
    groups, row_devices,
    tokens, lengths, w_query, w_key, w_value, w_out, w_up, w_down,
    gain_first, shift_first, gain_second, shift_second, cotangent,
):
    packed_rows = lengths.shape[0]
    own, width = tokens.shape
    row_length = groups * own // packed_rows
    row_blocks = row_length // BLK
    h = lax.axis_index("heads")
    n_vec = gain_first.shape[0]
    vec_own = jnp.concatenate([gain_first, shift_first, gain_second, shift_second])
    vec_own = jnp.broadcast_to(vec_own[None, :], (16, width))
    qkv_own = jnp.stack([w_query.T, w_key.T, w_value.T])
    mixed, o_down, o_up, o_out, o_qkv, o_tok, _, _, o_vec = layer(
        groups, row_blocks, row_devices, tokens, cotangent, qkv_own, w_out[None], w_up[None], w_down[None], vec_own, lengths
    )[:9]
    mine = lax.dynamic_slice(o_vec, (0, n_vec * h), (4, n_vec))
    wide = lambda a: a.astype(F32)
    return (
        mixed, o_tok, wide(o_qkv[0].T), wide(o_qkv[1].T), wide(o_qkv[2].T), wide(o_out), wide(o_up), wide(o_down),
        mine[0], mine[1], mine[2], mine[3],
    )


def solution(mesh):
    both, heads = P(("rows", "heads"), None), P("heads")
    cols, rows = P(None, "heads"), P("heads", None)
    return jax.shard_map(
        functools.partial(local, mesh.shape["heads"], mesh.shape["rows"]),
        mesh=mesh,
        in_specs=(both, P("rows", None), cols, cols, cols, rows, cols, rows, heads, heads, heads, heads, both),
        out_specs=(both, both, cols, cols, cols, rows, cols, rows, heads, heads, heads, heads),
        check_vma=False,
    )
```

```python
import functools

import jax
import jax.numpy as jnp
from jax import lax
from jax.experimental import pallas as pl
from jax.experimental.pallas import tpu as pltpu
from jax.sharding import PartitionSpec as P

MESH = pl.DeviceIdType.MESH
BF = jnp.bfloat16
F32 = jnp.float32
HEAD_WIDTH = 64
LONGEST_DOC = 512
BLK = 256
HALO = LONGEST_DOC // BLK
NORM_EPS = 1e-12
VMEM_LIMIT = 62 * 1024 * 1024


def nt(left, right):
    return lax.dot_general(left, right, (((1,), (1,)), ((), ())), preferred_element_type=F32)


def nn(left, right):
    return lax.dot_general(left, right, (((1,), (0,)), ((), ())), preferred_element_type=F32)


def flip(index, bit):
    return index + bit - 2 * bit * ((index // bit) % 2)


def place():
    r, h = lax.axis_index("rows"), lax.axis_index("heads")
    return r, h


def greet(ids):
    barrier = pltpu.get_barrier_semaphore()
    for who in ids:
        pl.semaphore_signal(barrier, inc=1, device_id=who, device_id_type=MESH)
    pl.semaphore_wait(barrier, len(ids))


def group_of(r, h, groups):
    return [(r, lax.rem(h + i, groups)) for i in range(1, groups)]


def remote(src, dst, send, recv, who):
    return pltpu.make_async_remote_copy(
        src_ref=src, dst_ref=dst, send_sem=send, recv_sem=recv, device_id=who, device_id_type=MESH
    )


class Gather:
    def __init__(self, own, full, sems, at):
        self.own, self.full, self.sems, self.at = own, full, sems, at
        self.n = own.shape[1]
        self.u = self.n // 12
        r, h = place()
        self.r, self.h = r, h
        y, z = r % 2, (r // 2) % 2
        self.k = 2 * z + y
        self.ky = 2 * z + 1 - y
        self.kz = 2 * (1 - z) + y
        self.kd = 3 - self.k
        self.hx = flip(h, 2)
        self.hc = flip(h, 1)
        self.by_x = (r, self.hx)
        self.by_c = (r, self.hc)
        self.by_y = (flip(r, 1), h)
        self.by_z = (flip(r, 2), h)

    def rows(self, shard, sub, count):
        u = self.u
        return pl.ds(pl.multiple_of(shard * self.n + sub * u, 16), count * u)

    def part(self, slot, who, shard, sub, count, own=False):
        dst = self.full.at[:, self.rows(shard, sub, count), :]
        src = self.own.at[:, self.rows(0, sub, count), :] if own else dst
        send, recv = self.sems
        return remote(src, dst, send.at[self.at, slot], recv.at[self.at, slot], who)

    def x_main(self):
        return self.part(0, self.by_x, self.h, 3 * self.k, 3, own=True)

    def x_diag(self):
        return self.part(1, self.by_x, self.h, 3 * self.kd, 1, own=True)

    def y_main(self):
        return self.part(2, self.by_y, self.hx, 3 * self.k, 3)

    def z_main(self):
        return self.part(3, self.by_z, self.hx, 3 * self.k, 3)

    def y_diag(self):
        return self.part(4, self.by_y, self.hx, 3 * self.kz + 1, 1)

    def z_diag(self):
        return self.part(5, self.by_z, self.hx, 3 * self.ky + 2, 1)

    def c_own(self):
        return self.part(6, self.by_c, self.h, 0, 12, own=True)

    def c_part(self, i):
        return self.part(7 + i, self.by_c, self.hx, 3 * (self.k, self.ky, self.kz, self.kd)[i], 3)

    def local(self):
        send, _ = self.sems
        return pltpu.make_async_copy(
            self.own, self.full.at[:, self.rows(self.h, 0, 12), :], send.at[self.at, 11]
        )

    def start_x(self):
        self.x_main().start()
        self.x_diag().start()

    def start_main(self):
        self.x_main().start()

    def start_diag(self):
        self.x_diag().start()

    def start_c(self, keep):
        self.c_own().start()
        if keep:
            self.local().start()

    def step_x(self):
        self.x_main().wait_recv()
        self.y_main().start()
        self.z_main().start()
        self.c_part(0).start()

    def step_yz(self):
        self.y_main().wait_recv()
        self.z_diag().start()
        self.c_part(1).start()
        self.z_main().wait_recv()
        self.y_diag().start()
        self.c_part(2).start()

    def step_diag(self):
        self.x_diag().wait_recv()
        self.y_diag().wait_recv()
        self.z_diag().wait_recv()
        self.c_part(3).start()

    def near(self, keep):
        self.c_own().wait_recv()
        if keep:
            self.local().wait()

    def far(self):
        for i in range(4):
            self.c_part(i).wait_recv()

    def sent(self):
        for copy in (self.x_main(), self.x_diag(), self.y_main(), self.z_main(), self.y_diag(), self.z_diag(), self.c_own()):
            copy.wait_send()
        for i in range(4):
            self.c_part(i).wait_send()


def window_start(h, j, own_blocks, row_blocks):
    g = own_blocks * h + j
    first = own_blocks * h - HALO
    row = row_blocks * (g // row_blocks)
    return jnp.clip(row, first, first + own_blocks + 2 * HALO - row_blocks) - first


def mask_of(keys, queries):
    down = jnp.broadcast_to(keys, (8, BLK)).T[:, 0:1]
    return jnp.where(down == queries, 0.0, -1e30).astype(F32)


ANY = pl.BlockSpec(memory_space=pl.ANY)
VM = pl.BlockSpec(memory_space=pltpu.VMEM)


def gelu_parts(u):
    bell = jnp.exp(-0.5 * u * u)
    base = 1.0 + (0.3275911 * 0.7071067811865476) * jnp.abs(u)
    t = pl.reciprocal(base, approx=True)
    t = t * (2.0 - base * t)
    poly = t * (0.127414796 + t * (-0.142248368 + t * (0.7107068705 + t * (-0.7265760135 + t * 0.5307027145))))
    tail = poly * bell
    cdf = jnp.where(u >= 0.0, 1.0 - tail, tail)
    return u * cdf, cdf + u * (bell * 0.3989422804014327)


class Sum:
    def __init__(self, n, bits, bufs, sems, at, turned):
        self.n, self.bits, self.at = n, bits, at
        self.mine, self.rc, self.rx, self.ry, self.rz, self.rest = bufs
        self.send, self.recv, self.keep = sems
        r, h = place()
        self.y, self.z = r % 2, (r // 2) % 2
        self.by_x, self.by_c = (r, flip(h, 2)), (r, flip(h, 1))
        self.by_y, self.by_z = (flip(r, 1), h), (flip(r, 2), h)
        if turned:
            self.y, self.z, self.by_y, self.by_z = self.z, self.y, self.by_z, self.by_y
        self.by_rest = [(flip(r, b), h) for b in bits]

    def copy(self, slot, src, dst, who):
        return remote(src, dst, self.send.at[self.at, slot], self.recv.at[self.at, slot], who)

    def core(self, i):
        return self.copy(i, self.mine.at[0], self.rc.at[i], self.by_c)

    def x(self):
        return self.copy(2, self.mine.at[1], self.rx, self.by_x)

    def half(self, which):
        return pl.ds(pl.multiple_of(which * (self.n // 2), 16), self.n // 2)

    def quarter(self, half, which):
        return pl.ds(pl.multiple_of(half * (self.n // 2) + which * (self.n // 4), 16), self.n // 4)

    def own(self):
        return self.mine.at[2, self.quarter(self.y, self.z), :]

    def landed(self, half, which):
        return self.rx.at[self.quarter(half, which), :]

    def y_down(self):
        return self.copy(3, self.mine.at[2, self.half(1 - self.y), :], self.ry, self.by_y)

    def z_down(self):
        return self.copy(4, self.mine.at[2, self.quarter(self.y, 1 - self.z), :], self.rz, self.by_z)

    def z_up(self):
        return self.copy(5, self.own(), self.landed(self.y, self.z), self.by_z)

    def y_up(self):
        return self.copy(6, self.own(), self.landed(self.y, self.z), self.by_y)

    def y_up2(self):
        return self.copy(7, self.landed(self.y, 1 - self.z), self.landed(self.y, 1 - self.z), self.by_y)

    def swap(self, i):
        return self.copy(8 + i, self.own(), self.rest.at[i], self.by_rest[i])

    def add(self, ref, got):
        step = self.n // 4

        def some(i, c):
            at = pl.ds(pl.multiple_of(i * step, 16), step)
            ref[at, :] = (ref[at, :].astype(F32) + got[at, :].astype(F32)).astype(BF)
            return c

        lax.fori_loop(0, ref.shape[0] // step, some, 0)

    def c0(self):
        self.core(0).start()

    def f(self):
        self.core(0).wait_recv()
        self.add(self.mine.at[1], self.rc.at[0])

    def xs(self):
        self.x().start()

    def c1(self):
        self.core(1).start()

    def s(self):
        self.core(1).wait_recv()
        self.add(self.mine.at[2], self.rc.at[1])

    def r(self):
        self.x().wait_recv()
        self.add(self.mine.at[2], self.rx)
        self.y_down().start()

    def yy(self):
        self.y_down().wait_recv()
        self.add(self.mine.at[2, self.half(self.y), :], self.ry)
        self.z_down().start()

    def zz(self):
        self.z_down().wait_recv()
        self.add(self.own(), self.rz)
        if self.bits:
            self.swap(0).start()

    def w(self):
        for i in range(len(self.bits)):
            self.swap(i).wait_recv()
            self.swap(i).wait_send()
            self.add(self.own(), self.rest.at[i])
            if i + 1 < len(self.bits):
                self.swap(i + 1).start()
        self.z_up().start()
        self.y_up().start()

    def u(self):
        self.z_up().wait_recv()
        self.y_up2().start()

    def outs(self, out, lo):
        def local(i, src, rows):
            start = pl.multiple_of(lo + rows.start, 16)
            return pltpu.make_async_copy(src, out.at[pl.ds(start, rows.size), :], self.keep.at[self.at, i])

        mine, beside, other = self.quarter(self.y, self.z), self.quarter(self.y, 1 - self.z), self.half(1 - self.y)
        return (
            local(0, self.own(), mine),
            local(1, self.rx.at[beside, :], beside),
            local(2, self.rx.at[other, :], other),
        )

    def e(self, out, lo):
        self.y_up().wait_recv()
        self.y_up2().wait_recv()
        for c in self.outs(out, lo):
            c.start()

    def sent(self, out, lo):
        for c in (self.core(1), self.x(), self.y_down(), self.z_down(), self.z_up(), self.y_up(), self.y_up2()):
            c.wait_send()
        for c in self.outs(out, lo):
            c.wait()


def other_bits(count):
    bits, b = [], 4
    while b < count:
        bits.append(b)
        b *= 2
    return tuple(bits)


def hooks_at(t, plan):
    for at, steps in plan.items():

        @pl.when(t == at)
        def _():
            for step in steps:
                step()


def layer_kernel(
    groups, row_blocks, bits, chunks,
    tok, cot, qkv_own, out_own, up_own, down_own, vec_own, lengths,
    mixed, o_down, o_up, o_out, o_qkv, o_tok, o_left, o_right, o_vec,
    out_w, up_w, down_w, ctxt, k_i, v_i, kt_i,
    w_v, x_v, q_v, ctx_v, lse, seg, vec_all, xhat, inv, g_hid, gx_side, vec_acc, vin, vacc, *scratch,
):
    r, h = place()
    own, width = tok.shape
    nb = own // BLK
    nw = nb + 2 * HALO
    halo = HALO * BLK
    shards = groups
    all_pairs = q_v.shape[0]
    pairs = all_pairs // 2
    half = pairs * 128
    shard_rows = half // 2
    x_half = (h // 2) % 2
    far_half = 1 - x_half
    core = h % 2
    rows = lambda b: pl.ds(pl.multiple_of(b * BLK, BLK), BLK)
    mean = lambda v: jnp.mean(v, axis=1, keepdims=True)
    n_chunks = len(chunks)
    (send, recv, keep, gsend, grecv, in_send, in_recv, side_send, side_recv, psend, precv, vsend, vrecv, loc) = scratch[6 * n_chunks :]
    sems = (send, recv, keep)
    turned = (1, 3, 6)
    outs = {"down": o_down, "up": o_up, "out": o_out, "q": o_qkv.at[0], "k": o_qkv.at[1], "v": o_qkv.at[2]}
    parts = [Sum(n, bits, scratch[6 * i : 6 * i + 6], sems, i, i in turned) for i, (_, _, n) in enumerate(chunks)]
    by_name = {}
    for part, (name, lo, _) in zip(parts, chunks):
        part.end = functools.partial(part.e, outs[name], lo)
        part.done = functools.partial(part.sent, outs[name], lo)
        by_name.setdefault(name, []).append(part)
    downs, ups, (out_c,) = by_name["down"], by_name["up"], by_name["out"]
    q_c, k_c, v_c = (by_name[name][0] for name in "qkv")
    one = parts[0]
    gq = Gather(qkv_own, w_v, (gsend, grecv), 0)
    go = Gather(out_own, out_w, (gsend, grecv), 1)
    gu = Gather(up_own, up_w, (gsend, grecv), 2)
    gd = Gather(down_own, down_w, (gsend, grecv), 3)

    def shard_of(i):
        across = 1 - i // 2
        other = 1 - i % 2
        return h + across * (2 - 4 * x_half) + other * (1 - 2 * core)

    def slot_of(i):
        return (i % 2) * (1 + i // 2)

    def fetch(src, dst, i):
        return pltpu.make_async_copy(src, dst, loc.at[i])

    vec_ids = [one.by_c, one.by_x, one.by_y, one.by_z] + one.by_rest

    def vstep(i):
        src = vec_acc if i == 0 else vacc.at[i - 1]
        return remote(src, vin.at[i], vsend.at[i], vrecv.at[i], vec_ids[i])

    def vnext(i):
        vstep(i).wait_recv()
        vacc[i] = (vec_acc[...] if i == 0 else vacc[i - 1]) + vin[i]
        if i + 1 < len(vec_ids):
            vstep(i + 1).start()

    def parameter(i):
        n = width // groups
        return jnp.concatenate([vec_all[s].astype(F32)[0:1, i * n : (i + 1) * n] for s in range(groups)], axis=1)

    def project(vt, k_s, v_s, kt_s, bias, ctx_t):
        total_blocks = groups * nb
        def to_right(i):
            src, dst = pl.ds(own - halo + i * BLK, BLK), pl.ds(i * BLK, BLK)
            return remote(tok.at[src, :], x_v.at[dst, :], in_send.at[i], in_recv.at[i], (r, h + 1))

        def to_left(i):
            src, dst = pl.ds(i * BLK, BLK), pl.ds(halo + own + i * BLK, BLK)
            return remote(tok.at[src, :], x_v.at[dst, :], in_send.at[HALO + i], in_recv.at[HALO + i], (r, h - 1))

        def both(to, step):
            for i in range(HALO):
                step(to(i))

        start, arrived, gone = (lambda c: c.start()), (lambda c: c.wait_recv()), (lambda c: c.wait_send())
        even = h % 2 == 0
        slow_right = jnp.logical_and(h % 2 == 1, h < groups - 1)
        slow_left = jnp.logical_and(even, h > 0)

        odd = h % 2 == 1

        def par(i):
            who = (r, lax.rem(h + 1 + i, groups))
            return remote(vec_own, vec_all.at[h], psend.at[i], precv.at[groups - 2 - i], who)

        def par_from(i):
            return remote(vec_own, vec_all.at[h], psend.at[i], precv.at[i], (r, lax.rem(h + 1 + i, groups)))

        mine = fetch(tok, x_v.at[pl.ds(halo, own), :], 0)
        mine.start()
        greet(group_of(r, h, groups) + [one.by_y, one.by_z] + one.by_rest)

        @pl.when(slow_right)
        def _():
            to_right(HALO - 1).start()

        @pl.when(slow_left)
        def _():
            to_left(0).start()

        gq.start_c(True)
        gq.start_x()

        @pl.when(even)
        def _():
            both(to_right, start)

        @pl.when(odd)
        def _():
            both(to_left, start)

        for i in range(groups - 1):
            par(i).start()
        vec_all[h] = vec_own[...]

        @pl.when(h == 0)
        def _():
            x_v[pl.ds(0, halo), :] = jnp.zeros((halo, width), BF)

        @pl.when(h == groups - 1)
        def _():
            x_v[pl.ds(halo + own, halo), :] = jnp.zeros((halo, width), BF)

        packed, docs = lengths.shape
        down = lax.broadcasted_iota(jnp.int32, (docs, docs), 0)
        across = lax.broadcasted_iota(jnp.int32, (docs, docs), 1)
        for b in range(nw):
            g = nb * h - HALO + b
            row = jnp.clip(g // row_blocks, 0, packed - 1)
            sizes = lengths[pl.ds(row, 1), :].astype(F32)
            ends = jnp.sum(jnp.where(across <= down, jnp.broadcast_to(sizes, (docs, docs)), 0.0), axis=1, keepdims=True)
            at = (lax.broadcasted_iota(jnp.int32, (docs, BLK), 1) + (g % row_blocks) * BLK).astype(F32)
            ids = jnp.sum(jnp.where(at >= ends, 1.0, 0.0), axis=0, keepdims=True) + (row * docs).astype(F32)
            inside = jnp.logical_and(g >= 0, g < total_blocks)
            seg[b] = jnp.where(inside, ids, -1.0)
        for j in range(nb):
            ws = window_start(h, j, nb, row_blocks)
            for kb in range(row_blocks):
                bias[j, kb] = mask_of(seg[ws + kb], seg[HALO + j])

        def project_keys(hx, b):
            base = pl.multiple_of(hx * half, 128)
            xb = x_v[rows(b), :]
            wk = w_v[1, pl.ds(base, half), :]
            wv = w_v[2, pl.ds(base, half), :]
            key = nt(xb, wk).astype(BF)
            value = nt(xb, wv).astype(BF)
            for i in range(pairs):
                k_s[hx * pairs + i, rows(b), :] = key[:, i * 128 : (i + 1) * 128]
                v_s[hx * pairs + i, rows(b), :] = value[:, i * 128 : (i + 1) * 128]
            kt_s[b, pl.ds(base, half), :] = nt(wk, xb).astype(BF)
            vt[b, pl.ds(base, half), :] = nt(wv, xb).astype(BF)

        def project_query(hx, b):
            base = pl.multiple_of(hx * half, 128)
            xb = x_v[rows(b + HALO), :]
            query = nt(xb, w_v[0, pl.ds(base, half), :]).astype(BF) * BF(HEAD_WIDTH**-0.5)
            for i in range(pairs):
                q_v[hx * pairs + i, rows(b), :] = query[:, i * 128 : (i + 1) * 128]

        def side_keys(hx, first):
            def body(b, c):
                project_keys(hx, first + b)
                return c

            lax.fori_loop(0, HALO, body, 0)

        def attend(hx, t):
            j = jnp.where(odd, t // pairs, nb - 1 - t // pairs)
            p = hx * pairs + t % pairs
            ws = window_start(h, j, nb, row_blocks)
            q = q_v[p, rows(j), :]
            lane = lax.broadcasted_iota(jnp.int32, q.shape, 1)
            q_both = jnp.concatenate([jnp.where(lane // HEAD_WIDTH == hh, q, jnp.zeros_like(q)) for hh in range(2)], axis=0)
            scores, tops = [[], []], [None, None]
            for kb in range(row_blocks):
                both_s = nt(k_s[p, rows(ws + kb), :], q_both)
                for hh in range(2):
                    s = both_s[:, hh * BLK : (hh + 1) * BLK] + bias[j, kb]
                    m = jnp.max(s.reshape(BLK // 8, 8, BLK), axis=0)
                    tops[hh] = m if kb == 0 else jnp.maximum(tops[hh], m)
                    scores[hh].append(s)
            tops = [jnp.max(m, axis=0, keepdims=True) for m in tops]
            totals = [jnp.zeros((8, BLK), F32) for _ in range(2)]
            accs = [jnp.zeros((HEAD_WIDTH, BLK), F32) for _ in range(2)]
            at = [pl.ds(pl.multiple_of((2 * p + hh) * HEAD_WIDTH, HEAD_WIDTH), HEAD_WIDTH) for hh in range(2)]
            for kb in range(row_blocks):
                for hh in range(2):
                    e = jnp.exp(scores[hh][kb] - tops[hh])
                    totals[hh] = totals[hh] + jnp.sum(e.reshape(BLK // 8, 8, BLK), axis=0)
                    accs[hh] = accs[hh] + nn(vt[ws + kb, at[hh], :], e.astype(BF))
            for hh in range(2):
                total = jnp.sum(totals[hh], axis=0, keepdims=True)
                ctx_t[j, at[hh], :] = accs[hh] / total
                lse[j, 2 * p + hh] = tops[hh] + jnp.log(total)

        def attend_all(hx, plan):
            def body(t, c):
                hooks_at(t, plan)
                attend(hx, t)
                return c

            lax.fori_loop(0, nb * pairs, body, 0)

        def slow_block(near):
            @pl.when(slow_right)
            def _():
                to_left(0 if near else 1).wait_recv()

            @pl.when(slow_left)
            def _():
                to_right(1 if near else 0).wait_recv()

            project_keys(x_half, jnp.where(odd, HALO + nb + (0 if near else 1), 1 if near else 0))

        def more_halo():
            @pl.when(slow_right)
            def _():
                to_right(0).start()

            @pl.when(slow_left)
            def _():
                to_left(1).start()

        mine.wait()
        gq.near(True)
        lax.fori_loop(0, nb, lambda b, c: (project_query(x_half, b), c)[1], 0)
        lax.fori_loop(HALO, HALO + nb, lambda b, c: (project_keys(x_half, b), c)[1], 0)

        @pl.when(odd)
        def _():
            both(to_right, arrived)

        @pl.when(even)
        def _():
            both(to_left, arrived)

        side_keys(x_half, jnp.where(odd, 0, HALO + nb))
        last = jnp.where(odd, nw - 1, 0)
        for i in range(all_pairs):
            k_s[i, rows(last), :] = jnp.zeros((BLK, 128), BF)
        vt[last] = jnp.zeros((width, BLK), BF)
        attend_all(x_half, {
            0: [lambda: go.start_c(True), lambda: gu.start_c(False)],
            2: [more_halo], 3: [gq.step_x, functools.partial(slow_block, True), lambda: gd.start_c(False)],
            6: [functools.partial(slow_block, False), go.start_x, gu.start_x], 7: [gq.step_yz],
        })
        gd.start_x()
        gq.step_diag()
        go.step_x()
        gq.far()
        lax.fori_loop(0, nb, lambda b, c: (project_query(far_half, b), c)[1], 0)
        lax.fori_loop(0, nw, lambda b, c: (project_keys(far_half, b), c)[1], 0)
        keys_out = [fetch(a, b, i) for i, (a, b) in enumerate(((k_s, k_i), (v_s, v_i), (kt_s, kt_i)))]
        for c in keys_out:
            c.start()
        attend_all(far_half, {
            0: [gu.step_x], 3: [go.step_yz], 8: [gd.step_x, gu.step_yz, go.step_diag],
        })
        ctx_out = fetch(ctx_t, ctxt, 3)
        ctx_out.start()
        for j in range(nb):
            ctx_v[j * BLK : (j + 1) * BLK, :] = ctx_t[j].T.astype(BF)
        go.near(True)
        go.far()
        for c in keys_out:
            c.wait()
        ctx_out.wait()
        for i in range(groups - 1):
            par(i).wait_send()
            par_from(i).wait_recv()

        @pl.when(h < groups - 1)
        def _():
            both(to_right, gone)

        @pl.when(h > 0)
        def _():
            both(to_left, gone)

    def dense(cot_v, out_v, up_v, down_v, hl, ht, act_t, slope):
        ffn, gup, mix_v, g_low = g_hid, hl, ctx_v, cot_v
        gain1, shift1, gain2, shift2 = (parameter(i) for i in range(4))
        first = [fetch(a, b, i) for i, (a, b) in enumerate(((out_w.at[0], out_v), (cot, cot_v)))]
        for c in first:
            c.start()

        def weights(i, slot):
            if i == shards - 1:
                return fetch(up_own.at[0], up_v.at[slot], 4 + slot), fetch(down_own.at[0], down_v.at[slot], 6 + slot)
            here = pl.ds(pl.multiple_of(shard_of(i) * width, 16), width)
            return fetch(up_w.at[0, here, :], up_v.at[slot], 4 + slot), fetch(down_w.at[0, here, :], down_v.at[slot], 6 + slot)

        def start_weights(i, slot):
            for c in weights(i, slot):
                c.start()

        def wait_weights(i, slot):
            for c in weights(i, slot):
                c.wait()

        start_weights(3, 0)
        gu.near(False)
        gd.near(False)
        start_weights(2, 1)
        vec_acc[...] = jnp.zeros_like(vec_acc)
        for c in first:
            c.wait()

        def before(b, c):
            resid = x_v[rows(b + HALO), :].astype(F32) + nn(ctx_v[rows(b), :], out_v[...])
            cen = resid - mean(resid)
            rs = lax.rsqrt(mean(cen * cen) + NORM_EPS)
            n = cen * rs
            hidden = n * gain1 + shift1
            xhat[rows(b), :] = n
            inv[rows(b), :] = jnp.broadcast_to(rs, (BLK, 128))
            low = hidden.astype(BF)
            hl[rows(b), :] = low
            ht[b] = low.T
            ffn[rows(b), :] = hidden
            return c

        lax.fori_loop(0, nb, before, 0)

        def forward(i, c):
            slot = i % 2
            wait_weights(0, slot)
            for b in range(nb):
                up = nn(hl[rows(b), :], up_v[slot])
                active, deriv = gelu_parts(up)
                active = active.astype(BF)
                slope[i, rows(b), :] = deriv.astype(BF)
                act_t[i, b] = active.T
                ffn[rows(b), :] += nn(active, down_v[slot])
            return c

        def forward_then(i, c):
            forward(i, c)
            hooks_at(i, {
                0: [gu.step_diag, gd.step_yz],
                1: [gd.step_diag, lambda: start_weights(1, 0)],
                2: [gu.far, gd.far, lambda: start_weights(0, 1)],
            })
            return c

        lax.fori_loop(0, shards, forward_then, 0)

        def middle(b, c):
            v = ffn[rows(b), :]
            cen = v - mean(v)
            rs = lax.rsqrt(mean(cen * cen) + NORM_EPS)
            n = cen * rs
            mix_v[rows(b), :] = (n * gain2 + shift2).astype(BF)
            ct = cot_v[rows(b), :].astype(F32)
            vec_acc[2:3, :] += jnp.sum(ct * n, axis=0, keepdims=True)
            vec_acc[3:4, :] += jnp.sum(ct, axis=0, keepdims=True)
            e = ct * gain2
            g = rs * (e - mean(e) - n * mean(e * n))
            g_hid[rows(b), :] = g
            g_low[rows(b), :] = g.astype(BF)
            return c

        lax.fori_loop(0, nb, middle, 0)
        mix_out = fetch(mix_v, mixed, 0)
        mix_out.start()

        def grad_rows(left, right, part, part_i, slot):
            n = part.n
            acc = jnp.zeros((n, width), F32)
            for b in range(nb):
                acc += nn(left(b, pl.ds(part_i * n, n)), right[b * BLK : (b + 1) * BLK, :])
            part.mine[slot] = acc.astype(BF)

        def down_grads(i, c):
            slot = slot_of(i)

            @pl.when(i == 2)
            def _():
                for p in downs:
                    p.core(0).wait_send()

            for k, p in enumerate(downs):
                grad_rows(lambda b, n: act_t[shards - 1 - i, b, n, :], g_low, p, k, slot)
            hooks_at(i, {
                0: [p.c0 for p in downs],
                1: [downs[0].f, downs[0].xs],
                2: [downs[1].f, *(p.c1 for p in downs)],
            })
            return c

        lax.fori_loop(0, shards, down_grads, 0)

        def backward(i, c):
            slot = 1 - i % 2

            @pl.when(i >= 2)
            def _():
                wait_weights(0, slot)

            def one_block(b, cc):
                ga = nt(g_low[rows(b), :], down_v[slot])
                gu = (slope[shards - 1 - i, rows(b), :].astype(F32) * ga).astype(BF)
                gup[rows(b), :] = gu
                g_hid[rows(b), :] += nt(gu, up_v[slot])
                return cc

            lax.fori_loop(0, nb, one_block, 0)

            for back in (0, 1):

                @pl.when(i == back)
                def _():
                    start_weights(back + 2, 1 - back)

            @pl.when(i == 2)
            def _():
                for p in ups:
                    p.core(0).wait_send()

            for k, p in enumerate(ups):
                grad_rows(lambda b, n: ht[b, n, :], gup, p, k, slot_of(i))
            hooks_at(i, {
                0: [p.c0 for p in ups] + [p.s for p in downs],
                1: [p.f for p in ups] + [downs[1].xs],
                2: [p.c1 for p in ups] + [downs[0].r],
                3: [p.s for p in ups],
            })
            return c

        lax.fori_loop(0, shards, backward, 0)
        mix_out.wait()

    pl.run_scoped(
        project,
        pltpu.VMEM((nw, width, BLK), BF),
        pltpu.VMEM((all_pairs, nw * BLK, 128), BF),
        pltpu.VMEM((all_pairs, nw * BLK, 128), BF),
        pltpu.VMEM((nw, width, BLK), BF),
        pltpu.VMEM((nb, row_blocks, BLK, BLK), F32),
        pltpu.VMEM((nb, width, BLK), F32),
    )
    pl.run_scoped(
        dense,
        pltpu.VMEM((own, width), BF),
        pltpu.VMEM((width, width), BF),
        pltpu.VMEM((2, width, width), BF),
        pltpu.VMEM((2, width, width), BF),
        pltpu.VMEM((own, width), BF),
        pltpu.VMEM((nb, width, BLK), BF),
        pltpu.VMEM((shards, nb, width, BLK), BF),
        pltpu.VMEM((shards, own, width), BF),
    )

    def attention(g_v, k_v, v_v, kt_v, delta, bias, dk, dv, dqt, dkt, dvt):
        gain1 = parameter(0)
        def keys(hf):
            base = pl.multiple_of(hf * half, 128)
            return (
                fetch(k_i.at[pl.ds(hf * pairs, pairs)], k_v, 0),
                fetch(v_i.at[pl.ds(hf * pairs, pairs)], v_v, 1),
                fetch(kt_i.at[:, pl.ds(base, half), :], kt_v, 2),
            )

        for c in keys(far_half):
            c.start()

        def between(out_v, ctxt_v):
            low_v = ctx_v
            o_in, c_in = fetch(out_w.at[0], out_v, 6), fetch(ctxt, ctxt_v, 7)
            o_in.start()
            c_in.start()

            def norm_back(b, c):
                g = g_hid[rows(b), :]
                n = xhat[rows(b), :]
                vec_acc[0:1, :] += jnp.sum(g * n, axis=0, keepdims=True)
                vec_acc[1:2, :] += jnp.sum(g, axis=0, keepdims=True)
                e = g * gain1
                res = inv[rows(b), 0:1] * (e - mean(e) - n * mean(e * n))
                g_hid[rows(b), :] = res
                low_v[rows(b), :] = res.astype(BF)
                return c

            lax.fori_loop(0, nb, norm_back, 0)
            o_in.wait()
            c_in.wait()

            def after(b, c):
                low = low_v[rows(b), :]
                gc = nt(low, out_v[...]).astype(BF)
                for i in range(all_pairs):
                    g_v[i, rows(b), :] = gc[:, i * 128 : (i + 1) * 128]
                prod = nt(out_v[...], low).astype(BF).astype(F32) * ctxt_v[b]
                for i in range(2 * all_pairs):
                    delta[b, i] = jnp.sum(prod[i * HEAD_WIDTH : (i + 1) * HEAD_WIDTH, :], axis=0, keepdims=True)
                return c

            lax.fori_loop(0, nb, after, 0)
            vstep(0).start()
            ups[0].xs()

            def grad_out(i, c):
                @pl.when(i == 2)
                def _():
                    out_c.core(0).wait_send()

                base = pl.multiple_of(shard_of(i) * shard_rows, 16)
                acc = jnp.zeros((shard_rows, width), F32)
                for b in range(nb):
                    acc += nn(ctxt_v[b, pl.ds(base, shard_rows), :].astype(BF), low_v[b * BLK : (b + 1) * BLK, :])
                out_c.mine[slot_of(i)] = acc.astype(BF)
                hooks_at(i, {0: [out_c.c0], 2: [out_c.c1]})
                return c

            lax.fori_loop(0, shards, grad_out, 0)
            downs[0].yy()
            downs[1].r()
            out_c.f()

        pl.run_scoped(
            between,
            pltpu.VMEM((width, width), BF),
            pltpu.VMEM((nb, width, BLK), F32),
        )
        def unit(hf, t):
            j, i = t // pairs, t % pairs
            p = hf * pairs + i
            ws = window_start(h, j, nb, row_blocks)

            @pl.when(i == 0)
            def _():
                for kb in range(row_blocks):
                    bias[kb * BLK : (kb + 1) * BLK, :] = mask_of(seg[ws + kb], seg[HALO + j])

            q = q_v[p, rows(j), :]
            g = g_v[p, rows(j), :]
            lane = lax.broadcasted_iota(jnp.int32, q.shape, 1)
            qm = [jnp.where(lane // HEAD_WIDTH == hh, q, jnp.zeros_like(q)) for hh in range(2)]
            gm = [jnp.where(lane // HEAD_WIDTH == hh, g, jnp.zeros_like(g)) for hh in range(2)]
            window = pl.ds(pl.multiple_of(ws * BLK, BLK), row_blocks * BLK)
            scores = nt(k_v[i, window, :], jnp.concatenate(qm, axis=0))
            g_probs = nt(v_v[i, window, :], jnp.concatenate(gm, axis=0))
            probs, g_scores = [], []
            for hh in range(2):
                cols = slice(hh * BLK, (hh + 1) * BLK)
                prob = jnp.exp(scores[:, cols] + bias[...] - lse[j, 2 * p + hh])
                g_scores.append((prob * (g_probs[:, cols] - delta[j, 2 * p + hh])).astype(BF))
                probs.append(prob.astype(BF))
            dv[i, window, :] += nn(probs[0], gm[0]) + nn(probs[1], gm[1])
            dk[i, window, :] += nn(g_scores[0], qm[0]) + nn(g_scores[1], qm[1])
            for hh in range(2):
                at = pl.ds(pl.multiple_of((2 * i + hh) * HEAD_WIDTH, HEAD_WIDTH), HEAD_WIDTH)
                acc = jnp.zeros((HEAD_WIDTH, BLK), F32)
                for kb in range(row_blocks):
                    acc += nn(kt_v[ws + kb, at, :], g_scores[hh][kb * BLK : (kb + 1) * BLK, :])
                dqt[j, at, :] = (acc * HEAD_WIDTH**-0.5).astype(BF)

        def attend_half(hf, plan, then):
            dk[...] = jnp.zeros_like(dk)
            dv[...] = jnp.zeros_like(dv)

            def body(t, c):
                hooks_at(t, plan)
                unit(hf, t)
                return c

            lax.fori_loop(0, nb * pairs, body, 0)
            for step in then:
                step()

            def turn(b, c):
                dkt[b] = jnp.concatenate([dk[p, rows(b), :].astype(BF) for p in range(pairs)], axis=1).T
                dvt[b] = jnp.concatenate([dv[p, rows(b), :].astype(BF) for p in range(pairs)], axis=1).T
                return c

            lax.fori_loop(0, nw, turn, 0)

        def weight_grads(which, slot, then):
            at = pl.multiple_of(which * shard_rows, 16)
            for c, src, blocks in ((q_c, dqt, range(HALO, HALO + nb)), (k_c, dkt, range(nw)), (v_c, dvt, range(nw))):
                acc = jnp.zeros((shard_rows, width), F32)
                for b in blocks:
                    acc += nn(src[b - blocks[0], pl.ds(at, shard_rows), :], x_v[b * BLK : (b + 1) * BLK, :])
                c.mine[slot] = acc.astype(BF)
                then(c)

        def input_grads(hf, last):
            base = pl.multiple_of(hf * half, 128)
            wk, wv = w_v.at[1, pl.ds(base, half), :], w_v.at[2, pl.ds(base, half), :]

            def block(b):
                kb = jnp.concatenate([dk[p, rows(b), :].astype(BF) for p in range(pairs)], axis=1)
                vb = jnp.concatenate([dv[p, rows(b), :].astype(BF) for p in range(pairs)], axis=1)
                return nn(kb, wk[...]) + nn(vb, wv[...])

            def side(i, c):
                b = i + jnp.where(i >= HALO, nb, 0)
                total = block(b)
                if last:
                    total = total + gx_side[rows(i), :].astype(F32)
                gx_side[rows(i), :] = total.astype(BF)
                return c

            lax.fori_loop(0, 2 * HALO, side, 0)

            def inner(j, c):
                g_hid[rows(j), :] += block(j + HALO) + nn(dqt[j].T, w_v[0, pl.ds(base, half), :])
                return c

            return lambda: lax.fori_loop(0, nb, inner, 0)

        for c in keys(far_half):
            c.wait()
        d0, d1 = downs
        u0, u1 = ups
        vs = [functools.partial(vnext, i) for i in range(len(vec_ids))]
        vs = [functools.partial(vnext, i) for i in range(len(vec_ids))]
        attend_half(far_half, {
            1: [vs[0], out_c.s], 3: [d0.zz], 5: [u1.xs], 6: [d1.yy], 7: [u0.r], 8: [d0.w],
        }, [d1.zz])
        for c in keys(x_half):
            c.start()
        weight_grads(1 - core, 0, lambda p: p.c0())
        out_c.xs()
        weight_grads(core, 1, lambda p: (p.f(), p.xs()))
        u0.yy()
        d0.u()
        input_grads(far_half, False)()
        u1.r()
        for c in keys(x_half):
            c.wait()
        attend_half(x_half, {
            1: [u0.zz, d1.w], 3: [out_c.r, vs[1]], 5: [u1.yy], 6: [u0.w], 7: [d0.end, d1.u], 8: [u1.zz, out_c.yy],
        }, [])
        for p in (q_c, k_c, v_c):
            p.core(0).wait_send()
        weight_grads(1 - core, 0, lambda p: p.c1())
        u0.u()
        out_c.zz()
        vs[2]()
        weight_grads(core, 2, lambda p: None)
        for p in (q_c, k_c, v_c):
            p.s()
            p.r()
        u1.w()
        finish = input_grads(x_half, True)

        @pl.when(h > 0)
        def _():
            to_left.start()

        @pl.when(h < groups - 1)
        def _():
            to_right.start()

        finish()
        q_c.yy()
        k_c.yy()
        out_c.w()
        q_c.zz()
        v_c.yy()
        k_c.zz()
        u1.u()
        v_c.zz()
        q_c.w()
        vs[3]()
        out_c.u()
        k_c.w()
        v_c.w()
        q_c.u()
        from_right, from_left = pl.ds(halo + own, halo), pl.ds(0, halo)

        @pl.when(h < groups - 1)
        def _():
            to_left.wait_recv()
            fetch(o_left, x_v.at[from_right, :], 0).start()

        @pl.when(h > 0)
        def _():
            to_right.wait_recv()
            fetch(o_right, x_v.at[from_left, :], 1).start()

        k_c.u()
        v_c.u()
        d1.end()
        u0.end()
        u1.end()
        out_c.end()
        for step in vs[4:]:
            step()

        @pl.when(h < groups - 1)
        def _():
            fetch(o_left, x_v.at[from_right, :], 0).wait()
            g_hid[own - halo :, :] += x_v[from_right, :].astype(F32)

        @pl.when(h > 0)
        def _():
            fetch(o_right, x_v.at[from_left, :], 1).wait()
            g_hid[:halo, :] += x_v[from_left, :].astype(F32)

        tok_out = fetch(g_hid, o_tok, 3)
        tok_out.start()
        for p in (q_c, k_c, v_c):
            p.end()
        tok_out.wait()

    to_left = remote(gx_side.at[pl.ds(0, halo), :], o_left, side_send.at[0], side_recv.at[0], (r, h - 1))
    to_right = remote(gx_side.at[pl.ds(halo, halo), :], o_right, side_send.at[1], side_recv.at[1], (r, h + 1))

    pl.run_scoped(
        attention,
        pltpu.VMEM((all_pairs, own, 128), BF),
        pltpu.VMEM((pairs, nw * BLK, 128), BF),
        pltpu.VMEM((pairs, nw * BLK, 128), BF),
        pltpu.VMEM((nw, half, BLK), BF),
        pltpu.VMEM((nb, 2 * all_pairs, 1, BLK), F32),
        pltpu.VMEM((row_blocks * BLK, BLK), F32),
        pltpu.VMEM((pairs, nw * BLK, 128), F32),
        pltpu.VMEM((pairs, nw * BLK, 128), F32),
        pltpu.VMEM((nb, half, BLK), BF),
        pltpu.VMEM((nw, half, BLK), BF),
        pltpu.VMEM((nw, half, BLK), BF),
    )

    o_vec[...] = vacc[len(vec_ids) - 1]
    for g in (gq, go, gu, gd):
        g.sent()
    for p in parts:
        p.done()
    for i in range(len(vec_ids)):
        vstep(i).wait_send()

    @pl.when(h > 0)
    def _():
        to_left.wait_send()

    @pl.when(h < groups - 1)
    def _():
        to_right.wait_send()


def layer(groups, row_blocks, row_devices, tok, cot, qkv_own, out_own, up_own, down_own, vec_own, lengths):
    own, width = tok.shape
    shard_rows = width // groups
    nb = own // BLK
    nw = nb + 2 * HALO
    all_pairs = width // 128
    bits = other_bits(row_devices)
    split = width // 2
    chunks = [(name, lo, split) for name in ("down", "up") for lo in range(0, width, split)]
    chunks += [(name, 0, shard_rows) for name in ("out", "q", "k", "v")]
    hops = 4 + len(bits)
    scratch = [
        pltpu.VMEM((3, width, width), BF),
        pltpu.VMEM((nw * BLK, width), BF),
        pltpu.VMEM((all_pairs, own, 128), BF),
        pltpu.VMEM((own, width), BF),
        pltpu.VMEM((nb, 2 * all_pairs, 1, BLK), F32),
        pltpu.VMEM((nw, 1, BLK), F32),
        pltpu.VMEM((groups,) + vec_own.shape, BF),
        pltpu.VMEM((own, width), F32),
        pltpu.VMEM((own, 128), F32),
        pltpu.VMEM((own, width), F32),
        pltpu.VMEM((2 * HALO * BLK, width), BF),
        pltpu.VMEM((8, width), F32),
        pltpu.VMEM((hops, 8, width), F32),
        pltpu.VMEM((hops, 8, width), F32),
    ]
    for _, _, n in chunks:
        scratch += [
            pltpu.VMEM((3, n, width), BF),
            pltpu.VMEM((2, n, width), BF),
            pltpu.VMEM((n, width), BF),
            pltpu.VMEM((n // 2, width), BF),
            pltpu.VMEM((n // 4, width), BF),
            pltpu.VMEM((max(1, len(bits)), n // 4, width), BF),
        ]
    dma = pltpu.SemaphoreType.DMA
    scratch += [dma((len(chunks), 8 + len(bits)))] * 2 + [dma((len(chunks), 3))] + [dma((4, 12))] * 2
    scratch += [dma((2 * HALO,))] * 2 + [dma((2,))] * 2 + [dma((groups - 1,))] * 2 + [dma((hops,))] * 2 + [dma((8,))]
    s = jax.ShapeDtypeStruct
    side = s((HALO * BLK, width), BF)
    outs = [
        (s((own, width), BF), ANY),
        (s((width, width), BF), ANY),
        (s((width, width), BF), ANY),
        (s((shard_rows, width), BF), ANY),
        (s((3, shard_rows, width), BF), ANY),
        (s((own, width), F32), ANY),
        (side, ANY),
        (side, ANY),
        (s((8, width), F32), VM),
        (s((1, width, width), BF), ANY),
        (s((1, groups * width, width), BF), ANY),
        (s((1, groups * width, width), BF), ANY),
        (s((nb, width, BLK), F32), ANY),
        (s((all_pairs, nw * BLK, 128), BF), ANY),
        (s((all_pairs, nw * BLK, 128), BF), ANY),
        (s((nw, width, BLK), BF), ANY),
    ]
    return pl.pallas_call(
        functools.partial(layer_kernel, groups, row_blocks, bits, chunks),
        out_shape=[o[0] for o in outs],
        in_specs=[ANY] * 6 + [VM] * 2,
        out_specs=[o[1] for o in outs],
        scratch_shapes=scratch,
        compiler_params=pltpu.CompilerParams(collective_id=0, has_side_effects=True, vmem_limit_bytes=VMEM_LIMIT),
        name="layer",
    )(tok, cot, qkv_own, out_own, up_own, down_own, vec_own, lengths)


def local(
    groups, row_devices,
    tokens, lengths, w_query, w_key, w_value, w_out, w_up, w_down,
    gain_first, shift_first, gain_second, shift_second, cotangent,
):
    packed_rows = lengths.shape[0]
    own, width = tokens.shape
    row_length = groups * own // packed_rows
    row_blocks = row_length // BLK
    h = lax.axis_index("heads")
    n_vec = gain_first.shape[0]
    vec_own = jnp.concatenate([gain_first, shift_first, gain_second, shift_second])
    vec_own = jnp.broadcast_to(vec_own[None, :], (16, width))
    qkv_own = jnp.stack([w_query.T, w_key.T, w_value.T])
    mixed, o_down, o_up, o_out, o_qkv, o_tok, _, _, o_vec = layer(
        groups, row_blocks, row_devices, tokens, cotangent, qkv_own, w_out[None], w_up[None], w_down[None], vec_own, lengths
    )[:9]
    mine = lax.dynamic_slice(o_vec, (0, n_vec * h), (4, n_vec))
    wide = lambda a: a.astype(F32)
    return (
        mixed, o_tok, wide(o_qkv[0].T), wide(o_qkv[1].T), wide(o_qkv[2].T), wide(o_out), wide(o_up), wide(o_down),
        mine[0], mine[1], mine[2], mine[3],
    )


def solution(mesh):
    both, heads = P(("rows", "heads"), None), P("heads")
    cols, rows = P(None, "heads"), P("heads", None)
    return jax.shard_map(
        functools.partial(local, mesh.shape["heads"], mesh.shape["rows"]),
        mesh=mesh,
        in_specs=(both, P("rows", None), cols, cols, cols, rows, cols, rows, heads, heads, heads, heads, both),
        out_specs=(both, both, cols, cols, cols, rows, cols, rows, heads, heads, heads, heads),
        check_vma=False,
    )
```
